32 devices in a mesh: dp: 16 (over z, y, x), chan: 2 (over core).
Axes of the slice: x: 2, y: 2, z: 4, core: 2. Of those that a mesh axis runs over, the one named last changes fastest.
Arguments:
- frames: bfloat16 [49152, 512], P('dp'), may hold values from -6 to 6
- cotangent: bfloat16 [49152, 512], P('dp', 'chan'), may hold values from -6 to 6
- lengths: int32 [96], P('dp'), may hold values from 1 to 512, as said below
- frame_mask: int32 [49152], P('dp'), may hold values 0 or 1
- code_index: int32 [2, 49152, 2], P(None, 'dp', 'chan'), may hold values from 0 to 1023
- conv_weight: float32 [2, 3, 512, 512], P(None, None, 'dp', 'chan'), may hold values from -0.15625 to 0.15625
- proj_weight: float32 [2, 512, 512], P(None, 'dp', 'chan'), may hold values from -0.25 to 0.25
- codebooks: float32 [2, 1024, 512], P(None, 'dp', 'chan'), may hold values from -6 to 6
- conv_rows: float32 [2, 3, 512], P(None, None, 'dp'), may hold values from 1916928 to 7569408
- conv_cols: float32 [2, 512], P(None, 'chan'), may hold values from 5750784 to 23003136
- proj_rows: float32 [2, 512], P(None, 'dp'), may hold values from 7176192 to 28311552
- proj_cols: float32 [2, 512], P(None, 'chan'), may hold values from 7176192 to 28311552
- book_rows: float32 [2, 1024], P(None, 'dp'), may hold values from 3.967285e-05 to 0.0001566569
- book_cols: float32 [2, 512], P(None, 'chan'), may hold values from 7.93457e-05 to 0.0003133138
Outputs:
- decoded_out: bfloat16 [49152, 512], P('dp', 'chan')
- input_grad: bfloat16 [49152, 512], P('dp', 'chan')
- conv_grad: float32 [2, 3, 512, 512], P(None, None, 'dp', 'chan')
- proj_grad: float32 [2, 512, 512], P(None, 'dp', 'chan')
- book_grad: float32 [2, 1024, 512], P(None, 'dp', 'chan')
- rowstat_conv: float32 [2, 3, 512], P(None, None, 'dp')
- colstat_conv: float32 [2, 512], P(None, 'chan')
- rowstat_proj: float32 [2, 512], P(None, 'dp')
- colstat_proj: float32 [2, 512], P(None, 'chan')
- rowstat_book: float32 [2, 1024], P(None, 'dp')
- colstat_book: float32 [2, 512], P(None, 'chan')
- updated_conv: float32 [2, 3, 512, 512], P(None, None, 'dp', 'chan')
- updated_proj: float32 [2, 512, 512], P(None, 'dp', 'chan')
- updated_book: float32 [2, 1024, 512], P(None, 'dp', 'chan')
The draws below stay inside these ranges and needn't reach their ends.
Inputs may be any that keep to these rules, and one draw needn't show every extreme that they name: `lengths`: clips at the lower sample rate hold at most 341 frames; the last clip holds 512.
All inputs are finite; a program needn't handle non-finite values. No bound on the sum of `frame_mask` on one device may be relied on, other than what follows from the above.
Results may differ from the reference program's by a relative error of at most 0.009.
Values may be sent and summed in bfloat16 or wider, within the bound.
A program may use at most 192 MiB of HBM per device.

```python
import math
from functools import partial
import jax
import jax.numpy as jnp
from jax import lax

D = 512
CODE_DIM = 256
GROUPS = 2
LEVELS = 2
CODES = 1024
KERNEL = 3
STEP = 10
MAXLEN = 512
CLIPS = 3
CLIPS_ALL = 96
FRAMES = 49152


def draw_lengths(key, part):
    key = jax.random.fold_in(key, 7)
    rate_key, span_key = jax.random.split(key)
    clip_number = jnp.arange(CLIPS_ALL, dtype=jnp.int32)
    fast_rate = jax.random.randint(rate_key, (CLIPS_ALL,), 0, 2)
    fast_rate = jnp.where(clip_number == CLIPS_ALL - 1, 1, fast_rate)
    ceiling = jnp.where(fast_rate == 1, MAXLEN, 2 * MAXLEN // 3)
    low_end = ceiling * (CLIPS_ALL + 6 * clip_number) // (10 * CLIPS_ALL)
    spread_width = ceiling * 3 // 10 + 1
    extra = jax.random.randint(span_key, (CLIPS_ALL,), 0, 1 << 20) % spread_width
    length_value = jnp.minimum(low_end + extra, ceiling)
    length_value = jnp.where(clip_number == CLIPS_ALL - 1, MAXLEN, length_value)
    return jnp.maximum(length_value, 1).astype(jnp.int32)


def touch_ends(array, stream_key, least, top_value):
    shape = array.shape
    place = [jax.random.randint(jax.random.fold_in(stream_key, axis), (), 0, shape[axis]) for axis in range(len(shape))]
    array = array.at[tuple(place)].set(least)
    longest = shape.index(max(shape))
    place[longest] = (place[longest] + 1) % shape[longest]
    return array.at[tuple(place)].set(top_value)


def block_scale(key, dims, shards, least, top_value):
    gain, own = 1.0, jax.random.fold_in(key, 6)
    for axis_at, shards_of in shards:
        heights = jnp.exp(jax.random.uniform(jax.random.fold_in(own, axis_at), (shards_of,), jnp.float32, least / len(shards), top_value / len(shards)))
        gain = gain * jnp.repeat(heights, dims[axis_at] // shards_of).reshape([-1 if axis == axis_at else 1 for axis in range(len(dims))])
    return gain


def gaussian(own_key, shape, width, bound, cuts=(), kind=jnp.bfloat16):
    drawn = width * jax.random.normal(own_key, shape, jnp.float32)
    if cuts:
        drawn = drawn * block_scale(own_key, shape, cuts, -0.22, 0.18)
    return jnp.clip(drawn, -bound, bound).astype(kind)


def setup_inputs(seed: int = 0) -> dict:
    key_of = jax.random.split(jax.random.key(seed), 15)
    return {
        "frames": gaussian(key_of[0], (FRAMES, D), 1.0, 6.0, ((0, 16),)),
        "cotangent": gaussian(key_of[1], (FRAMES, D), 1.0, 6.0, ((0, 16), (1, 2))),
        "lengths": draw_lengths(jax.random.fold_in(key_of[14], 71), 0),
        "frame_mask": touch_ends((jax.random.randint(key_of[3], (FRAMES,), 0, 16) < 15).astype(jnp.int32), jax.random.fold_in(key_of[3], 1), 0, 1),
        "code_index": touch_ends(jax.random.randint(key_of[4], (LEVELS, FRAMES, GROUPS), 0, CODES), jax.random.fold_in(key_of[4], 1), 0, CODES - 1).astype(jnp.int32),
        "conv_weight": gaussian(key_of[5], (2, KERNEL, D, D), (KERNEL * D) ** -0.5, 0.15625, ((2, 16), (3, 2)), jnp.float32),
        "proj_weight": gaussian(key_of[6], (2, D, D), D ** -0.5, 0.25, ((1, 16), (2, 2)), jnp.float32),
        "codebooks": gaussian(key_of[7], (LEVELS, CODES, D), 1.0, 6.0, ((1, 16), (2, 2)), jnp.float32),
        "conv_rows": jnp.clip(jnp.exp(math.log(7569408) - 1.37339096 * jax.random.uniform(key_of[8], (2, KERNEL, D), jnp.float32) ** block_scale(key_of[8], (2, KERNEL, D), ((2, 16),), -0.2, 0.2)), 1916928, 7569408),
        "conv_cols": jnp.clip(jnp.exp(math.log(23003136) - 1.3862944 * jax.random.uniform(key_of[9], (2, D), jnp.float32) ** block_scale(key_of[9], (2, D), ((1, 2),), -0.2, 0.2)), 5750784, 23003136),
        "proj_rows": jnp.clip(jnp.exp(math.log(28311552) - 1.372501 * jax.random.uniform(key_of[10], (2, D), jnp.float32) ** block_scale(key_of[10], (2, D), ((1, 16),), -0.2, 0.2)), 7176192, 28311552),
        "proj_cols": jnp.clip(jnp.exp(math.log(28311552) - 1.372501 * jax.random.uniform(key_of[11], (2, D), jnp.float32) ** block_scale(key_of[11], (2, D), ((1, 2),), -0.2, 0.2)), 7176192, 28311552),
        "book_rows": jnp.clip(jnp.exp(math.log(0.0001566569) - 1.37339097 * jax.random.uniform(key_of[12], (LEVELS, CODES), jnp.float32) ** block_scale(key_of[12], (LEVELS, CODES), ((1, 16),), -0.2, 0.2)), 3.967285010730848e-05, 0.0001566569),
        "book_cols": jnp.clip(jnp.exp(math.log(0.0003133138) - 1.37339097 * jax.random.uniform(key_of[13], (LEVELS, D), jnp.float32) ** block_scale(key_of[13], (LEVELS, D), ((1, 2),), -0.2, 0.2)), 7.934570021461695e-05, 0.0003133138),
    }


@jax.custom_vjp
def low(v):
    return lax.optimization_barrier(v.astype(jnp.bfloat16)).astype(jnp.float32)

@jax.custom_vjp
def low_back(v):
    return v

def low_keep(v):
    return (low(v), None)

def low_pass(kept, grad):
    return (grad,)

def back_keep(v):
    return (v, None)

def back_low(kept, grad):
    return (low(grad),)
low.defvjp(low_keep, low_pass)
low_back.defvjp(back_keep, back_low)
highest = lax.Precision.HIGHEST
square_floor = 1e-30
clip_level = 0.5

def shifted(signal):
    length = signal.shape[1]
    padded = jnp.pad(signal, ((0, 0), (1, 1), (0, 0)))
    return jnp.concatenate([padded[:, 0:length], padded[:, 1:length + 1], padded[:, 2:length + 2]], axis=2)

def convolve(signal, kernel):
    flat = kernel.reshape(kernel.shape[0] * kernel.shape[1], kernel.shape[2])
    return jnp.einsum('blc,cd->bld', shifted(signal), flat, precision=highest)

def lookup(codebook, selected):
    pieces = []
    for group_index in range(GROUPS):
        columns = codebook[:, group_index * CODE_DIM:(group_index + 1) * CODE_DIM]
        pieces.append(jnp.take(columns, selected[..., group_index], axis=0))
    return jnp.concatenate(pieces, axis=-1)

def forward(shift_term, live_mask, selected, live_total, conv_master, proj_master, book_master, frame_input):
    conv_low = low(conv_master)
    proj_low = low(proj_master)
    book_low = low(book_master)
    activated = low(jax.nn.gelu(frame_input) * live_mask)
    branch = low_back(convolve(activated, conv_low[0]))
    encoded = (frame_input + branch) * live_mask
    latent = low_back(jnp.einsum('bld,de->ble', low(encoded), proj_low[0], precision=highest))
    level_one = low_back(lookup(book_low[0], selected[0]))
    level_two = low_back(lookup(book_low[1], selected[1]))
    quantized = level_one + level_two
    straight = low(latent + shift_term)
    decoded = low_back(jnp.einsum('bld,de->ble', straight, proj_low[1], precision=highest))
    decoder_in = low(jax.nn.gelu(decoded) * live_mask)
    result = (decoded + convolve(decoder_in, conv_low[1])) * live_mask
    resid_one = latent - level_one
    resid_two = resid_one - level_two
    loss = jnp.sum(live_mask * (resid_one * resid_one + resid_two * resid_two)) / live_total
    return ((result, loss), (latent, quantized))

def adafactor(gradient, weight, row_state, col_state, step_rate):
    beta_two = 1.0 - STEP ** (-0.8)
    squares = gradient * gradient + square_floor
    middle = tuple(range(1, gradient.ndim - 1))
    new_rows = beta_two * row_state + (1.0 - beta_two) * lax.optimization_barrier(jnp.sum(squares, axis=-1))
    new_cols = beta_two * col_state + (1.0 - beta_two) * lax.optimization_barrier(jnp.sum(squares, axis=middle))
    row_total = lax.optimization_barrier(jnp.sum(new_rows, axis=middle))
    shape_cols = (col_state.shape[0],) + (1,) * len(middle) + (col_state.shape[1],)
    shape_total = (col_state.shape[0],) + (1,) * (gradient.ndim - 1)
    estimate = new_rows[..., None] * new_cols.reshape(shape_cols) / row_total.reshape(shape_total)
    update = gradient * lax.rsqrt(estimate)
    all_axes = tuple(range(1, gradient.ndim))
    root_mean = jnp.sqrt(lax.optimization_barrier(jnp.mean(update * update, axis=all_axes)))
    factor = jnp.maximum(1.0, root_mean / clip_level).reshape(shape_total)
    return (new_rows, new_cols, weight - step_rate * (update / factor))

def reference(frames, cotangent, lengths, frame_mask, code_index, conv_weight, proj_weight, codebooks, conv_rows, conv_cols, proj_rows, proj_cols, book_rows, book_cols):
    clip_count = lengths.shape[0]
    step_count = clip_count // CLIPS
    position = jnp.arange(MAXLEN, dtype=jnp.int32)
    live = (position[None, :] < lengths[:, None]) & (frame_mask.reshape(clip_count, MAXLEN) > 0)
    live_mask = live.astype(jnp.float32)[:, :, None]
    live_total = jnp.sum(live_mask)
    frame_blocks = frames.astype(jnp.float32).reshape(step_count, CLIPS, MAXLEN, D)
    cot_blocks = cotangent.astype(jnp.float32).reshape(step_count, CLIPS, MAXLEN, D)
    mask_blocks = live_mask.reshape(step_count, CLIPS, MAXLEN, 1)
    index_blocks = jnp.moveaxis(code_index.reshape(LEVELS, step_count, CLIPS, MAXLEN, GROUPS), 1, 0)

    def advance(running, inputs):
        frame_block, cot_block, mask_block, index_block = inputs
        zero_shift = jnp.zeros((CLIPS, MAXLEN, D), jnp.float32)
        kept = forward(zero_shift, mask_block, index_block, live_total, conv_weight, proj_weight, codebooks, frame_block)[1]
        shift_term = kept[1] - kept[0]
        primal, pullback, unused = jax.vjp(partial(forward, shift_term, mask_block, index_block, live_total), conv_weight, proj_weight, codebooks, frame_block, has_aux=True)
        gradients = pullback((cot_block, jnp.ones((), jnp.float32)))
        running = (running[0] + gradients[0], running[1] + gradients[1], running[2] + gradients[2])
        return (running, (primal[0].astype(jnp.bfloat16), gradients[3].astype(jnp.bfloat16)))
    start_sums = (jnp.zeros(conv_weight.shape, jnp.float32), jnp.zeros(proj_weight.shape, jnp.float32), jnp.zeros(codebooks.shape, jnp.float32))
    sums, stacked = lax.scan(advance, start_sums, (frame_blocks, cot_blocks, mask_blocks, index_blocks))
    decoded_out = stacked[0].reshape(clip_count * MAXLEN, D)
    input_grad = stacked[1].reshape(clip_count * MAXLEN, D)
    rate_conv = 2.0 / math.sqrt(KERNEL * D)
    rate_proj = 2.0 / math.sqrt(D)
    conv_new = adafactor(sums[0], conv_weight, conv_rows, conv_cols, rate_conv)
    proj_new = adafactor(sums[1], proj_weight, proj_rows, proj_cols, rate_proj)
    book_new = adafactor(sums[2], codebooks, book_rows, book_cols, 2.0)
    return (decoded_out, input_grad, sums[0], sums[1], sums[2], conv_new[0], conv_new[1], proj_new[0], proj_new[1], book_new[0], book_new[1], conv_new[2], proj_new[2], book_new[2])
```

```python
import functools
import math

import jax
import jax.numpy as jnp
from jax import lax
from jax.experimental import pallas as pl
from jax.experimental.pallas import tpu as pltpu
from jax.sharding import PartitionSpec as P

D = 512
CODES = 1024
KERNEL = 3
STEP = 10
MAXLEN = 512
MICRO = 2


square_floor = 1e-30
clip_level = 0.5
f32 = jnp.float32
bf16 = jnp.bfloat16


def shifted(signal, length):
    channels = signal.shape[-1]
    blocks = signal.reshape(-1, length, channels)
    padded = jnp.pad(blocks, ((0, 0), (1, 1), (0, 0)))
    joined = jnp.concatenate(
        [padded[:, 0:length], padded[:, 1 : length + 1], padded[:, 2 : length + 2]], axis=2
    )
    return joined.reshape(-1, 3 * channels)


def unshift(partial_terms, length):
    channels = partial_terms.shape[-1] // 3
    blocks = partial_terms.reshape(-1, length, 3, channels)
    padded = jnp.pad(blocks, ((0, 0), (1, 1), (0, 0), (0, 0)))
    summed = padded[:, 2 : length + 2, 0] + padded[:, 1 : length + 1, 1] + padded[:, 0:length, 2]
    return summed.reshape(-1, channels)


def gelu_back(values, upstream):
    return jax.vjp(jax.nn.gelu, values)[1](upstream)[0]


def fetch(conv_weight, proj_weight, codebooks):
    return (
        lax.all_gather(conv_weight.astype(bf16), "dp", axis=2, tiled=True),
        lax.all_gather(proj_weight.astype(bf16), "dp", axis=1, tiled=True),
        lax.all_gather(codebooks.astype(bf16), "dp", axis=1, tiled=True),
    )


def reduce_grads(conv_total, proj_total, book_total):
    return (
        lax.psum_scatter(conv_total, "dp", scatter_dimension=2, tiled=True),
        lax.psum_scatter(proj_total, "dp", scatter_dimension=1, tiled=True),
        lax.psum_scatter(book_total, "dp", scatter_dimension=1, tiled=True),
    )


def contract(left, right):
    return jnp.einsum("fc,fd->cd", left, right, preferred_element_type=f32)


def transpose_product(left, right):
    return jnp.einsum("fd,cd->fc", left, right, preferred_element_type=f32)


def general_body(
    frames,
    cotangent,
    lengths,
    frame_mask,
    code_index,
    conv_weight,
    proj_weight,
    codebooks,
    conv_rows,
    conv_cols,
    proj_rows,
    proj_cols,
    book_rows,
    book_cols,
):
    length = MAXLEN
    block_rows = frames.shape[0] // MICRO
    half_width = cotangent.shape[1]
    chan_place = lax.axis_index("chan")
    row_place = jnp.arange(frames.shape[0], dtype=jnp.int32) % length
    live = (row_place < jnp.repeat(lengths, length, total_repeat_length=frames.shape[0])) & (
        frame_mask > 0
    )
    weight_mask = live.astype(f32)[:, None]
    live_total = lax.psum(jnp.sum(weight_mask), "dp")
    vq_scale = 2.0 / live_total
    running = None
    out_pieces = []
    grad_pieces = []
    for block_number in range(MICRO):
        first_row = block_number * block_rows
        last_row = first_row + block_rows
        conv_bank, proj_bank, book_bank = fetch(conv_weight, proj_weight, codebooks)
        conv_enc = conv_bank[0].reshape(-1, half_width)
        conv_dec = conv_bank[1].reshape(-1, half_width)
        frame_part = frames[first_row:last_row]
        frame_wide = frame_part.astype(f32)
        own_part = lax.dynamic_slice_in_dim(frame_wide, chan_place * half_width, half_width, 1)
        masked = weight_mask[first_row:last_row]
        cot_part = jnp.where(masked > 0, cotangent[first_row:last_row], jnp.zeros((), bf16))
        code_range = jnp.arange(book_bank.shape[1], dtype=jnp.int32)
        onehot_one = (code_index[0, first_row:last_row, 0][:, None] == code_range[None, :]).astype(
            bf16
        )
        onehot_two = (code_index[1, first_row:last_row, 0][:, None] == code_range[None, :]).astype(
            bf16
        )
        activated = (jax.nn.gelu(frame_wide) * masked).astype(bf16)
        stack_one = shifted(activated, length)
        branch = jnp.dot(stack_one, conv_enc, preferred_element_type=f32)
        encoded = (own_part + branch) * masked
        enc_full = lax.all_gather(encoded.astype(bf16), "chan", axis=1, tiled=True)
        latent = jnp.dot(enc_full, proj_bank[0], preferred_element_type=f32)
        level_one = jnp.dot(onehot_one, book_bank[0], preferred_element_type=f32)
        level_two = jnp.dot(onehot_two, book_bank[1], preferred_element_type=f32)
        quantized = level_one + level_two
        straight = (latent + (quantized - latent)).astype(bf16)
        straight_full = lax.all_gather(straight, "chan", axis=1, tiled=True)
        decoded = jnp.dot(straight_full, proj_bank[1], preferred_element_type=f32)
        decoder_in = (jax.nn.gelu(decoded) * masked).astype(bf16)
        decoder_full = lax.all_gather(decoder_in, "chan", axis=1, tiled=True)
        stack_two = shifted(decoder_full, length)
        result = (decoded + jnp.dot(stack_two, conv_dec, preferred_element_type=f32)) * masked
        out_pieces.append(result.astype(bf16))
        conv_dec_grad = contract(stack_two, cot_part)
        in_partial = unshift(transpose_product(cot_part, conv_dec), length)
        in_back = lax.psum_scatter(in_partial, "chan", scatter_dimension=1, tiled=True)
        decoded_back = (cot_part.astype(f32) + gelu_back(decoded, masked * in_back)).astype(bf16)
        proj_dec_grad = contract(straight_full, decoded_back)
        straight_back = lax.psum_scatter(
            transpose_product(decoded_back, proj_bank[1]), "chan", scatter_dimension=1, tiled=True
        )
        resid_one = latent - level_one
        resid_two = resid_one - level_two
        pulled = vq_scale * masked * (resid_one + resid_two)
        latent_back = (straight_back + pulled).astype(bf16)
        one_back = (-pulled).astype(bf16)
        two_back = (-(vq_scale * masked * resid_two)).astype(bf16)
        book_one_grad = contract(onehot_one, one_back)
        book_two_grad = contract(onehot_two, two_back)
        proj_enc_grad = contract(enc_full, latent_back)
        encoded_back = lax.psum_scatter(
            transpose_product(latent_back, proj_bank[0]), "chan", scatter_dimension=1, tiled=True
        )
        branch_back = (encoded_back * masked).astype(bf16)
        conv_enc_grad = contract(stack_one, branch_back)
        activated_back = unshift(transpose_product(branch_back, conv_enc), length)
        input_partial = gelu_back(frame_wide, masked * activated_back)
        input_own = lax.psum_scatter(input_partial, "chan", scatter_dimension=1, tiled=True)
        grad_pieces.append((encoded_back * masked + input_own).astype(bf16))
        conv_blockgrad = jnp.stack(
            [
                conv_enc_grad.reshape(KERNEL, -1, half_width),
                conv_dec_grad.reshape(KERNEL, -1, half_width),
            ]
        )
        proj_blockgrad = jnp.stack([proj_enc_grad, proj_dec_grad])
        book_blockgrad = jnp.stack([book_one_grad, book_two_grad])
        reduced = reduce_grads(conv_blockgrad, proj_blockgrad, book_blockgrad)
        running = (
            reduced
            if running is None
            else (running[0] + reduced[0], running[1] + reduced[1], running[2] + reduced[2])
        )
    conv_grad, proj_grad, book_grad = running
    decoded_out = jnp.concatenate(out_pieces, axis=0)
    input_grad = jnp.concatenate(grad_pieces, axis=0)
    beta_two = 1.0 - STEP ** (-0.8)
    squares_conv = conv_grad * conv_grad + square_floor
    squares_proj = proj_grad * proj_grad + square_floor
    squares_book = book_grad * book_grad + square_floor
    row_sums = lax.psum(
        (
            jnp.sum(squares_conv, axis=3),
            jnp.sum(squares_proj, axis=2),
            jnp.sum(squares_book, axis=2),
        ),
        "chan",
    )
    rowstat_conv = beta_two * conv_rows + (1.0 - beta_two) * row_sums[0]
    rowstat_proj = beta_two * proj_rows + (1.0 - beta_two) * row_sums[1]
    rowstat_book = beta_two * book_rows + (1.0 - beta_two) * row_sums[2]
    col_sums = lax.psum(
        (
            jnp.sum(squares_conv, axis=(1, 2)),
            jnp.sum(squares_proj, axis=1),
            jnp.sum(squares_book, axis=1),
            jnp.sum(rowstat_conv, axis=(1, 2)),
            jnp.sum(rowstat_proj, axis=1),
            jnp.sum(rowstat_book, axis=1),
        ),
        "dp",
    )
    colstat_conv = beta_two * conv_cols + (1.0 - beta_two) * col_sums[0]
    colstat_proj = beta_two * proj_cols + (1.0 - beta_two) * col_sums[1]
    colstat_book = beta_two * book_cols + (1.0 - beta_two) * col_sums[2]
    update_conv = conv_grad * lax.rsqrt(
        rowstat_conv[..., None] * colstat_conv[:, None, None, :] / col_sums[3][:, None, None, None]
    )
    update_proj = proj_grad * lax.rsqrt(
        rowstat_proj[..., None] * colstat_proj[:, None, :] / col_sums[4][:, None, None]
    )
    update_book = book_grad * lax.rsqrt(
        rowstat_book[..., None] * colstat_book[:, None, :] / col_sums[5][:, None, None]
    )
    norm_sums = lax.psum(
        (
            jnp.sum(update_conv * update_conv, axis=(1, 2, 3)),
            jnp.sum(update_proj * update_proj, axis=(1, 2)),
            jnp.sum(update_book * update_book, axis=(1, 2)),
        ),
        ("dp", "chan"),
    )
    factor_conv = jnp.maximum(1.0, jnp.sqrt(norm_sums[0] / (KERNEL * D * D)) / clip_level)
    factor_proj = jnp.maximum(1.0, jnp.sqrt(norm_sums[1] / (D * D)) / clip_level)
    factor_book = jnp.maximum(1.0, jnp.sqrt(norm_sums[2] / (CODES * D)) / clip_level)
    rate_conv = 2.0 / math.sqrt(KERNEL * D)
    rate_proj = 2.0 / math.sqrt(D)
    updated_conv = conv_weight - rate_conv * (update_conv / factor_conv[:, None, None, None])
    updated_proj = proj_weight - rate_proj * (update_proj / factor_proj[:, None, None])
    updated_book = codebooks - 2.0 * (update_book / factor_book[:, None, None])
    return (
        decoded_out,
        input_grad,
        conv_grad,
        proj_grad,
        book_grad,
        rowstat_conv,
        colstat_conv,
        rowstat_proj,
        colstat_proj,
        rowstat_book,
        colstat_book,
        updated_conv,
        updated_proj,
        updated_book,
    )


MESH = pl.DeviceIdType.MESH
CLIPS = 3
ROWS = CLIPS * MAXLEN
GROUPS12 = 12
NZ, NY, NX = 4, 2, 2
BLOCK = 32
HALF = 256
GELU_A = math.sqrt(2.0 / math.pi)
GELU_B = 0.044715
MATRICES = ((0, 3), (3, 4), (4, 6), (6, 8), (8, 9), (9, 12))


def gelu_pair(x):
    x2 = x * x
    t = jnp.tanh(GELU_A * x * (1.0 + GELU_B * x2))
    half = 0.5 * (1.0 + t)
    return x * half, half + 0.5 * x * (1.0 - t * t) * (GELU_A + 3.0 * GELU_A * GELU_B * x2)


def lanes(m, n):
    return jnp.concatenate([m] * n, axis=1)


def dot_nn(a, b):
    return jnp.dot(a, b, preferred_element_type=f32)


def dot_nt(a, b):
    return lax.dot_general(a, b, (((1,), (1,)), ((), ())), preferred_element_type=f32)


def neighbours(v):
    rows = lax.broadcasted_iota(jnp.int32, v.shape, 0)
    before = jnp.where(rows == 0, 0.0, pltpu.roll(v, 1, 0))
    after = jnp.where(rows == v.shape[0] - 1, 0.0, pltpu.roll(v, v.shape[0] - 1, 0))
    return before.astype(bf16), after.astype(bf16)


def fused_kernel(
    lengths,
    frames_hbm,
    cot_hbm,
    frame_mask,
    code_index,
    conv_weight,
    proj_weight,
    codebooks,
    old_rows,
    conv_cols,
    proj_cols,
    book_cols,
    out_hbm,
    input_hbm,
    conv_grad,
    proj_grad,
    book_grad,
    rows_out,
    conv_cols_out,
    proj_cols_out,
    book_cols_out,
    conv_new,
    proj_new,
    book_new,
    W,
    G,
    RP,
    AX,
    AY,
    BX,
    BY,
    BXS,
    BYS,
    TS,
    ZR,
    GF,
    FR,
    S,
    O,
    AT,
    ENCT,
    STRT,
    DINT,
    LAT,
    DEC,
    DGD,
    B1,
    B2,
    STR,
    DB,
    LB,
    OB,
    MASK,
    IDX,
    CN,
    ST,
    STS,
    NM,
    NMP,
    NMS,
    RSUM,
    RSUMP,
    ssem,
    rsem,
    lsem,
):
    me = lax.axis_index("dp")
    c = lax.axis_index("chan")
    z, y, x = me // (NY * NX), (me // NX) % NY, me % NX
    peers = NZ * NY * NX
    far_y, far_x, other = 1 - y, 1 - x, 1 - c

    def dp_of(zz, yy, xx):
        return (zz * (NY * NX) + yy * NX + xx, c)

    dev_x, dev_y, dev_peer = dp_of(z, y, far_x), dp_of(z, far_y, x), (me, other)
    cols = pl.ds(pl.multiple_of(c * HALF, HALF), HALF)
    cols_other = pl.ds(pl.multiple_of(other * HALF, HALF), HALF)
    quarter = (
        pl.ds(pl.multiple_of(c * HALF, HALF), 128),
        pl.ds(pl.multiple_of(c * HALF + 128, 128), 128),
    )
    mine = pl.ds(pl.multiple_of(c * ROWS, ROWS), ROWS)
    theirs = pl.ds(pl.multiple_of(other * ROWS, ROWS), ROWS)

    counter = [0]
    unsent = []

    def place(n=1):
        counter[0] += n
        return counter[0] - n

    def send(src, dst, dev, at):
        copy = pltpu.make_async_remote_copy(
            src_ref=src,
            dst_ref=dst,
            send_sem=ssem.at[at],
            recv_sem=rsem.at[at],
            device_id=dev,
            device_id_type=MESH,
        )
        copy.start()
        unsent.append(copy)

    def arrived(dst, at):
        pltpu.make_async_remote_copy(
            src_ref=dst,
            dst_ref=dst,
            send_sem=ssem.at[at],
            recv_sem=rsem.at[at],
            device_id=dev_peer,
            device_id_type=MESH,
        ).wait_recv()

    frames_in = pltpu.make_async_copy(frames_hbm.at[mine, :], FR, lsem.at[0])
    frames_in.start()
    cot_in = pltpu.make_async_copy(cot_hbm.at[mine, :], OB.at[:, cols], lsem.at[1])
    cot_in.start()
    index_in = pltpu.make_async_copy(code_index.at[:, c], IDX.at[:, c], lsem.at[2])
    index_in.start()
    barrier = pltpu.get_barrier_semaphore()
    for k in range(1, peers):
        pl.semaphore_signal(barrier, inc=1, device_id=(lax.rem(me + k, peers), c), device_id_type=MESH)
    pl.semaphore_signal(barrier, inc=1, device_id=dev_peer, device_id_type=MESH)

    for k in range(3):
        W[k, z, y, x, :, cols] = conv_weight[0, k].astype(bf16)
        W[9 + k, z, y, x, :, cols] = conv_weight[1, k].astype(bf16)
    W[3, z, y, x, :, cols] = proj_weight[0].astype(bf16)
    W[8, z, y, x, :, cols] = proj_weight[1].astype(bf16)
    for level in range(2):
        for t in range(2):
            W[4 + 2 * level + t, z, y, x, :, cols] = codebooks[level, BLOCK * t : BLOCK * (t + 1)].astype(bf16)
    lane_row = lax.broadcasted_iota(jnp.int32, (1, MAXLEN), 1)
    count = jnp.zeros((1, MAXLEN), f32)
    for core in range(2):
        for b in range(CLIPS):
            live = (lane_row < lengths[core * CLIPS + b]) & (frame_mask[core, b] > 0)
            count = count + jnp.where(live, 1.0, 0.0)
    CN[peers - 1] = jnp.broadcast_to(jnp.sum(count, axis=1, keepdims=True), (8, 128))
    pl.semaphore_wait(barrier, peers)

    pieces = ((0, 3), (3, 8), (8, 12))
    at_z = [place(3) for p in pieces]
    at_l = [place(2) for p in pieces]
    at_d = [place(2) for p in pieces]
    at_p = [place(2) for p in pieces]
    at_cot, at_idx, at_count = place(), place(), place()

    def gather_z(p):
        g0, g1 = pieces[p]
        own = W.at[g0:g1, z, y, x, :, cols]
        for k in range(1, NZ):
            send(own, own, dp_of(lax.rem(z + k, NZ), y, x), at_z[p] + k - 1)

    def gather_line(p):
        g0, g1 = pieces[p]
        for k in range(1, NZ):
            arrived(W.at[g0:g1, lax.rem(z + NZ - k, NZ), y, x, :, cols], at_z[p] + k - 1)
        line = W.at[g0:g1, :, y, x, :, cols]
        send(line, line, dev_x, at_l[p])
        send(line, line, dev_y, at_l[p] + 1)

    def gather_diagonal(p):
        g0, g1 = pieces[p]
        arrived(W.at[g0:g1, :, y, far_x, :, cols], at_l[p])
        arrived(W.at[g0:g1, :, far_y, x, :, cols], at_l[p] + 1)
        part = W.at[g0:g1, :, far_y, x, :, quarter[0]]
        send(part, part, dev_x, at_d[p])
        part = W.at[g0:g1, :, y, far_x, :, quarter[1]]
        send(part, part, dev_y, at_d[p] + 1)
        part = W.at[g0:g1, :, y, :, :, cols]
        send(part, part, dev_peer, at_p[p])

    def gather_peer(p):
        g0, g1 = pieces[p]
        arrived(W.at[g0:g1, :, far_y, far_x, :, quarter[0]], at_d[p])
        arrived(W.at[g0:g1, :, far_y, far_x, :, quarter[1]], at_d[p] + 1)
        part = W.at[g0:g1, :, far_y, :, :, cols]
        send(part, part, dev_peer, at_p[p] + 1)

    def gathered(p):
        g0, g1 = pieces[p]
        arrived(W.at[g0:g1, :, y, :, :, cols_other], at_p[p])
        arrived(W.at[g0:g1, :, far_y, :, :, cols_other], at_p[p] + 1)

    parts = ((4, 8), (8, 12), (0, 4))
    at_rp = [place() for p in parts]
    at_ra = [place(2) for p in parts]
    at_rb = [place(2) for p in parts]
    at_rz = [place(3) for p in parts]

    def reduce_peer(p):
        g0, g1 = parts[p]
        send(G.at[other, g0:g1], RP.at[g0:g1], dev_peer, at_rp[p])

    def reduce_a(p):
        g0, g1 = parts[p]
        arrived(RP.at[g0:g1], at_rp[p])

        @pl.loop(g0, g1)
        def _(g):
            G[c, g] = (G[c, g].astype(f32) + RP[g].astype(f32)).astype(bf16)

        send(G.at[c, g0:g1, :, :, far_x, :, 0:128], AX.at[g0:g1], dev_x, at_ra[p])
        send(G.at[c, g0:g1, :, far_y, :, :, 128:256], AY.at[g0:g1], dev_y, at_ra[p] + 1)

    def reduce_b(p):
        g0, g1 = parts[p]
        arrived(AX.at[g0:g1], at_ra[p])
        arrived(AY.at[g0:g1], at_ra[p] + 1)

        @pl.loop(g0, g1)
        def _(g):
            BXS[g] = (G[c, g, :, y, far_x, :, 128:256].astype(f32) + AY[g, :, far_x].astype(f32)).astype(bf16)
            BYS[g] = (G[c, g, :, far_y, x, :, 0:128].astype(f32) + AX[g, :, far_y].astype(f32)).astype(bf16)

        send(BXS.at[g0:g1], BX.at[g0:g1], dev_x, at_rb[p])
        send(BYS.at[g0:g1], BY.at[g0:g1], dev_y, at_rb[p] + 1)

    def reduce_z(p):
        g0, g1 = parts[p]
        arrived(BX.at[g0:g1], at_rb[p])
        arrived(BY.at[g0:g1], at_rb[p] + 1)

        @pl.loop(g0, g1)
        def _(g):
            base = G[c, g, :, y, x].astype(f32)
            left = base[:, :, 0:128] + (AX[g, :, y].astype(f32) + BY[g].astype(f32))
            right = base[:, :, 128:256] + (AY[g, :, x].astype(f32) + BX[g].astype(f32))
            TS[g, :, :, 0:128] = left.astype(bf16)
            TS[g, :, :, 128:256] = right.astype(bf16)

        for k in range(1, NZ):
            to = lax.rem(z + k, NZ)
            send(TS.at[g0:g1, to], ZR.at[k - 1, g0:g1], dp_of(to, y, x), at_rz[p] + k - 1)

    def reduce_end(p):
        g0, g1 = parts[p]
        for k in range(1, NZ):
            arrived(ZR.at[k - 1, g0:g1], at_rz[p] + k - 1)

        @pl.loop(g0, g1)
        def _(g):
            GF[g] = (TS[g, z].astype(f32) + ZR[0, g].astype(f32)) + (ZR[1, g].astype(f32) + ZR[2, g].astype(f32))

    def w(a, b):
        return W[a:b].reshape((b - a) * D, D)

    def each(step):
        pl.loop(0, CLIPS)(lambda b: step(b, pl.multiple_of(b * MAXLEN, MAXLEN)))

    def put(half, group, value):
        G[half, group] = value.astype(bf16).reshape(NZ, NY, NX, BLOCK, HALF)

    gather_z(0)
    gather_z(1)
    gather_z(2)
    for k in range(1, peers):
        send(CN.at[peers - 1], CN.at[k - 1], (lax.rem(me + k, peers), c), at_count)
        unsent.pop()
    send(code_index.at[:, other], IDX.at[:, c], dev_peer, at_idx)
    send(cot_hbm.at[theirs, :], OB.at[:, cols], dev_peer, at_cot)

    @pl.loop(0, CLIPS)
    def _(b):
        live = (lane_row < lengths[c * CLIPS + b]) & (frame_mask[c, b] > 0)
        row = jnp.where(live, 1.0, 0.0)
        MASK[pl.ds(pl.multiple_of(b * MAXLEN, MAXLEN), MAXLEN), :] = jnp.broadcast_to(row, (128, MAXLEN)).T

    frames_in.wait()

    def activate(b, r0):
        m = lanes(MASK[pl.ds(r0, MAXLEN), :], 4)
        a = gelu_pair(FR[pl.ds(r0, MAXLEN), :].astype(f32))[0] * m
        before, after = neighbours(a)
        a = a.astype(bf16)
        S[pl.ds(r0, MAXLEN), 0:D] = before
        S[pl.ds(r0, MAXLEN), D : 2 * D] = a
        S[pl.ds(r0, MAXLEN), 2 * D : 3 * D] = after
        AT[:, pl.ds(r0, MAXLEN)] = a.T

    each(activate)
    gather_line(0)
    cot_in.wait()
    index_in.wait()
    arrived(OB.at[:, cols_other], at_cot)
    arrived(IDX.at[:, other], at_idx)

    def upstream(b, r0):
        m = lanes(MASK[pl.ds(r0, MAXLEN), :], 4)
        ob = OB[pl.ds(r0, MAXLEN), :].astype(f32) * m
        before, after = neighbours(ob)
        O[pl.ds(r0, MAXLEN), 0:D] = after
        O[pl.ds(r0, MAXLEN), D : 2 * D] = ob.astype(bf16)
        O[pl.ds(r0, MAXLEN), 2 * D : 3 * D] = before

    each(upstream)
    gather_diagonal(0)
    gather_line(1)
    gather_peer(0)
    arrived(CN.at[0 : peers - 1], at_count)
    scale = 2.0 / jnp.sum(CN[...], axis=0)[0:1]
    gathered(0)

    def encode(b, r0):
        m = lanes(MASK[pl.ds(r0, MAXLEN), :], 4)
        branch = dot_nn(S[pl.ds(r0, MAXLEN), :], w(0, 3))
        enc = ((FR[pl.ds(r0, MAXLEN), :].astype(f32) + branch) * m).astype(bf16)
        STR[pl.ds(r0, MAXLEN), :] = enc
        ENCT[:, pl.ds(r0, MAXLEN)] = enc.T

    each(encode)
    gather_diagonal(1)
    gather_line(2)
    gather_peer(1)
    gathered(1)
    gather_diagonal(2)

    def project(b, r0):
        LAT[pl.ds(r0, MAXLEN), :] = dot_nn(STR[pl.ds(r0, MAXLEN), :], w(3, 4))

    each(project)

    def slot(row):
        return ((row >> 5) & 1) * 512 + (row >> 6) * BLOCK + (row & 31)

    def quantize(b, r0):
        m = lanes(MASK[pl.ds(r0, MAXLEN), :], 2)
        sc = lanes(scale, 2) * m
        lane = lax.broadcasted_iota(jnp.int32, (MAXLEN, 128), 1)
        for g in range(2):
            gc = slice(HALF * g, HALF * (g + 1))
            level = []
            for l in range(2):
                col = jnp.broadcast_to(slot(IDX[l, g, b]), (128, MAXLEN)).T
                onehot = jnp.concatenate(
                    [jnp.where(col == lane + 128 * k, 1.0, 0.0).astype(bf16) for k in range(CODES // 128)], axis=1
                )
                book = W[4 + 2 * l : 6 + 2 * l, :, :, :, :, gc].reshape(CODES, HALF)
                level.append(dot_nn(onehot, book))
            latent = LAT[pl.ds(r0, MAXLEN), gc]
            quantized = level[0] + level[1]
            straight = (latent + (quantized - latent)).astype(bf16)
            resid_one = latent - level[0]
            resid_two = resid_one - level[1]
            pulled = sc * (resid_one + resid_two)
            STR[pl.ds(r0, MAXLEN), gc] = straight
            STRT[gc, pl.ds(r0, MAXLEN)] = straight.T
            LAT[pl.ds(r0, MAXLEN), gc] = pulled
            B1[pl.ds(r0, MAXLEN), gc] = (-pulled).astype(bf16)
            B2[pl.ds(r0, MAXLEN), gc] = (-(sc * resid_two)).astype(bf16)

    each(quantize)
    gather_peer(2)

    for l, back in ((0, B1), (1, B2)):

        @pl.loop(0, 4)
        def _(part):
            code = lax.broadcasted_iota(jnp.int32, (256, MAXLEN), 0) + part * 256
            for g in range(2):
                onehot = jnp.concatenate(
                    [
                        jnp.where(jnp.broadcast_to(slot(IDX[l, g, b]), (256, MAXLEN)) == code, 1.0, 0.0).astype(bf16)
                        for b in range(CLIPS)
                    ],
                    axis=1,
                )
                value = dot_nn(onehot, back[:, HALF * g : HALF * (g + 1)]).astype(bf16)
                G[g, 4 + 2 * l + part // 2, pl.ds((part % 2) * 2, 2)] = value.reshape(2, NY, NX, BLOCK, HALF)

    reduce_peer(0)
    gathered(2)

    def decode(b, r0):
        m = lanes(MASK[pl.ds(r0, MAXLEN), :], 4)
        dec = dot_nn(STR[pl.ds(r0, MAXLEN), :], w(8, 9))
        DEC[pl.ds(r0, MAXLEN), :] = dec
        value, slope = gelu_pair(dec)
        value = value * m
        DGD[pl.ds(r0, MAXLEN), :] = slope * m
        before, after = neighbours(value)
        value = value.astype(bf16)
        S[pl.ds(r0, MAXLEN), 0:D] = before
        S[pl.ds(r0, MAXLEN), D : 2 * D] = value
        S[pl.ds(r0, MAXLEN), 2 * D : 3 * D] = after
        DINT[:, pl.ds(r0, MAXLEN)] = value.T

    each(decode)
    reduce_a(0)

    def kernel_grad(left, base):
        @pl.loop(0, KERNEL)
        def _(k):
            for half in range(2):
                right = O[:, pl.ds(pl.multiple_of(k * D + half * HALF, HALF), HALF)]
                put(half, base + k, dot_nn(left[...], right))

    kernel_grad(DINT, 9)
    reduce_b(0)

    def decode_back(b, r0):
        total = None
        for k in range(KERNEL):
            term = dot_nt(O[pl.ds(r0, MAXLEN), k * D : (k + 1) * D], w(9 + k, 10 + k))
            total = term if total is None else total + term
        back = O[pl.ds(r0, MAXLEN), D : 2 * D].astype(f32) + DGD[pl.ds(r0, MAXLEN), :] * total
        back = back.astype(bf16)
        DB[pl.ds(r0, MAXLEN), :] = back
        LB[pl.ds(r0, MAXLEN), :] = (dot_nt(back, w(8, 9)) + LAT[pl.ds(r0, MAXLEN), :]).astype(bf16)

    each(decode_back)
    reduce_z(0)

    def proj_grads(left, right, group):
        for half in range(2):
            put(half, group, dot_nn(left[...], right[:, HALF * half : HALF * (half + 1)]))

    proj_grads(STRT, DB, 8)
    reduce_peer(1)

    def decoded_result(b, r0):
        m = lanes(MASK[pl.ds(r0, MAXLEN), :], 4)
        value = (DEC[pl.ds(r0, MAXLEN), :] + dot_nn(S[pl.ds(r0, MAXLEN), :], w(9, 12))) * m
        OB[pl.ds(r0, MAXLEN), :] = value.astype(bf16)

    each(decoded_result)
    out_own = pltpu.make_async_copy(OB.at[:, cols], out_hbm.at[mine, :], lsem.at[3])
    out_own.start()
    at_out = place()
    send(OB.at[:, cols_other], out_hbm.at[mine, :], dev_peer, at_out)

    def encode_back(b, r0):
        m = lanes(MASK[pl.ds(r0, MAXLEN), :], 4)
        back = dot_nt(LB[pl.ds(r0, MAXLEN), :], w(3, 4)) * m
        DEC[pl.ds(r0, MAXLEN), :] = back
        low = back.astype(bf16)
        before, after = neighbours(low.astype(f32))
        O[pl.ds(r0, MAXLEN), 0:D] = after
        O[pl.ds(r0, MAXLEN), D : 2 * D] = low
        O[pl.ds(r0, MAXLEN), 2 * D : 3 * D] = before

    each(encode_back)
    reduce_a(1)
    proj_grads(ENCT, LB, 3)
    kernel_grad(AT, 0)
    reduce_peer(2)
    reduce_end(0)
    reduce_b(1)

    def input_back(b, r0):
        m = lanes(MASK[pl.ds(r0, MAXLEN), :], 4)
        total = None
        for k in range(KERNEL):
            term = dot_nt(O[pl.ds(r0, MAXLEN), k * D : (k + 1) * D], w(k, k + 1))
            total = term if total is None else total + term
        slope = gelu_pair(FR[pl.ds(r0, MAXLEN), :].astype(f32))[1]
        STR[pl.ds(r0, MAXLEN), :] = (DEC[pl.ds(r0, MAXLEN), :] + slope * m * total).astype(bf16)

    reduce_a(2)
    reduce_z(1)
    each(input_back)
    in_own = pltpu.make_async_copy(STR.at[:, cols], input_hbm.at[mine, :], lsem.at[4])
    in_own.start()
    at_in = place()
    send(STR.at[:, cols_other], input_hbm.at[mine, :], dev_peer, at_in)
    reduce_b(2)
    reduce_end(1)
    reduce_z(2)
    reduce_end(2)

    at_rows, at_st, at_nmp, at_nm = place(), place(), place(), place()
    beta = 1.0 - STEP ** (-0.8)
    grads = GF[...].reshape(GROUPS12 * BLOCK, HALF)
    squares = grads * grads + square_floor
    RSUM[...] = jnp.broadcast_to(jnp.sum(squares, axis=1, keepdims=True), (GROUPS12 * BLOCK, 128))
    send(RSUM, RSUMP, dev_peer, at_rows)
    for i, (g0, g1) in enumerate(MATRICES):
        STS[i : i + 1, :] = jnp.sum(squares[g0 * BLOCK : g1 * BLOCK], axis=0, keepdims=True)
    old = jnp.broadcast_to(old_rows[...], (128, GROUPS12 * BLOCK)).T
    arrived(RSUMP, at_rows)
    rowstat = beta * old + (1.0 - beta) * (RSUM[...] + RSUMP[...])
    for i, (g0, g1) in enumerate(MATRICES):
        STS[8 + i : 9 + i, 0:128] = jnp.sum(rowstat[g0 * BLOCK : g1 * BLOCK], axis=0, keepdims=True)
    STS[6:8, :] = jnp.zeros((2, HALF), f32)
    STS[14:16, :] = jnp.zeros((2, HALF), f32)
    STS[8:14, 128:256] = jnp.zeros((6, 128), f32)
    ST[peers - 1] = STS[...]
    for k in range(1, peers):
        send(STS, ST.at[k - 1], (lax.rem(me + k, peers), c), at_st)
        unsent.pop()
    rows_out[...] = rowstat.T[0:8]
    for k in range(3):
        conv_grad[0, k] = GF[k]
        conv_grad[1, k] = GF[9 + k]
    proj_grad[0] = GF[3]
    proj_grad[1] = GF[8]
    for level in range(2):
        for t in range(2):
            book_grad[level, BLOCK * t : BLOCK * (t + 1)] = GF[4 + 2 * level + t]
    arrived(ST.at[0 : peers - 1], at_st)
    totals = jnp.sum(ST[...], axis=0)
    old_cols = (conv_cols[0:1], proj_cols[0:1], book_cols[0:1], book_cols[1:2], proj_cols[1:2], conv_cols[1:2])
    updates = []
    for i, (g0, g1) in enumerate(MATRICES):
        part = slice(g0 * BLOCK, g1 * BLOCK)
        colstat = beta * old_cols[i] + (1.0 - beta) * totals[i : i + 1]
        if i in (0, 5):
            conv_cols_out[i // 5 : i // 5 + 1, :] = colstat
        elif i in (1, 4):
            proj_cols_out[i // 4 : i // 4 + 1, :] = colstat
        else:
            book_cols_out[i - 2 : i - 1, :] = colstat
        total = lanes(totals[8 + i : 9 + i, 0:128], 2)
        update = grads[part] * lax.rsqrt(lanes(rowstat[part], 2) * colstat / total)
        updates.append(update)
        norm = jnp.sum(jnp.sum(update * update, axis=0, keepdims=True), axis=1, keepdims=True)
        NMS[i : i + 1, :] = jnp.broadcast_to(norm, (1, 128))
    NMS[6:8, :] = jnp.zeros((2, 128), f32)
    send(NMS, NMP, dev_peer, at_nmp)
    arrived(NMP, at_nmp)
    NM[peers - 1] = NMS[...] + NMP[...]
    for k in range(1, peers):
        send(NM.at[peers - 1], NM.at[k - 1], (lax.rem(me + k, peers), c), at_nm)
        unsent.pop()
    arrived(NM.at[0 : peers - 1], at_nm)
    norms = jnp.sum(NM[...], axis=0)
    for i, (g0, g1) in enumerate(MATRICES):
        size = (g1 - g0) * BLOCK * peers * D
        factor = jnp.maximum(1.0, jnp.sqrt(norms[i : i + 1] / size) / clip_level)
        rate = (2.0 / math.sqrt(KERNEL * D), 2.0 / math.sqrt(D), 2.0)[(0, 1, 2, 2, 1, 0)[i]]
        step = rate * (updates[i] / lanes(factor, 2))
        if i in (0, 5):
            for k in range(3):
                conv_new[i // 5, k] = conv_weight[i // 5, k] - step[k * BLOCK : (k + 1) * BLOCK]
        elif i in (1, 4):
            proj_new[i // 4] = proj_weight[i // 4] - step
        else:
            book_new[i - 2] = codebooks[i - 2] - step

    arrived(out_hbm.at[theirs, :], at_out)
    arrived(input_hbm.at[theirs, :], at_in)
    out_own.wait()
    in_own.wait()
    for slots, at in ((CN, at_count), (ST, at_st), (NM, at_nm)):
        part = slots.at[0 : peers - 1]
        unsent.append(
            pltpu.make_async_remote_copy(
                src_ref=part,
                dst_ref=part,
                send_sem=ssem.at[at],
                recv_sem=rsem.at[at],
                device_id=dev_peer,
                device_id_type=MESH,
            )
        )
    for copy in unsent:
        copy.wait_send()


def fused_body(
    frames,
    cotangent,
    lengths,
    frame_mask,
    code_index,
    conv_weight,
    proj_weight,
    codebooks,
    conv_rows,
    conv_cols,
    proj_rows,
    proj_cols,
    book_rows,
    book_cols,
):
    old_rows = jnp.concatenate(
        [
            conv_rows[0].reshape(-1),
            proj_rows[0],
            book_rows[0],
            book_rows[1],
            proj_rows[1],
            conv_rows[1].reshape(-1),
        ]
    ).reshape(1, -1)
    vmem = pl.BlockSpec(memory_space=pltpu.VMEM)
    hbm = pl.BlockSpec(memory_space=pl.ANY)
    shape = jax.ShapeDtypeStruct
    quad = (NZ, NY, NX, BLOCK)
    out = pl.pallas_call(
        fused_kernel,
        out_shape=(
            shape(cotangent.shape, bf16),
            shape(cotangent.shape, bf16),
            shape(conv_weight.shape, f32),
            shape(proj_weight.shape, f32),
            shape(codebooks.shape, f32),
            shape((8, GROUPS12 * BLOCK), f32),
            shape(conv_cols.shape, f32),
            shape(proj_cols.shape, f32),
            shape(book_cols.shape, f32),
            shape(conv_weight.shape, f32),
            shape(proj_weight.shape, f32),
            shape(codebooks.shape, f32),
        ),
        in_specs=[pl.BlockSpec(memory_space=pltpu.SMEM), hbm, hbm] + [vmem] * 9,
        out_specs=(hbm, hbm) + (vmem,) * 10,
        scratch_shapes=[
            pltpu.VMEM((GROUPS12,) + quad + (D,), bf16),
            pltpu.VMEM((2, GROUPS12) + quad + (HALF,), bf16),
            pltpu.VMEM((GROUPS12,) + quad + (HALF,), bf16),
            pltpu.VMEM((GROUPS12, NZ, NY, BLOCK, 128), bf16),
            pltpu.VMEM((GROUPS12, NZ, NX, BLOCK, 128), bf16),
            pltpu.VMEM((GROUPS12, NZ, BLOCK, 128), bf16),
            pltpu.VMEM((GROUPS12, NZ, BLOCK, 128), bf16),
            pltpu.VMEM((GROUPS12, NZ, BLOCK, 128), bf16),
            pltpu.VMEM((GROUPS12, NZ, BLOCK, 128), bf16),
            pltpu.VMEM((GROUPS12, NZ, BLOCK, HALF), bf16),
            pltpu.VMEM((NZ - 1, GROUPS12, BLOCK, HALF), bf16),
            pltpu.VMEM((GROUPS12, BLOCK, HALF), f32),
            pltpu.VMEM((ROWS, D), bf16),
            pltpu.VMEM((ROWS, 3 * D), bf16),
            pltpu.VMEM((ROWS, 3 * D), bf16),
            pltpu.VMEM((D, ROWS), bf16),
            pltpu.VMEM((D, ROWS), bf16),
            pltpu.VMEM((D, ROWS), bf16),
            pltpu.VMEM((D, ROWS), bf16),
            pltpu.VMEM((ROWS, D), f32),
            pltpu.VMEM((ROWS, D), f32),
            pltpu.VMEM((ROWS, D), f32),
            pltpu.VMEM((ROWS, D), bf16),
            pltpu.VMEM((ROWS, D), bf16),
            pltpu.VMEM((ROWS, D), bf16),
            pltpu.VMEM((ROWS, D), bf16),
            pltpu.VMEM((ROWS, D), bf16),
            pltpu.VMEM((ROWS, D), bf16),
            pltpu.VMEM((ROWS, 128), f32),
            pltpu.VMEM((2, 2, CLIPS, 1, MAXLEN), jnp.int32),
            pltpu.VMEM((NZ * NY * NX, 8, 128), f32),
            pltpu.VMEM((NZ * NY * NX, 16, HALF), f32),
            pltpu.VMEM((16, HALF), f32),
            pltpu.VMEM((NZ * NY * NX, 8, 128), f32),
            pltpu.VMEM((8, 128), f32),
            pltpu.VMEM((8, 128), f32),
            pltpu.VMEM((GROUPS12 * BLOCK, 128), f32),
            pltpu.VMEM((GROUPS12 * BLOCK, 128), f32),
            pltpu.SemaphoreType.DMA((72,)),
            pltpu.SemaphoreType.DMA((72,)),
            pltpu.SemaphoreType.DMA((8,)),
        ],
        compiler_params=pltpu.CompilerParams(
            collective_id=0, has_side_effects=True, vmem_limit_bytes=63 * 2**20
        ),
        name="step",
    )(
        lengths,
        frames,
        cotangent,
        frame_mask.reshape(2, CLIPS, 1, MAXLEN),
        code_index.reshape(2, 2, CLIPS, 1, MAXLEN),
        conv_weight,
        proj_weight,
        codebooks,
        old_rows,
        conv_cols,
        proj_cols,
        book_cols,
    )
    rows = out[5][0]
    rowstat_conv = jnp.stack([rows[0:96], rows[288:384]]).reshape(conv_rows.shape)
    rowstat_proj = jnp.stack([rows[96:128], rows[256:288]])
    rowstat_book = rows[128:256].reshape(book_rows.shape)
    return (
        out[0],
        out[1],
        out[2],
        out[3],
        out[4],
        rowstat_conv,
        out[6],
        rowstat_proj,
        out[7],
        rowstat_book,
        out[8],
        out[9],
        out[10],
        out[11],
    )


def solution(mesh):
    placed = (
        P("dp", None),
        P("dp", "chan"),
        P("dp"),
        P("dp"),
        P(None, "dp", "chan"),
        P(None, None, "dp", "chan"),
        P(None, "dp", "chan"),
        P(None, "dp", "chan"),
        P(None, None, "dp"),
        P(None, "chan"),
        P(None, "dp"),
        P(None, "chan"),
        P(None, "dp"),
        P(None, "chan"),
    )
    fits = mesh.shape["dp"] == NZ * NY * NX and mesh.shape["chan"] == 2
    return jax.shard_map(
        fused_body if fits else general_body,
        mesh=mesh,
        in_specs=placed,
        out_specs=(
            P("dp", "chan"),
            P("dp", "chan"),
            P(None, None, "dp", "chan"),
            P(None, "dp", "chan"),
            P(None, "dp", "chan"),
            P(None, None, "dp"),
            P(None, "chan"),
            P(None, "dp"),
            P(None, "chan"),
            P(None, "dp"),
            P(None, "chan"),
            P(None, None, "dp", "chan"),
            P(None, "dp", "chan"),
            P(None, "dp", "chan"),
        ),
        check_vma=False,
    )
```

```python
import functools
import math

import jax
import jax.numpy as jnp
from jax import lax
from jax.experimental import pallas as pl
from jax.experimental.pallas import tpu as pltpu
from jax.sharding import PartitionSpec as P

D = 512
CODES = 1024
KERNEL = 3
STEP = 10
MAXLEN = 512
MICRO = 2


square_floor = 1e-30
clip_level = 0.5
f32 = jnp.float32
bf16 = jnp.bfloat16


def shifted(signal, length):
    channels = signal.shape[-1]
    blocks = signal.reshape(-1, length, channels)
    padded = jnp.pad(blocks, ((0, 0), (1, 1), (0, 0)))
    joined = jnp.concatenate(
        [padded[:, 0:length], padded[:, 1 : length + 1], padded[:, 2 : length + 2]], axis=2
    )
    return joined.reshape(-1, 3 * channels)


def unshift(partial_terms, length):
    channels = partial_terms.shape[-1] // 3
    blocks = partial_terms.reshape(-1, length, 3, channels)
    padded = jnp.pad(blocks, ((0, 0), (1, 1), (0, 0), (0, 0)))
    summed = padded[:, 2 : length + 2, 0] + padded[:, 1 : length + 1, 1] + padded[:, 0:length, 2]
    return summed.reshape(-1, channels)


def gelu_back(values, upstream):
    return jax.vjp(jax.nn.gelu, values)[1](upstream)[0]


def fetch(conv_weight, proj_weight, codebooks):
    return (
        lax.all_gather(conv_weight.astype(bf16), "dp", axis=2, tiled=True),
        lax.all_gather(proj_weight.astype(bf16), "dp", axis=1, tiled=True),
        lax.all_gather(codebooks.astype(bf16), "dp", axis=1, tiled=True),
    )


def reduce_grads(conv_total, proj_total, book_total):
    return (
        lax.psum_scatter(conv_total, "dp", scatter_dimension=2, tiled=True),
        lax.psum_scatter(proj_total, "dp", scatter_dimension=1, tiled=True),
        lax.psum_scatter(book_total, "dp", scatter_dimension=1, tiled=True),
    )


def contract(left, right):
    return jnp.einsum("fc,fd->cd", left, right, preferred_element_type=f32)


def transpose_product(left, right):
    return jnp.einsum("fd,cd->fc", left, right, preferred_element_type=f32)


def general_body(
    frames,
    cotangent,
    lengths,
    frame_mask,
    code_index,
    conv_weight,
    proj_weight,
    codebooks,
    conv_rows,
    conv_cols,
    proj_rows,
    proj_cols,
    book_rows,
    book_cols,
):
    length = MAXLEN
    block_rows = frames.shape[0] // MICRO
    half_width = cotangent.shape[1]
    chan_place = lax.axis_index("chan")
    row_place = jnp.arange(frames.shape[0], dtype=jnp.int32) % length
    live = (row_place < jnp.repeat(lengths, length, total_repeat_length=frames.shape[0])) & (
        frame_mask > 0
    )
    weight_mask = live.astype(f32)[:, None]
    live_total = lax.psum(jnp.sum(weight_mask), "dp")
    vq_scale = 2.0 / live_total
    running = None
    out_pieces = []
    grad_pieces = []
    for block_number in range(MICRO):
        first_row = block_number * block_rows
        last_row = first_row + block_rows
        conv_bank, proj_bank, book_bank = fetch(conv_weight, proj_weight, codebooks)
        conv_enc = conv_bank[0].reshape(-1, half_width)
        conv_dec = conv_bank[1].reshape(-1, half_width)
        frame_part = frames[first_row:last_row]
        frame_wide = frame_part.astype(f32)
        own_part = lax.dynamic_slice_in_dim(frame_wide, chan_place * half_width, half_width, 1)
        masked = weight_mask[first_row:last_row]
        cot_part = jnp.where(masked > 0, cotangent[first_row:last_row], jnp.zeros((), bf16))
        code_range = jnp.arange(book_bank.shape[1], dtype=jnp.int32)
        onehot_one = (code_index[0, first_row:last_row, 0][:, None] == code_range[None, :]).astype(
            bf16
        )
        onehot_two = (code_index[1, first_row:last_row, 0][:, None] == code_range[None, :]).astype(
            bf16
        )
        activated = (jax.nn.gelu(frame_wide) * masked).astype(bf16)
        stack_one = shifted(activated, length)
        branch = jnp.dot(stack_one, conv_enc, preferred_element_type=f32)
        encoded = (own_part + branch) * masked
        enc_full = lax.all_gather(encoded.astype(bf16), "chan", axis=1, tiled=True)
        latent = jnp.dot(enc_full, proj_bank[0], preferred_element_type=f32)
        level_one = jnp.dot(onehot_one, book_bank[0], preferred_element_type=f32)
        level_two = jnp.dot(onehot_two, book_bank[1], preferred_element_type=f32)
        quantized = level_one + level_two
        straight = (latent + (quantized - latent)).astype(bf16)
        straight_full = lax.all_gather(straight, "chan", axis=1, tiled=True)
        decoded = jnp.dot(straight_full, proj_bank[1], preferred_element_type=f32)
        decoder_in = (jax.nn.gelu(decoded) * masked).astype(bf16)
        decoder_full = lax.all_gather(decoder_in, "chan", axis=1, tiled=True)
        stack_two = shifted(decoder_full, length)
        result = (decoded + jnp.dot(stack_two, conv_dec, preferred_element_type=f32)) * masked
        out_pieces.append(result.astype(bf16))
        conv_dec_grad = contract(stack_two, cot_part)
        in_partial = unshift(transpose_product(cot_part, conv_dec), length)
        in_back = lax.psum_scatter(in_partial, "chan", scatter_dimension=1, tiled=True)
        decoded_back = (cot_part.astype(f32) + gelu_back(decoded, masked * in_back)).astype(bf16)
        proj_dec_grad = contract(straight_full, decoded_back)
        straight_back = lax.psum_scatter(
            transpose_product(decoded_back, proj_bank[1]), "chan", scatter_dimension=1, tiled=True
        )
        resid_one = latent - level_one
        resid_two = resid_one - level_two
        pulled = vq_scale * masked * (resid_one + resid_two)
        latent_back = (straight_back + pulled).astype(bf16)
        one_back = (-pulled).astype(bf16)
        two_back = (-(vq_scale * masked * resid_two)).astype(bf16)
        book_one_grad = contract(onehot_one, one_back)
        book_two_grad = contract(onehot_two, two_back)
        proj_enc_grad = contract(enc_full, latent_back)
        encoded_back = lax.psum_scatter(
            transpose_product(latent_back, proj_bank[0]), "chan", scatter_dimension=1, tiled=True
        )
        branch_back = (encoded_back * masked).astype(bf16)
        conv_enc_grad = contract(stack_one, branch_back)
        activated_back = unshift(transpose_product(branch_back, conv_enc), length)
        input_partial = gelu_back(frame_wide, masked * activated_back)
        input_own = lax.psum_scatter(input_partial, "chan", scatter_dimension=1, tiled=True)
        grad_pieces.append((encoded_back * masked + input_own).astype(bf16))
        conv_blockgrad = jnp.stack(
            [
                conv_enc_grad.reshape(KERNEL, -1, half_width),
                conv_dec_grad.reshape(KERNEL, -1, half_width),
            ]
        )
        proj_blockgrad = jnp.stack([proj_enc_grad, proj_dec_grad])
        book_blockgrad = jnp.stack([book_one_grad, book_two_grad])
        reduced = reduce_grads(conv_blockgrad, proj_blockgrad, book_blockgrad)
        running = (
            reduced
            if running is None
            else (running[0] + reduced[0], running[1] + reduced[1], running[2] + reduced[2])
        )
    conv_grad, proj_grad, book_grad = running
    decoded_out = jnp.concatenate(out_pieces, axis=0)
    input_grad = jnp.concatenate(grad_pieces, axis=0)
    beta_two = 1.0 - STEP ** (-0.8)
    squares_conv = conv_grad * conv_grad + square_floor
    squares_proj = proj_grad * proj_grad + square_floor
    squares_book = book_grad * book_grad + square_floor
    row_sums = lax.psum(
        (
            jnp.sum(squares_conv, axis=3),
            jnp.sum(squares_proj, axis=2),
            jnp.sum(squares_book, axis=2),
        ),
        "chan",
    )
    rowstat_conv = beta_two * conv_rows + (1.0 - beta_two) * row_sums[0]
    rowstat_proj = beta_two * proj_rows + (1.0 - beta_two) * row_sums[1]
    rowstat_book = beta_two * book_rows + (1.0 - beta_two) * row_sums[2]
    col_sums = lax.psum(
        (
            jnp.sum(squares_conv, axis=(1, 2)),
            jnp.sum(squares_proj, axis=1),
            jnp.sum(squares_book, axis=1),
            jnp.sum(rowstat_conv, axis=(1, 2)),
            jnp.sum(rowstat_proj, axis=1),
            jnp.sum(rowstat_book, axis=1),
        ),
        "dp",
    )
    colstat_conv = beta_two * conv_cols + (1.0 - beta_two) * col_sums[0]
    colstat_proj = beta_two * proj_cols + (1.0 - beta_two) * col_sums[1]
    colstat_book = beta_two * book_cols + (1.0 - beta_two) * col_sums[2]
    update_conv = conv_grad * lax.rsqrt(
        rowstat_conv[..., None] * colstat_conv[:, None, None, :] / col_sums[3][:, None, None, None]
    )
    update_proj = proj_grad * lax.rsqrt(
        rowstat_proj[..., None] * colstat_proj[:, None, :] / col_sums[4][:, None, None]
    )
    update_book = book_grad * lax.rsqrt(
        rowstat_book[..., None] * colstat_book[:, None, :] / col_sums[5][:, None, None]
    )
    norm_sums = lax.psum(
        (
            jnp.sum(update_conv * update_conv, axis=(1, 2, 3)),
            jnp.sum(update_proj * update_proj, axis=(1, 2)),
            jnp.sum(update_book * update_book, axis=(1, 2)),
        ),
        ("dp", "chan"),
    )
    factor_conv = jnp.maximum(1.0, jnp.sqrt(norm_sums[0] / (KERNEL * D * D)) / clip_level)
    factor_proj = jnp.maximum(1.0, jnp.sqrt(norm_sums[1] / (D * D)) / clip_level)
    factor_book = jnp.maximum(1.0, jnp.sqrt(norm_sums[2] / (CODES * D)) / clip_level)
    rate_conv = 2.0 / math.sqrt(KERNEL * D)
    rate_proj = 2.0 / math.sqrt(D)
    updated_conv = conv_weight - rate_conv * (update_conv / factor_conv[:, None, None, None])
    updated_proj = proj_weight - rate_proj * (update_proj / factor_proj[:, None, None])
    updated_book = codebooks - 2.0 * (update_book / factor_book[:, None, None])
    return (
        decoded_out,
        input_grad,
        conv_grad,
        proj_grad,
        book_grad,
        rowstat_conv,
        colstat_conv,
        rowstat_proj,
        colstat_proj,
        rowstat_book,
        colstat_book,
        updated_conv,
        updated_proj,
        updated_book,
    )


MESH = pl.DeviceIdType.MESH
CLIPS = 3
ROWS = CLIPS * MAXLEN
GROUPS12 = 12
NZ, NY, NX = 4, 2, 2
BLOCK = 32
HALF = 256
GELU_A = math.sqrt(2.0 / math.pi)
GELU_B = 0.044715
MATRICES = ((0, 3), (3, 4), (4, 6), (6, 8), (8, 9), (9, 12))


def gelu_pair(x):
    x2 = x * x
    t = jnp.tanh(GELU_A * x * (1.0 + GELU_B * x2))
    half = 0.5 * (1.0 + t)
    return x * half, half + 0.5 * x * (1.0 - t * t) * (GELU_A + 3.0 * GELU_A * GELU_B * x2)


def lanes(m, n):
    return jnp.concatenate([m] * n, axis=1)


def dot_nn(a, b):
    return jnp.dot(a, b, preferred_element_type=f32)


def dot_nt(a, b):
    return lax.dot_general(a, b, (((1,), (1,)), ((), ())), preferred_element_type=f32)


def neighbours(v):
    rows = lax.broadcasted_iota(jnp.int32, v.shape, 0)
    before = jnp.where(rows == 0, 0.0, pltpu.roll(v, 1, 0))
    after = jnp.where(rows == v.shape[0] - 1, 0.0, pltpu.roll(v, v.shape[0] - 1, 0))
    return before.astype(bf16), after.astype(bf16)


def fused_kernel(
    lengths,
    frames_hbm,
    cot_hbm,
    frame_mask,
    code_index,
    conv_weight,
    proj_weight,
    codebooks,
    conv_rows,
    proj_rows,
    book_rows,
    conv_cols,
    proj_cols,
    book_cols,
    out_hbm,
    input_hbm,
    GF,
    ROWSTAT,
    COLSTAT,
    SCALARS,
    W,
    G,
    RP,
    AX,
    AY,
    BX,
    BY,
    BXS,
    BYS,
    TS,
    ZR,
    FR,
    S,
    O,
    AT,
    ENCT,
    STRT,
    DINT,
    LAT,
    DEC,
    DGD,
    B1,
    B2,
    STR,
    DB,
    LB,
    OB,
    MASK,
    IDX,
    CN,
    ST,
    NM,
    RSUM,
    ssem,
    rsem,
    lsem,
):
    me = lax.axis_index("dp")
    c = lax.axis_index("chan")
    z, y, x = me // (NY * NX), (me // NX) % NY, me % NX
    far_y, far_x, other = 1 - y, 1 - x, 1 - c

    def dp_of(zz, yy, xx):
        return (zz * (NY * NX) + yy * NX + xx, c)

    dev_x, dev_y, dev_diagonal = dp_of(z, y, far_x), dp_of(z, far_y, x), dp_of(z, far_y, far_x)
    dev_z = [dp_of(lax.rem(z + k, NZ), y, x) for k in range(1, NZ)]
    dev_peer = (me, other)
    to_z = [lax.rem(z + k, NZ) for k in range(1, NZ)]
    from_z = [lax.rem(z + NZ - k, NZ) for k in range(1, NZ)]
    cols = pl.ds(pl.multiple_of(c * HALF, HALF), HALF)
    cols_other = pl.ds(pl.multiple_of(other * HALF, HALF), HALF)
    quarter = (
        pl.ds(pl.multiple_of(c * HALF, HALF), 128),
        pl.ds(pl.multiple_of(c * HALF + 128, 128), 128),
    )
    mine = pl.ds(pl.multiple_of(c * ROWS, ROWS), ROWS)
    theirs = pl.ds(pl.multiple_of(other * ROWS, ROWS), ROWS)

    counter = [0]
    unsent = []

    def place(n=1):
        counter[0] += n
        return counter[0] - n

    def remote(src, dst, dev, at):
        return pltpu.make_async_remote_copy(
            src_ref=src,
            dst_ref=dst,
            send_sem=ssem.at[at],
            recv_sem=rsem.at[at],
            device_id=dev,
            device_id_type=MESH,
        )

    def send(src, dst, dev, at):
        remote(src(), dst(), dev, at).start()
        unsent.append((src, at))

    def arrived(dst, at):
        remote(dst, dst, dev_peer, at).wait_recv()

    frames_in = pltpu.make_async_copy(frames_hbm.at[mine, :], FR, lsem.at[0])
    frames_in.start()
    cot_in = pltpu.make_async_copy(cot_hbm.at[mine, :], OB.at[:, cols], lsem.at[1])
    cot_in.start()
    index_in = pltpu.make_async_copy(code_index.at[:, c], IDX.at[:, c], lsem.at[2])
    index_in.start()
    barrier = pltpu.get_barrier_semaphore()
    partners = [dev_x, dev_y, dev_diagonal, dev_peer] + dev_z
    for dev in partners:
        pl.semaphore_signal(barrier, inc=1, device_id=dev, device_id_type=MESH)

    for k in range(3):
        W[k, z, y, x, :, cols] = conv_weight[0, k].astype(bf16)
        W[9 + k, z, y, x, :, cols] = conv_weight[1, k].astype(bf16)
    W[3, z, y, x, :, cols] = proj_weight[0].astype(bf16)
    W[8, z, y, x, :, cols] = proj_weight[1].astype(bf16)
    for level in range(2):
        for t in range(2):
            W[4 + 2 * level + t, z, y, x, :, cols] = codebooks[level, BLOCK * t : BLOCK * (t + 1)].astype(bf16)
    lane_row = lax.broadcasted_iota(jnp.int32, (1, MAXLEN), 1)
    count = jnp.zeros((1, MAXLEN), f32)
    for core in range(2):
        for b in range(CLIPS):
            live = (lane_row < lengths[core * CLIPS + b]) & (frame_mask[core, b] > 0)
            count = count + jnp.where(live, 1.0, 0.0)
    CN[0] = jnp.broadcast_to(jnp.sum(count, axis=1, keepdims=True), (8, 128))
    pl.semaphore_wait(barrier, len(partners))

    pieces = ((0, 1), (1, 2), (2, 4), (4, 6), (6, 8), (8, 10), (10, 12))
    at_z = [place(3) for p in pieces]
    at_l = [place(2) for p in pieces]
    at_d = [place(2) for p in pieces]
    at_p = [place(2) for p in pieces]
    at_cot, at_idx, at_count = place(), place(), place(6)

    def gather_z(p):
        g0, g1 = pieces[p]
        for k in range(NZ - 1):
            own = lambda: W.at[g0:g1, z, y, x, :, cols]
            send(own, own, dev_z[k], at_z[p] + k)

    def gather_line(p):
        g0, g1 = pieces[p]
        for k in range(NZ - 1):
            arrived(W.at[g0:g1, from_z[k], y, x, :, cols], at_z[p] + k)
        line = lambda: W.at[g0:g1, :, y, x, :, cols]
        send(line, line, dev_x, at_l[p])
        send(line, line, dev_y, at_l[p] + 1)

    def gather_diagonal(p):
        g0, g1 = pieces[p]
        arrived(W.at[g0:g1, :, y, far_x, :, cols], at_l[p])
        arrived(W.at[g0:g1, :, far_y, x, :, cols], at_l[p] + 1)
        part_y = lambda: W.at[g0:g1, :, far_y, x, :, quarter[0]]
        send(part_y, part_y, dev_x, at_d[p])
        part_x = lambda: W.at[g0:g1, :, y, far_x, :, quarter[1]]
        send(part_x, part_x, dev_y, at_d[p] + 1)
        near = lambda: W.at[g0:g1, :, y, :, :, cols]
        send(near, near, dev_peer, at_p[p])

    def gather_peer(p):
        g0, g1 = pieces[p]
        arrived(W.at[g0:g1, :, far_y, far_x, :, quarter[0]], at_d[p])
        arrived(W.at[g0:g1, :, far_y, far_x, :, quarter[1]], at_d[p] + 1)
        far = lambda: W.at[g0:g1, :, far_y, :, :, cols]
        send(far, far, dev_peer, at_p[p] + 1)

    def gathered(p):
        g0, g1 = pieces[p]
        arrived(W.at[g0:g1, :, y, :, :, cols_other], at_p[p])
        arrived(W.at[g0:g1, :, far_y, :, :, cols_other], at_p[p] + 1)

    parts = ((4, 6), (6, 8), (9, 10), (10, 11), (11, 12), (8, 9), (3, 4), (0, 1), (1, 2), (2, 3))
    at_rp = [place() for p in parts]
    at_ra = [place(2) for p in parts]
    at_rb = [place(2) for p in parts]
    at_rz = [place(3) for p in parts]

    def reduce_peer(p):
        g0, g1 = parts[p]
        send(lambda: G.at[other, g0:g1], lambda: RP.at[g0:g1], dev_peer, at_rp[p])

    def reduce_a(p):
        g0, g1 = parts[p]
        arrived(RP.at[g0:g1], at_rp[p])

        @pl.loop(g0, g1)
        def _(g):
            G[c, g] = (G[c, g].astype(f32) + RP[g].astype(f32)).astype(bf16)

        send(lambda: G.at[c, g0:g1, :, :, far_x, :, 0:128], lambda: AX.at[g0:g1], dev_x, at_ra[p])
        send(lambda: G.at[c, g0:g1, :, far_y, :, :, 128:256], lambda: AY.at[g0:g1], dev_y, at_ra[p] + 1)

    def reduce_b(p):
        g0, g1 = parts[p]
        arrived(AX.at[g0:g1], at_ra[p])
        arrived(AY.at[g0:g1], at_ra[p] + 1)

        @pl.loop(g0, g1)
        def _(g):
            BXS[g] = (G[c, g, :, y, far_x, :, 128:256].astype(f32) + AY[g, :, far_x].astype(f32)).astype(bf16)
            BYS[g] = (G[c, g, :, far_y, x, :, 0:128].astype(f32) + AX[g, :, far_y].astype(f32)).astype(bf16)

        send(lambda: BXS.at[g0:g1], lambda: BX.at[g0:g1], dev_x, at_rb[p])
        send(lambda: BYS.at[g0:g1], lambda: BY.at[g0:g1], dev_y, at_rb[p] + 1)

    def reduce_z(p):
        g0, g1 = parts[p]
        arrived(BX.at[g0:g1], at_rb[p])
        arrived(BY.at[g0:g1], at_rb[p] + 1)

        @pl.loop(g0, g1)
        def _(g):
            base = G[c, g, :, y, x].astype(f32)
            left = base[:, :, 0:128] + (AX[g, :, y].astype(f32) + BY[g].astype(f32))
            right = base[:, :, 128:256] + (AY[g, :, x].astype(f32) + BX[g].astype(f32))
            TS[g, :, :, 0:128] = left.astype(bf16)
            TS[g, :, :, 128:256] = right.astype(bf16)

        for k in range(NZ - 1):
            send(
                lambda k=k: TS.at[g0:g1, to_z[k]],
                lambda k=k: ZR.at[k, g0:g1],
                dev_z[k],
                at_rz[p] + k,
            )

    def reduce_end(p):
        g0, g1 = parts[p]
        for k in range(NZ - 1):
            arrived(ZR.at[k, g0:g1], at_rz[p] + k)

        @pl.loop(g0, g1)
        def _(g):
            GF[g] = (TS[g, z].astype(f32) + ZR[0, g].astype(f32)) + (ZR[1, g].astype(f32) + ZR[2, g].astype(f32))

    def after(b, hooks):
        for k, steps in (hooks or {}).items():

            @pl.when(b == k)
            def _():
                for step, p in steps:
                    step(p)

    def w(a, b):
        return W[a:b].reshape((b - a) * D, D)

    def each(step, hooks=None):

        @pl.loop(0, CLIPS)
        def _(b):
            step(b, pl.multiple_of(b * MAXLEN, MAXLEN))
            after(b, hooks)

    def put(half, group, value):
        G[half, group] = value.astype(bf16).reshape(NZ, NY, NX, BLOCK, HALF)

    for p in range(4):
        gather_z(p)
    for k, dev in enumerate((dev_x, dev_y, dev_diagonal)):
        send(lambda: CN.at[0], lambda k=k: CN.at[1 + k], dev, at_count + k)
    send(lambda: code_index.at[:, other], lambda: IDX.at[:, c], dev_peer, at_idx)
    send(lambda: cot_hbm.at[theirs, :], lambda: OB.at[:, cols], dev_peer, at_cot)

    @pl.loop(0, CLIPS)
    def _(b):
        live = (lane_row < lengths[c * CLIPS + b]) & (frame_mask[c, b] > 0)
        row = jnp.where(live, 1.0, 0.0)
        MASK[pl.ds(pl.multiple_of(b * MAXLEN, MAXLEN), MAXLEN), :] = jnp.broadcast_to(row, (128, MAXLEN)).T

    frames_in.wait()

    def activate(b, r0):
        m = lanes(MASK[pl.ds(r0, MAXLEN), :], 4)
        a = gelu_pair(FR[pl.ds(r0, MAXLEN), :].astype(f32))[0] * m
        before, after = neighbours(a)
        a = a.astype(bf16)
        S[pl.ds(r0, MAXLEN), 0:D] = before
        S[pl.ds(r0, MAXLEN), D : 2 * D] = a
        S[pl.ds(r0, MAXLEN), 2 * D : 3 * D] = after
        AT[:, pl.ds(r0, MAXLEN)] = a.T

    each(
        activate,
        {
            0: [(gather_line, 0)],
            1: [(gather_line, 1), (gather_diagonal, 0)],
            2: [(gather_z, 4), (gather_line, 2), (gather_diagonal, 1), (gather_peer, 0)],
        },
    )
    for k in range(3):
        arrived(CN.at[1 + k], at_count + k)
    CN[4] = (CN[0] + CN[1]) + (CN[2] + CN[3])
    for k in range(NZ - 1):
        send(lambda: CN.at[4], lambda k=k: CN.at[5 + k], dev_z[k], at_count + 3 + k)
    cot_in.wait()
    index_in.wait()
    arrived(OB.at[:, cols_other], at_cot)
    arrived(IDX.at[:, other], at_idx)

    def upstream(b, r0):
        m = lanes(MASK[pl.ds(r0, MAXLEN), :], 4)
        ob = OB[pl.ds(r0, MAXLEN), :].astype(f32) * m
        before, after = neighbours(ob)
        O[pl.ds(r0, MAXLEN), 0:D] = after
        O[pl.ds(r0, MAXLEN), D : 2 * D] = ob.astype(bf16)
        O[pl.ds(r0, MAXLEN), 2 * D : 3 * D] = before

    each(
        upstream,
        {
            0: [(gather_z, 5), (gather_line, 3), (gather_diagonal, 2), (gather_peer, 1)],
            1: [(gather_z, 6), (gather_line, 4), (gather_diagonal, 3), (gather_peer, 2)],
        },
    )
    for k in range(NZ - 1):
        arrived(CN.at[5 + k], at_count + 3 + k)
    scale = 2.0 / ((CN[4, 0:1] + CN[5, 0:1]) + (CN[6, 0:1] + CN[7, 0:1]))
    gathered(0)
    gathered(1)
    gathered(2)

    def encode(b, r0):
        m = lanes(MASK[pl.ds(r0, MAXLEN), :], 4)
        branch = dot_nn(S[pl.ds(r0, MAXLEN), :], w(0, 3))
        enc = ((FR[pl.ds(r0, MAXLEN), :].astype(f32) + branch) * m).astype(bf16)
        STR[pl.ds(r0, MAXLEN), :] = enc
        ENCT[:, pl.ds(r0, MAXLEN)] = enc.T

    each(
        encode,
        {
            0: [(gather_line, 5), (gather_peer, 3)],
            1: [(gather_diagonal, 4)],
            2: [(gather_line, 6)],
        },
    )

    def project(b, r0):
        LAT[pl.ds(r0, MAXLEN), :] = dot_nn(STR[pl.ds(r0, MAXLEN), :], w(3, 4))

    each(
        project,
        {
            0: [(gather_peer, 4)],
            2: [(gather_diagonal, 5)],
        },
    )
    gathered(3)
    gathered(4)

    def slot(row):
        return ((row >> 5) & 1) * 512 + (row >> 6) * BLOCK + (row & 31)

    def quantize(b, r0):
        m = lanes(MASK[pl.ds(r0, MAXLEN), :], 2)
        sc = lanes(scale, 2) * m
        lane = lax.broadcasted_iota(jnp.int32, (MAXLEN, 128), 1)
        for g in range(2):
            gc = slice(HALF * g, HALF * (g + 1))
            level = []
            for l in range(2):
                col = jnp.broadcast_to(slot(IDX[l, g, b]), (128, MAXLEN)).T
                onehot = jnp.concatenate(
                    [jnp.where(col == lane + 128 * k, 1.0, 0.0).astype(bf16) for k in range(CODES // 128)], axis=1
                )
                book = W[4 + 2 * l : 6 + 2 * l, :, :, :, :, gc].reshape(CODES, HALF)
                level.append(dot_nn(onehot, book))
            latent = LAT[pl.ds(r0, MAXLEN), gc]
            quantized = level[0] + level[1]
            straight = (latent + (quantized - latent)).astype(bf16)
            resid_one = latent - level[0]
            resid_two = resid_one - level[1]
            pulled = sc * (resid_one + resid_two)
            STR[pl.ds(r0, MAXLEN), gc] = straight
            STRT[gc, pl.ds(r0, MAXLEN)] = straight.T
            LAT[pl.ds(r0, MAXLEN), gc] = pulled
            B1[pl.ds(r0, MAXLEN), gc] = (-pulled).astype(bf16)
            B2[pl.ds(r0, MAXLEN), gc] = (-(sc * resid_two)).astype(bf16)

    each(
        quantize,
        {
            0: [(gather_peer, 5), (gather_diagonal, 6)],
            2: [(gather_peer, 6)],
        },
    )

    def book_grads(l, back, hooks):
        def step(g):
            code = lax.broadcasted_iota(jnp.int32, (CODES, MAXLEN), 0)
            onehot = jnp.concatenate(
                [
                    jnp.where(jnp.broadcast_to(slot(IDX[l, g, b]), (CODES, MAXLEN)) == code, 1.0, 0.0).astype(bf16)
                    for b in range(CLIPS)
                ],
                axis=1,
            )
            value = dot_nn(onehot, back[:, pl.ds(pl.multiple_of(g * HALF, HALF), HALF)]).astype(bf16)
            G[g, 4 + 2 * l : 6 + 2 * l] = value.reshape(2, NZ, NY, NX, BLOCK, HALF)


        @pl.loop(0, 2)
        def _(g):
            step(g)
            after(g, hooks)

    book_grads(0, B1, {1: [(reduce_peer, 0)]})
    book_grads(1, B2, {0: [(reduce_a, 0)], 1: [(reduce_peer, 1)]})
    gathered(5)
    gathered(6)

    def decode(b, r0):
        m = lanes(MASK[pl.ds(r0, MAXLEN), :], 4)
        dec = dot_nn(STR[pl.ds(r0, MAXLEN), :], w(8, 9))
        DEC[pl.ds(r0, MAXLEN), :] = dec
        value, slope = gelu_pair(dec)
        value = value * m
        DGD[pl.ds(r0, MAXLEN), :] = slope * m
        before, after = neighbours(value)
        value = value.astype(bf16)
        S[pl.ds(r0, MAXLEN), 0:D] = before
        S[pl.ds(r0, MAXLEN), D : 2 * D] = value
        S[pl.ds(r0, MAXLEN), 2 * D : 3 * D] = after
        DINT[:, pl.ds(r0, MAXLEN)] = value.T

    each(decode, {0: [(reduce_a, 1)], 1: [(reduce_b, 0)]})

    def kernel_grad(left, base, hooks):
        def step(k):
            for half in range(2):
                right = O[:, pl.ds(pl.multiple_of(k * D + half * HALF, HALF), HALF)]
                put(half, base + k, dot_nn(left[...], right))


        @pl.loop(0, KERNEL)
        def _(k):
            step(k)
            after(k, hooks)

    kernel_grad(
        DINT,
        9,
        {
            0: [(reduce_peer, 2), (reduce_z, 0), (reduce_b, 1)],
            1: [(reduce_peer, 3), (reduce_a, 2)],
            2: [(reduce_peer, 4), (reduce_a, 3)],
        },
    )

    def decode_back(b, r0):
        total = None
        for k in range(KERNEL):
            term = dot_nt(O[pl.ds(r0, MAXLEN), k * D : (k + 1) * D], w(9 + k, 10 + k))
            total = term if total is None else total + term
        back = O[pl.ds(r0, MAXLEN), D : 2 * D].astype(f32) + DGD[pl.ds(r0, MAXLEN), :] * total
        back = back.astype(bf16)
        DB[pl.ds(r0, MAXLEN), :] = back
        LB[pl.ds(r0, MAXLEN), :] = (dot_nt(back, w(8, 9)) + LAT[pl.ds(r0, MAXLEN), :]).astype(bf16)

    each(
        decode_back,
        {
            0: [(reduce_z, 1), (reduce_a, 4), (reduce_end, 0)],
            1: [(reduce_b, 2), (reduce_b, 3)],
            2: [(reduce_z, 2), (reduce_b, 4), (reduce_end, 1)],
        },
    )

    def proj_grads(left, right, group):
        for half in range(2):
            put(half, group, dot_nn(left[...], right[:, HALF * half : HALF * (half + 1)]))

    proj_grads(STRT, DB, 8)
    reduce_peer(5)
    reduce_z(3)

    def encode_back(b, r0):
        m = lanes(MASK[pl.ds(r0, MAXLEN), :], 4)
        back = dot_nt(LB[pl.ds(r0, MAXLEN), :], w(3, 4)) * m
        DGD[pl.ds(r0, MAXLEN), :] = back
        low = back.astype(bf16)
        before, after = neighbours(low.astype(f32))
        O[pl.ds(r0, MAXLEN), 0:D] = after
        O[pl.ds(r0, MAXLEN), D : 2 * D] = low
        O[pl.ds(r0, MAXLEN), 2 * D : 3 * D] = before

    each(encode_back, {0: [(reduce_a, 5), (reduce_z, 4), (reduce_end, 2)]})
    proj_grads(ENCT, LB, 3)
    reduce_peer(6)
    kernel_grad(
        AT,
        0,
        {
            0: [(reduce_peer, 7), (reduce_a, 6), (reduce_b, 5)],
            1: [(reduce_peer, 8), (reduce_a, 7), (reduce_end, 3)],
            2: [(reduce_peer, 9), (reduce_a, 8), (reduce_z, 5), (reduce_end, 4)],
        },
    )

    def decoded_result(b, r0):
        m = lanes(MASK[pl.ds(r0, MAXLEN), :], 4)
        value = (DEC[pl.ds(r0, MAXLEN), :] + dot_nn(S[pl.ds(r0, MAXLEN), :], w(9, 12))) * m
        OB[pl.ds(r0, MAXLEN), :] = value.astype(bf16)

    def input_back(b, r0):
        m = lanes(MASK[pl.ds(r0, MAXLEN), :], 4)
        total = None
        for k in range(KERNEL):
            term = dot_nt(O[pl.ds(r0, MAXLEN), k * D : (k + 1) * D], w(k, k + 1))
            total = term if total is None else total + term
        slope = gelu_pair(FR[pl.ds(r0, MAXLEN), :].astype(f32))[1]
        STR[pl.ds(r0, MAXLEN), :] = (DGD[pl.ds(r0, MAXLEN), :] + slope * m * total).astype(bf16)

    each(
        decoded_result,
        {
            0: [(reduce_a, 9), (reduce_b, 6)],
            1: [(reduce_b, 7), (reduce_z, 6)],
            2: [(reduce_b, 8), (reduce_z, 7), (reduce_end, 5)],
        },
    )
    out_own = pltpu.make_async_copy(OB.at[:, cols], out_hbm.at[mine, :], lsem.at[3])
    out_own.start()
    at_out = place()
    send(lambda: OB.at[:, cols_other], lambda: out_hbm.at[mine, :], dev_peer, at_out)
    each(
        input_back,
        {
            0: [(reduce_b, 9), (reduce_z, 8), (reduce_end, 6)],
            1: [(reduce_z, 9), (reduce_end, 7)],
            2: [(reduce_end, 8)],
        },
    )
    in_own = pltpu.make_async_copy(STR.at[:, cols], input_hbm.at[mine, :], lsem.at[4])
    in_own.start()
    at_in = place()
    send(lambda: STR.at[:, cols_other], lambda: input_hbm.at[mine, :], dev_peer, at_in)
    reduce_end(9)

    at_rows, at_quad, at_line, at_norm = place(), place(3), place(3), place()

    def adafactor():
        beta = 1.0 - STEP ** (-0.8)
        grads = GF[...].reshape(GROUPS12 * BLOCK, HALF)
        squares = grads * grads
        floored = squares + square_floor
        RSUM[0] = jnp.broadcast_to(jnp.sum(floored, axis=1, keepdims=True), (GROUPS12 * BLOCK, 128))
        send(lambda: RSUM.at[0], lambda: RSUM.at[1], dev_peer, at_rows)
        old = []
        for g in range(GROUPS12):
            if g < 3:
                row = conv_rows[g, 0:1]
            elif g >= 9:
                row = conv_rows[g - 9, 1:2]
            elif g in (3, 8):
                row = proj_rows[g // 8 : g // 8 + 1]
            else:
                level, t = (g - 4) // 2, g % 2
                row = book_rows[level : level + 1, BLOCK * t : BLOCK * (t + 1)]
            old.append(jnp.broadcast_to(row, (128, BLOCK)).T)
        old = jnp.concatenate(old, axis=0)
        ST[0] = jnp.zeros((16, HALF), f32)
        for i, (g0, g1) in enumerate(MATRICES):
            ST[0, i : i + 1, :] = jnp.sum(floored[g0 * BLOCK : g1 * BLOCK], axis=0, keepdims=True)
        arrived(RSUM.at[1], at_rows)
        rowstat = beta * old + (1.0 - beta) * (RSUM[0] + RSUM[1])
        ROWSTAT[...] = rowstat
        weighted = squares / lanes(rowstat, 2)
        lane_at = lax.broadcasted_iota(jnp.int32, (1, 128), 1)
        packed = jnp.zeros((1, 128), f32)
        for i, (g0, g1) in enumerate(MATRICES):
            part = slice(g0 * BLOCK, g1 * BLOCK)
            ST[0, 6 + i : 7 + i, :] = jnp.sum(weighted[part], axis=0, keepdims=True)
            packed = jnp.where(lane_at == i, jnp.sum(rowstat[part], axis=0, keepdims=True), packed)
        ST[0, 12:13, 0:128] = packed
        for k, dev in enumerate((dev_x, dev_y, dev_diagonal)):
            send(lambda: ST.at[0], lambda k=k: ST.at[1 + k], dev, at_quad + k)
        for k in range(3):
            arrived(ST.at[1 + k], at_quad + k)
        ST[4] = (ST[0] + ST[1]) + (ST[2] + ST[3])
        for k in range(NZ - 1):
            send(lambda: ST.at[4], lambda k=k: ST.at[5 + k], dev_z[k], at_line + k)
        for k in range(NZ - 1):
            arrived(ST.at[5 + k], at_line + k)
        sums = (ST[4] + ST[5]) + (ST[6] + ST[7])
        old_cols = (conv_cols[0:1], proj_cols[0:1], book_cols[0:1], book_cols[1:2], proj_cols[1:2], conv_cols[1:2])
        NM[0] = jnp.zeros((8, 128), f32)
        COLSTAT[6:8, :] = jnp.zeros((2, HALF), f32)
        SCALARS[6:8, :] = jnp.zeros((2, 128), f32)
        for i in range(len(MATRICES)):
            colstat = beta * old_cols[i] + (1.0 - beta) * sums[i : i + 1]
            COLSTAT[i : i + 1, :] = colstat
            total = jnp.sum(jnp.where(lane_at == i, sums[12:13, 0:128], 0.0), axis=1, keepdims=True)
            norm = total * jnp.sum(sums[6 + i : 7 + i] / colstat, axis=1, keepdims=True)
            SCALARS[i : i + 1, :] = jnp.broadcast_to(total, (1, 128))
            NM[0, i : i + 1, :] = jnp.broadcast_to(norm, (1, 128))
        send(lambda: NM.at[0], lambda: NM.at[1], dev_peer, at_norm)
        arrived(NM.at[1], at_norm)
        SCALARS[8:16, :] = NM[0] + NM[1]

    adafactor()

    arrived(out_hbm.at[theirs, :], at_out)
    arrived(input_hbm.at[theirs, :], at_in)
    out_own.wait()
    in_own.wait()
    for src, at in unsent:
        remote(src(), src(), dev_peer, at).wait_send()


def final_kernel(
    decoded_hbm,
    back_hbm,
    grads,
    rowstat,
    colstat,
    scalars,
    conv_weight,
    proj_weight,
    codebooks,
    out_hbm,
    input_hbm,
    conv_grad,
    proj_grad,
    book_grad,
    conv_rows_out,
    conv_cols_out,
    proj_rows_out,
    proj_cols_out,
    book_rows_out,
    book_cols_out,
    conv_new,
    proj_new,
    book_new,
    buffer,
    sem,
):
    chunks = 4
    rows = decoded_hbm.shape[0] // chunks
    loads, stores = [], []
    for i, (src, dst) in enumerate(((decoded_hbm, out_hbm), (back_hbm, input_hbm))):
        for k in range(chunks):
            at = pl.ds(k * rows, rows)
            loads.append(pltpu.make_async_copy(src.at[at, :], buffer.at[i, at, :], sem.at[i * chunks + k]))
            stores.append(pltpu.make_async_copy(buffer.at[i, at, :], dst.at[at, :], sem.at[(2 + i) * chunks + k]))
    for copy in loads:
        copy.start()
    for load, store in zip(loads, stores):
        load.wait()
        store.start()
    size = grads.shape[1] * NZ * NY * NX * D
    for i, (g0, g1) in enumerate(MATRICES):
        factor = jnp.maximum(1.0, jnp.sqrt(scalars[8 + i : 9 + i] / ((g1 - g0) * size)) / clip_level)
        total = lanes(scalars[i : i + 1], 2)
        rate = (2.0 / math.sqrt(KERNEL * D), 2.0 / math.sqrt(D), 2.0)[(0, 1, 2, 2, 1, 0)[i]]
        for g in range(g0, g1):
            grad = grads[g]
            rows = rowstat[g * BLOCK : (g + 1) * BLOCK]
            update = grad * lax.rsqrt(lanes(rows, 2) * colstat[i : i + 1] / total)
            step = rate * (update / lanes(factor, 2))
            row = rows.T[0:1]
            k = g - g0
            if i in (0, 5):
                conv_grad[i // 5, k] = grad
                conv_new[i // 5, k] = conv_weight[i // 5, k] - step
                conv_rows_out[k, i // 5 : i // 5 + 1] = row
            elif i in (1, 4):
                proj_grad[i // 4] = grad
                proj_new[i // 4] = proj_weight[i // 4] - step
                proj_rows_out[i // 4 : i // 4 + 1] = row
            else:
                part = slice(BLOCK * k, BLOCK * (k + 1))
                book_grad[i - 2, part] = grad
                book_new[i - 2, part] = codebooks[i - 2, part] - step
                book_rows_out[i - 2 : i - 1, part] = row
    conv_cols_out[0:1] = colstat[0:1]
    conv_cols_out[1:2] = colstat[5:6]
    proj_cols_out[0:1] = colstat[1:2]
    proj_cols_out[1:2] = colstat[4:5]
    book_cols_out[...] = colstat[2:4]
    for store in stores:
        store.wait()


def fused_body(
    frames,
    cotangent,
    lengths,
    frame_mask,
    code_index,
    conv_weight,
    proj_weight,
    codebooks,
    conv_rows,
    conv_cols,
    proj_rows,
    proj_cols,
    book_rows,
    book_cols,
):
    vmem = pl.BlockSpec(memory_space=pltpu.VMEM)
    hbm = pl.BlockSpec(memory_space=pl.ANY)
    shape = jax.ShapeDtypeStruct
    quad = (NZ, NY, NX, BLOCK)
    part = pl.pallas_call(
        fused_kernel,
        out_shape=(
            shape(cotangent.shape, bf16),
            shape(cotangent.shape, bf16),
            shape((GROUPS12, BLOCK, HALF), f32),
            shape((GROUPS12 * BLOCK, 128), f32),
            shape((8, HALF), f32),
            shape((16, 128), f32),
        ),
        in_specs=[pl.BlockSpec(memory_space=pltpu.SMEM), hbm, hbm] + [vmem] * 11,
        out_specs=(hbm, hbm) + (vmem,) * 4,
        scratch_shapes=[
            pltpu.VMEM((GROUPS12,) + quad + (D,), bf16),
            pltpu.VMEM((2, GROUPS12) + quad + (HALF,), bf16),
            pltpu.VMEM((GROUPS12,) + quad + (HALF,), bf16),
            pltpu.VMEM((GROUPS12, NZ, NY, BLOCK, 128), bf16),
            pltpu.VMEM((GROUPS12, NZ, NX, BLOCK, 128), bf16),
            pltpu.VMEM((GROUPS12, NZ, BLOCK, 128), bf16),
            pltpu.VMEM((GROUPS12, NZ, BLOCK, 128), bf16),
            pltpu.VMEM((GROUPS12, NZ, BLOCK, 128), bf16),
            pltpu.VMEM((GROUPS12, NZ, BLOCK, 128), bf16),
            pltpu.VMEM((GROUPS12, NZ, BLOCK, HALF), bf16),
            pltpu.VMEM((NZ - 1, GROUPS12, BLOCK, HALF), bf16),
            pltpu.VMEM((ROWS, D), bf16),
            pltpu.VMEM((ROWS, 3 * D), bf16),
            pltpu.VMEM((ROWS, 3 * D), bf16),
            pltpu.VMEM((D, ROWS), bf16),
            pltpu.VMEM((D, ROWS), bf16),
            pltpu.VMEM((D, ROWS), bf16),
            pltpu.VMEM((D, ROWS), bf16),
            pltpu.VMEM((ROWS, D), f32),
            pltpu.VMEM((ROWS, D), f32),
            pltpu.VMEM((ROWS, D), f32),
            pltpu.VMEM((ROWS, D), bf16),
            pltpu.VMEM((ROWS, D), bf16),
            pltpu.VMEM((ROWS, D), bf16),
            pltpu.VMEM((ROWS, D), bf16),
            pltpu.VMEM((ROWS, D), bf16),
            pltpu.VMEM((ROWS, D), bf16),
            pltpu.VMEM((ROWS, 128), f32),
            pltpu.VMEM((2, 2, CLIPS, 1, MAXLEN), jnp.int32),
            pltpu.VMEM((8, 8, 128), f32),
            pltpu.VMEM((8, 16, HALF), f32),
            pltpu.VMEM((2, 8, 128), f32),
            pltpu.VMEM((2, GROUPS12 * BLOCK, 128), f32),
            pltpu.SemaphoreType.DMA((192,)),
            pltpu.SemaphoreType.DMA((192,)),
            pltpu.SemaphoreType.DMA((8,)),
        ],
        compiler_params=pltpu.CompilerParams(
            collective_id=0, has_side_effects=True, vmem_limit_bytes=63 * 2**20
        ),
        name="step",
    )(
        lengths,
        frames,
        cotangent,
        frame_mask.reshape(2, CLIPS, 1, MAXLEN),
        code_index.reshape(2, 2, CLIPS, 1, MAXLEN),
        conv_weight,
        proj_weight,
        codebooks,
        jnp.swapaxes(conv_rows, 0, 1),
        proj_rows,
        book_rows,
        conv_cols,
        proj_cols,
        book_cols,
    )
    out = pl.pallas_call(
        final_kernel,
        out_shape=(
            shape(cotangent.shape, bf16),
            shape(cotangent.shape, bf16),
            shape(conv_weight.shape, f32),
            shape(proj_weight.shape, f32),
            shape(codebooks.shape, f32),
            shape((KERNEL, 2, BLOCK), f32),
            shape(conv_cols.shape, f32),
            shape(proj_rows.shape, f32),
            shape(proj_cols.shape, f32),
            shape(book_rows.shape, f32),
            shape(book_cols.shape, f32),
            shape(conv_weight.shape, f32),
            shape(proj_weight.shape, f32),
            shape(codebooks.shape, f32),
        ),
        in_specs=[hbm, hbm] + [vmem] * 7,
        out_specs=(hbm, hbm) + (vmem,) * 12,
        scratch_shapes=[pltpu.VMEM((2,) + cotangent.shape, bf16), pltpu.SemaphoreType.DMA((16,))],
        compiler_params=pltpu.CompilerParams(vmem_limit_bytes=63 * 2**20),
        name="final",
    )(*part, conv_weight, proj_weight, codebooks)
    return out[:5] + (jnp.swapaxes(out[5], 0, 1),) + out[6:]


def solution(mesh):
    placed = (
        P("dp", None),
        P("dp", "chan"),
        P("dp"),
        P("dp"),
        P(None, "dp", "chan"),
        P(None, None, "dp", "chan"),
        P(None, "dp", "chan"),
        P(None, "dp", "chan"),
        P(None, None, "dp"),
        P(None, "chan"),
        P(None, "dp"),
        P(None, "chan"),
        P(None, "dp"),
        P(None, "chan"),
    )
    fits = mesh.shape["dp"] == NZ * NY * NX and mesh.shape["chan"] == 2
    return jax.shard_map(
        fused_body if fits else general_body,
        mesh=mesh,
        in_specs=placed,
        out_specs=(
            P("dp", "chan"),
            P("dp", "chan"),
            P(None, None, "dp", "chan"),
            P(None, "dp", "chan"),
            P(None, "dp", "chan"),
            P(None, None, "dp"),
            P(None, "chan"),
            P(None, "dp"),
            P(None, "chan"),
            P(None, "dp"),
            P(None, "chan"),
            P(None, None, "dp", "chan"),
            P(None, "dp", "chan"),
            P(None, "dp", "chan"),
        ),
        check_vma=False,
    )
```

```python
import functools
import math

import jax
import jax.numpy as jnp
from jax import lax
from jax.experimental import pallas as pl
from jax.experimental.pallas import tpu as pltpu
from jax.sharding import PartitionSpec as P

D = 512
CODES = 1024
KERNEL = 3
STEP = 10
MAXLEN = 512
MICRO = 2


square_floor = 1e-30
clip_level = 0.5
f32 = jnp.float32
bf16 = jnp.bfloat16


def shifted(signal, length):
    channels = signal.shape[-1]
    blocks = signal.reshape(-1, length, channels)
    padded = jnp.pad(blocks, ((0, 0), (1, 1), (0, 0)))
    joined = jnp.concatenate(
        [padded[:, 0:length], padded[:, 1 : length + 1], padded[:, 2 : length + 2]], axis=2
    )
    return joined.reshape(-1, 3 * channels)


def unshift(partial_terms, length):
    channels = partial_terms.shape[-1] // 3
    blocks = partial_terms.reshape(-1, length, 3, channels)
    padded = jnp.pad(blocks, ((0, 0), (1, 1), (0, 0), (0, 0)))
    summed = padded[:, 2 : length + 2, 0] + padded[:, 1 : length + 1, 1] + padded[:, 0:length, 2]
    return summed.reshape(-1, channels)


def gelu_back(values, upstream):
    return jax.vjp(jax.nn.gelu, values)[1](upstream)[0]


def fetch(conv_weight, proj_weight, codebooks):
    return (
        lax.all_gather(conv_weight.astype(bf16), "dp", axis=2, tiled=True),
        lax.all_gather(proj_weight.astype(bf16), "dp", axis=1, tiled=True),
        lax.all_gather(codebooks.astype(bf16), "dp", axis=1, tiled=True),
    )


def reduce_grads(conv_total, proj_total, book_total):
    return (
        lax.psum_scatter(conv_total, "dp", scatter_dimension=2, tiled=True),
        lax.psum_scatter(proj_total, "dp", scatter_dimension=1, tiled=True),
        lax.psum_scatter(book_total, "dp", scatter_dimension=1, tiled=True),
    )


def contract(left, right):
    return jnp.einsum("fc,fd->cd", left, right, preferred_element_type=f32)


def transpose_product(left, right):
    return jnp.einsum("fd,cd->fc", left, right, preferred_element_type=f32)


def general_body(
    frames,
    cotangent,
    lengths,
    frame_mask,
    code_index,
    conv_weight,
    proj_weight,
    codebooks,
    conv_rows,
    conv_cols,
    proj_rows,
    proj_cols,
    book_rows,
    book_cols,
):
    length = MAXLEN
    block_rows = frames.shape[0] // MICRO
    half_width = cotangent.shape[1]
    chan_place = lax.axis_index("chan")
    row_place = jnp.arange(frames.shape[0], dtype=jnp.int32) % length
    live = (row_place < jnp.repeat(lengths, length, total_repeat_length=frames.shape[0])) & (
        frame_mask > 0
    )
    weight_mask = live.astype(f32)[:, None]
    live_total = lax.psum(jnp.sum(weight_mask), "dp")
    vq_scale = 2.0 / live_total
    running = None
    out_pieces = []
    grad_pieces = []
    for block_number in range(MICRO):
        first_row = block_number * block_rows
        last_row = first_row + block_rows
        conv_bank, proj_bank, book_bank = fetch(conv_weight, proj_weight, codebooks)
        conv_enc = conv_bank[0].reshape(-1, half_width)
        conv_dec = conv_bank[1].reshape(-1, half_width)
        frame_part = frames[first_row:last_row]
        frame_wide = frame_part.astype(f32)
        own_part = lax.dynamic_slice_in_dim(frame_wide, chan_place * half_width, half_width, 1)
        masked = weight_mask[first_row:last_row]
        cot_part = jnp.where(masked > 0, cotangent[first_row:last_row], jnp.zeros((), bf16))
        code_range = jnp.arange(book_bank.shape[1], dtype=jnp.int32)
        onehot_one = (code_index[0, first_row:last_row, 0][:, None] == code_range[None, :]).astype(
            bf16
        )
        onehot_two = (code_index[1, first_row:last_row, 0][:, None] == code_range[None, :]).astype(
            bf16
        )
        activated = (jax.nn.gelu(frame_wide) * masked).astype(bf16)
        stack_one = shifted(activated, length)
        branch = jnp.dot(stack_one, conv_enc, preferred_element_type=f32)
        encoded = (own_part + branch) * masked
        enc_full = lax.all_gather(encoded.astype(bf16), "chan", axis=1, tiled=True)
        latent = jnp.dot(enc_full, proj_bank[0], preferred_element_type=f32)
        level_one = jnp.dot(onehot_one, book_bank[0], preferred_element_type=f32)
        level_two = jnp.dot(onehot_two, book_bank[1], preferred_element_type=f32)
        quantized = level_one + level_two
        straight = (latent + (quantized - latent)).astype(bf16)
        straight_full = lax.all_gather(straight, "chan", axis=1, tiled=True)
        decoded = jnp.dot(straight_full, proj_bank[1], preferred_element_type=f32)
        decoder_in = (jax.nn.gelu(decoded) * masked).astype(bf16)
        decoder_full = lax.all_gather(decoder_in, "chan", axis=1, tiled=True)
        stack_two = shifted(decoder_full, length)
        result = (decoded + jnp.dot(stack_two, conv_dec, preferred_element_type=f32)) * masked
        out_pieces.append(result.astype(bf16))
        conv_dec_grad = contract(stack_two, cot_part)
        in_partial = unshift(transpose_product(cot_part, conv_dec), length)
        in_back = lax.psum_scatter(in_partial, "chan", scatter_dimension=1, tiled=True)
        decoded_back = (cot_part.astype(f32) + gelu_back(decoded, masked * in_back)).astype(bf16)
        proj_dec_grad = contract(straight_full, decoded_back)
        straight_back = lax.psum_scatter(
            transpose_product(decoded_back, proj_bank[1]), "chan", scatter_dimension=1, tiled=True
        )
        resid_one = latent - level_one
        resid_two = resid_one - level_two
        pulled = vq_scale * masked * (resid_one + resid_two)
        latent_back = (straight_back + pulled).astype(bf16)
        one_back = (-pulled).astype(bf16)
        two_back = (-(vq_scale * masked * resid_two)).astype(bf16)
        book_one_grad = contract(onehot_one, one_back)
        book_two_grad = contract(onehot_two, two_back)
        proj_enc_grad = contract(enc_full, latent_back)
        encoded_back = lax.psum_scatter(
            transpose_product(latent_back, proj_bank[0]), "chan", scatter_dimension=1, tiled=True
        )
        branch_back = (encoded_back * masked).astype(bf16)
        conv_enc_grad = contract(stack_one, branch_back)
        activated_back = unshift(transpose_product(branch_back, conv_enc), length)
        input_partial = gelu_back(frame_wide, masked * activated_back)
        input_own = lax.psum_scatter(input_partial, "chan", scatter_dimension=1, tiled=True)
        grad_pieces.append((encoded_back * masked + input_own).astype(bf16))
        conv_blockgrad = jnp.stack(
            [
                conv_enc_grad.reshape(KERNEL, -1, half_width),
                conv_dec_grad.reshape(KERNEL, -1, half_width),
            ]
        )
        proj_blockgrad = jnp.stack([proj_enc_grad, proj_dec_grad])
        book_blockgrad = jnp.stack([book_one_grad, book_two_grad])
        reduced = reduce_grads(conv_blockgrad, proj_blockgrad, book_blockgrad)
        running = (
            reduced
            if running is None
            else (running[0] + reduced[0], running[1] + reduced[1], running[2] + reduced[2])
        )
    conv_grad, proj_grad, book_grad = running
    decoded_out = jnp.concatenate(out_pieces, axis=0)
    input_grad = jnp.concatenate(grad_pieces, axis=0)
    beta_two = 1.0 - STEP ** (-0.8)
    squares_conv = conv_grad * conv_grad + square_floor
    squares_proj = proj_grad * proj_grad + square_floor
    squares_book = book_grad * book_grad + square_floor
    row_sums = lax.psum(
        (
            jnp.sum(squares_conv, axis=3),
            jnp.sum(squares_proj, axis=2),
            jnp.sum(squares_book, axis=2),
        ),
        "chan",
    )
    rowstat_conv = beta_two * conv_rows + (1.0 - beta_two) * row_sums[0]
    rowstat_proj = beta_two * proj_rows + (1.0 - beta_two) * row_sums[1]
    rowstat_book = beta_two * book_rows + (1.0 - beta_two) * row_sums[2]
    col_sums = lax.psum(
        (
            jnp.sum(squares_conv, axis=(1, 2)),
            jnp.sum(squares_proj, axis=1),
            jnp.sum(squares_book, axis=1),
            jnp.sum(rowstat_conv, axis=(1, 2)),
            jnp.sum(rowstat_proj, axis=1),
            jnp.sum(rowstat_book, axis=1),
        ),
        "dp",
    )
    colstat_conv = beta_two * conv_cols + (1.0 - beta_two) * col_sums[0]
    colstat_proj = beta_two * proj_cols + (1.0 - beta_two) * col_sums[1]
    colstat_book = beta_two * book_cols + (1.0 - beta_two) * col_sums[2]
    update_conv = conv_grad * lax.rsqrt(
        rowstat_conv[..., None] * colstat_conv[:, None, None, :] / col_sums[3][:, None, None, None]
    )
    update_proj = proj_grad * lax.rsqrt(
        rowstat_proj[..., None] * colstat_proj[:, None, :] / col_sums[4][:, None, None]
    )
    update_book = book_grad * lax.rsqrt(
        rowstat_book[..., None] * colstat_book[:, None, :] / col_sums[5][:, None, None]
    )
    norm_sums = lax.psum(
        (
            jnp.sum(update_conv * update_conv, axis=(1, 2, 3)),
            jnp.sum(update_proj * update_proj, axis=(1, 2)),
            jnp.sum(update_book * update_book, axis=(1, 2)),
        ),
        ("dp", "chan"),
    )
    factor_conv = jnp.maximum(1.0, jnp.sqrt(norm_sums[0] / (KERNEL * D * D)) / clip_level)
    factor_proj = jnp.maximum(1.0, jnp.sqrt(norm_sums[1] / (D * D)) / clip_level)
    factor_book = jnp.maximum(1.0, jnp.sqrt(norm_sums[2] / (CODES * D)) / clip_level)
    rate_conv = 2.0 / math.sqrt(KERNEL * D)
    rate_proj = 2.0 / math.sqrt(D)
    updated_conv = conv_weight - rate_conv * (update_conv / factor_conv[:, None, None, None])
    updated_proj = proj_weight - rate_proj * (update_proj / factor_proj[:, None, None])
    updated_book = codebooks - 2.0 * (update_book / factor_book[:, None, None])
    return (
        decoded_out,
        input_grad,
        conv_grad,
        proj_grad,
        book_grad,
        rowstat_conv,
        colstat_conv,
        rowstat_proj,
        colstat_proj,
        rowstat_book,
        colstat_book,
        updated_conv,
        updated_proj,
        updated_book,
    )


MESH = pl.DeviceIdType.MESH
CLIPS = 3
ROWS = CLIPS * MAXLEN
GROUPS12 = 12
NZ, NY, NX = 4, 2, 2
BLOCK = 32
SEMAPHORES = 256
HALF = 256
GELU_A = math.sqrt(2.0 / math.pi)
GELU_B = 0.044715
MATRICES = ((0, 3), (3, 4), (4, 6), (6, 8), (8, 9), (9, 12))


def gelu_pair(x):
    x2 = x * x
    t = jnp.tanh(x * (GELU_A + GELU_A * GELU_B * x2))
    half = 0.5 + 0.5 * t
    value = x * half
    return value, half + value * (1.0 - t) * (GELU_A + 3.0 * GELU_A * GELU_B * x2)


def lanes(m, n):
    return jnp.concatenate([m] * n, axis=1)


def dot_nn(a, b):
    return jnp.dot(a, b, preferred_element_type=f32)


def dot_nt(a, b):
    return lax.dot_general(a, b, (((1,), (1,)), ((), ())), preferred_element_type=f32)


def neighbours(v):
    rows = v.shape[0]
    row = lax.broadcasted_iota(jnp.int32, (8, v.shape[1]), 0)
    before, after = pltpu.roll(v, 1, 0), pltpu.roll(v, rows - 1, 0)
    before = jnp.concatenate([jnp.where(row == 0, 0.0, before[:8]), before[8:]], axis=0)
    after = jnp.concatenate([after[:-8], jnp.where(row == 7, 0.0, after[-8:])], axis=0)
    return before.astype(bf16), after.astype(bf16)


PIECES = ((0, 1, "f"), (1, 2, "f"), (2, 3, "f"), (3, 4, "f"), (4, 6, "f"), (6, 8, "f"), (8, 9, "f"), (9, 11, "f"), (11, 12, "f"))
PARTS = ((4, 6, "f"), (6, 8, "f"), (9, 10, "f"), (10, 12, "f"), (8, 9, "f"), (3, 4, "f"), (0, 1, "f"), (1, 2, "f"), (2, 3, "f"))
PLANES = max(1, sum((g1 - g0) * (kind == "l") for g0, g1, kind in PARTS))
SCHEDULE = {
    "start": {
        0: (("z", 2), ("z", 0), ("z", 1), ("z", 3), ("z", 4), ("z", 5), ("z", 7),),
    },
    "upstream": {
        1: (("l", 2),),
        2: (("l", 0), ("l", 1), ("l", 3), ("d", 2), ("d", 0), ("l", 4), ("d", 1), ("q", 2), ("l", 5), ("d", 3), ("q", 0), ("d", 4), ("z", 6), ("q", 1),),
    },
    "encode": {
        1: (("d", 5), ("l", 6), ("z", 8),),
        2: (("q", 3), ("q", 4), ("l", 7),),
    },
    "project": {
        2: (("q", 5),),
    },
    "level_one": {
        0: (("l", 8),),
        2: (("d", 6),),
    },
    "quantize": {
        2: (("d", 7),),
    },
    "book0": {
        0: (("d", 8),),
        1: (("P", 0), ("q", 6),),
    },
    "book1": {
        1: (("q", 7), ("P", 1),),
    },
    "decode": {
        0: (("q", 8), ("A", 0),),
        2: (("A", 1),),
    },
    "kg9": {
        1: (("P", 2),),
        5: (("B", 0), ("P", 3), ("A", 2),),
    },
    "decode_back": {
        1: (("A", 3),),
        2: (("Z", 0),),
    },
    "pg8": {
        0: (("B", 2),),
        1: (("P", 4), ("B", 1),),
    },
    "encode_back": {
        2: (("A", 4),),
    },
    "pg3": {
        1: (("P", 5), ("B", 3),),
    },
    "kg0": {
        0: (("Z", 2),),
        1: (("P", 6),),
        2: (("A", 5), ("Z", 1),),
        3: (("P", 7),),
        4: (("A", 6), ("B", 4),),
        5: (("P", 8),),
    },
    "decoded": {
        0: (("A", 7), ("E", 2),),
        3: (("B", 5), ("A", 8), ("Z", 3),),
        5: (("B", 6), ("E", 1),),
    },
    "input": {
        0: (("Z", 4),),
        2: (("B", 7),),
        3: (("Z", 5), ("E", 0),),
        4: (("B", 8),),
        5: (("Z", 6), ("E", 3),),
    },
    "end": {
        0: (("Z", 7), ("E", 4), ("R", 0), ("Z", 8), ("S", 0), ("E", 5), ("E", 6), ("E", 7), ("T", 0), ("E", 8), ("R", 1), ("S", 1), ("N", 0), ("T", 1), ("N", 1),),
    },
}


def fused_kernel(
    lengths,
    frames_hbm,
    cot_hbm,
    index_hbm,
    conv_hbm,
    proj_hbm,
    books_hbm,
    frame_mask,
    conv_rows,
    proj_rows,
    book_rows,
    conv_cols,
    proj_cols,
    book_cols,
    out_hbm,
    input_hbm,
    grads_hbm,
    rows_hbm,
    COLSTAT,
    SCALARS,
    W,
    G,
    RP,
    AX,
    AY,
    BX,
    BY,
    BXS,
    BYS,
    TS,
    ZR,
    FR,
    S,
    O,
    AT,
    ENCT,
    STRT,
    DINT,
    LAT,
    DEC,
    DGD,
    B1,
    B2,
    STR,
    DB,
    LB,
    OB,
    ZQ,
    PS,
    QX,
    QY,
    QS,
    QB,
    conv_weight,
    proj_weight,
    codebooks,
    MASK,
    IDX,
    CN,
    GF,
    ROWSTAT,
    STA,
    STB,
    NM,
    RSUM,
    ssem,
    rsem,
    lsem,
):
    me = lax.axis_index("dp")
    c = lax.axis_index("chan")
    z, y, x = me // (NY * NX), (me // NX) % NY, me % NX
    far_y, far_x, other = 1 - y, 1 - x, 1 - c

    def dp_of(zz, yy, xx):
        return (zz * (NY * NX) + yy * NX + xx, c)

    dev_x, dev_y, dev_diagonal = dp_of(z, y, far_x), dp_of(z, far_y, x), dp_of(z, far_y, far_x)
    dev_z = [dp_of(lax.rem(z + k, NZ), y, x) for k in range(1, NZ)]
    dev_peer = (me, other)
    to_z = [lax.rem(z + k, NZ) for k in range(1, NZ)]
    from_z = [lax.rem(z + NZ - k, NZ) for k in range(1, NZ)]
    cols = pl.ds(pl.multiple_of(c * HALF, HALF), HALF)
    cols_other = pl.ds(pl.multiple_of(other * HALF, HALF), HALF)
    quarter = (
        pl.ds(pl.multiple_of(c * HALF, HALF), 128),
        pl.ds(pl.multiple_of(c * HALF + 128, 128), 128),
    )
    mine = pl.ds(pl.multiple_of(c * ROWS, ROWS), ROWS)
    theirs = pl.ds(pl.multiple_of(other * ROWS, ROWS), ROWS)

    counter = [0]
    unsent = []

    def place(n=1):
        counter[0] += n
        return counter[0] - n

    def remote(src, dst, dev, at):
        return pltpu.make_async_remote_copy(
            src_ref=src,
            dst_ref=dst,
            send_sem=ssem.at[at],
            recv_sem=rsem.at[at],
            device_id=dev,
            device_id_type=MESH,
        )

    def send(src, dst, dev, at):
        remote(src(), dst(), dev, at).start()
        unsent.append((src, at))

    def arrived(dst, at):
        remote(dst, dst, dev_peer, at).wait_recv()

    barrier = pltpu.get_barrier_semaphore()
    partners = [dev_x, dev_y, dev_diagonal, dev_peer] + dev_z
    for dev in partners:
        pl.semaphore_signal(barrier, inc=1, device_id=dev, device_id_type=MESH)
    weights_in = [
        pltpu.make_async_copy(src, dst, lsem.at[9 + i])
        for i, (src, dst) in enumerate(((conv_hbm, conv_weight), (proj_hbm, proj_weight), (books_hbm, codebooks)))
    ]
    for load in weights_in:
        load.start()
    index_in = pltpu.make_async_copy(index_hbm.at[:, c], IDX.at[:, c], lsem.at[2])
    index_in.start()
    frames_in = pltpu.make_async_copy(frames_hbm.at[mine, :], FR, lsem.at[0])
    frames_in.start()
    cot_in = pltpu.make_async_copy(cot_hbm.at[mine, :], OB.at[:, cols], lsem.at[1])
    cot_in.start()
    for load in weights_in:
        load.wait()

    for k in range(3):
        W[k, z, y, x, :, cols] = conv_weight[0, k].astype(bf16)
        W[9 + k, z, y, x, :, cols] = conv_weight[1, k].astype(bf16)
    W[3, z, y, x, :, cols] = proj_weight[0].astype(bf16)
    W[8, z, y, x, :, cols] = proj_weight[1].astype(bf16)
    for level in range(2):
        for t in range(2):
            W[4 + 2 * level + t, z, y, x, :, cols] = codebooks[level, BLOCK * t : BLOCK * (t + 1)].astype(bf16)
    pl.semaphore_wait(barrier, len(partners))

    pieces = PIECES
    at_z = [place(3) for p in pieces]
    at_l = [place(2) for p in pieces]
    at_d = [place(2) for p in pieces]
    at_p = [place(2) for p in pieces]
    at_cot, at_idx, at_count = place(), place(), place(6)

    def gather_z(p):
        g0, g1 = pieces[p][:2]
        for k in range(NZ - 1):
            own = lambda: W.at[g0:g1, z, y, x, :, cols]
            send(own, own, dev_z[k], at_z[p] + k)

    def gather_line(p):
        g0, g1 = pieces[p][:2]
        for k in range(NZ - 1):
            arrived(W.at[g0:g1, from_z[k], y, x, :, cols], at_z[p] + k)
        line = lambda: W.at[g0:g1, :, y, x, :, cols]
        send(line, line, dev_x, at_l[p])
        send(line, line, dev_y, at_l[p] + 1)

    def gather_diagonal(p):
        g0, g1 = pieces[p][:2]
        arrived(W.at[g0:g1, :, y, far_x, :, cols], at_l[p])
        arrived(W.at[g0:g1, :, far_y, x, :, cols], at_l[p] + 1)
        part_y = lambda: W.at[g0:g1, :, far_y, x, :, quarter[0]]
        send(part_y, part_y, dev_x, at_d[p])
        part_x = lambda: W.at[g0:g1, :, y, far_x, :, quarter[1]]
        send(part_x, part_x, dev_y, at_d[p] + 1)
        near = lambda: W.at[g0:g1, :, y, :, :, cols]
        send(near, near, dev_peer, at_p[p])

    def gather_peer(p):
        g0, g1 = pieces[p][:2]
        arrived(W.at[g0:g1, :, far_y, far_x, :, quarter[0]], at_d[p])
        arrived(W.at[g0:g1, :, far_y, far_x, :, quarter[1]], at_d[p] + 1)
        far = lambda: W.at[g0:g1, :, far_y, :, :, cols]
        send(far, far, dev_peer, at_p[p] + 1)

    def plane_own(p):
        g0, g1 = pieces[p][:2]
        own = lambda: W.at[g0:g1, z, y, x, :, cols]
        send(own, own, dev_x, at_l[p])
        send(own, own, dev_y, at_l[p] + 1)

    def plane_diagonal(p):
        g0, g1 = pieces[p][:2]
        arrived(W.at[g0:g1, z, y, far_x, :, cols], at_l[p])
        arrived(W.at[g0:g1, z, far_y, x, :, cols], at_l[p] + 1)
        part_y = lambda: W.at[g0:g1, z, far_y, x, :, quarter[0]]
        send(part_y, part_y, dev_x, at_d[p])
        part_x = lambda: W.at[g0:g1, z, y, far_x, :, quarter[1]]
        send(part_x, part_x, dev_y, at_d[p] + 1)

    def plane_line(p):
        g0, g1 = pieces[p][:2]
        arrived(W.at[g0:g1, z, far_y, far_x, :, quarter[0]], at_d[p])
        arrived(W.at[g0:g1, z, far_y, far_x, :, quarter[1]], at_d[p] + 1)
        plane = lambda: W.at[g0:g1, z, :, :, :, cols]
        for k in range(NZ - 1):
            send(plane, plane, dev_z[k], at_z[p] + k)

    def plane_peer(p):
        g0, g1 = pieces[p][:2]
        for k in range(NZ - 1):
            arrived(W.at[g0:g1, from_z[k], :, :, :, cols], at_z[p] + k)
        whole = lambda: W.at[g0:g1, :, :, :, :, cols]
        send(whole, whole, dev_peer, at_p[p])

    def gathered(p):
        g0, g1 = pieces[p][:2]
        if pieces[p][2] == "l":
            arrived(W.at[g0:g1, :, :, :, :, cols_other], at_p[p])
            return
        arrived(W.at[g0:g1, :, y, :, :, cols_other], at_p[p])
        arrived(W.at[g0:g1, :, far_y, :, :, cols_other], at_p[p] + 1)

    parts = PARTS
    local, planes = [], 0
    for g0, g1, kind in parts:
        local.append(planes)
        planes += (g1 - g0) * (kind == "l")
    at_rp = [place() for p in parts]
    at_ra = [place(2) for p in parts]
    at_rb = [place(2) for p in parts]
    at_rz = [place(3) for p in parts]

    def reduce_peer(p):
        g0, g1 = parts[p][:2]
        send(lambda: G.at[other, g0:g1], lambda: RP.at[g0:g1], dev_peer, at_rp[p])

    def reduce_a(p):
        g0, g1 = parts[p][:2]
        arrived(RP.at[g0:g1], at_rp[p])

        @pl.loop(g0, g1)
        def _(g):
            G[c, g] = (G[c, g].astype(f32) + RP[g].astype(f32)).astype(bf16)

        send(lambda: G.at[c, g0:g1, :, :, far_x, :, 0:128], lambda: AX.at[g0:g1], dev_x, at_ra[p])
        send(lambda: G.at[c, g0:g1, :, far_y, :, :, 128:256], lambda: AY.at[g0:g1], dev_y, at_ra[p] + 1)

    def reduce_b(p):
        g0, g1 = parts[p][:2]
        arrived(AX.at[g0:g1], at_ra[p])
        arrived(AY.at[g0:g1], at_ra[p] + 1)

        @pl.loop(g0, g1)
        def _(g):
            BXS[g] = (G[c, g, :, y, far_x, :, 128:256].astype(f32) + AY[g, :, far_x].astype(f32)).astype(bf16)
            BYS[g] = (G[c, g, :, far_y, x, :, 0:128].astype(f32) + AX[g, :, far_y].astype(f32)).astype(bf16)

        send(lambda: BXS.at[g0:g1], lambda: BX.at[g0:g1], dev_x, at_rb[p])
        send(lambda: BYS.at[g0:g1], lambda: BY.at[g0:g1], dev_y, at_rb[p] + 1)

    def reduce_z(p):
        g0, g1 = parts[p][:2]
        arrived(BX.at[g0:g1], at_rb[p])
        arrived(BY.at[g0:g1], at_rb[p] + 1)

        @pl.loop(g0, g1)
        def _(g):
            base = G[c, g, :, y, x].astype(f32)
            left = base[:, :, 0:128] + (AX[g, :, y].astype(f32) + BY[g].astype(f32))
            right = base[:, :, 128:256] + (AY[g, :, x].astype(f32) + BX[g].astype(f32))
            TS[g, :, :, 0:128] = left.astype(bf16)
            TS[g, :, :, 128:256] = right.astype(bf16)

        for k in range(NZ - 1):
            send(
                lambda k=k: TS.at[g0:g1, to_z[k]],
                lambda k=k: ZR.at[k, g0:g1],
                dev_z[k],
                at_rz[p] + k,
            )

    def reduce_end(p):
        g0, g1 = parts[p][:2]
        for k in range(NZ - 1):
            arrived(ZR.at[k, g0:g1], at_rz[p] + k)

        @pl.loop(g0, g1)
        def _(g):
            GF[g] = (TS[g, z].astype(f32) + ZR[0, g].astype(f32)) + (ZR[1, g].astype(f32) + ZR[2, g].astype(f32))

    def plane_reduce(p):
        g0, g1 = parts[p][:2]
        arrived(RP.at[g0:g1], at_rp[p])

        @pl.loop(g0, g1)
        def _(g):
            G[c, g] = (G[c, g].astype(f32) + RP[g].astype(f32)).astype(bf16)

        for k in range(NZ - 1):
            send(
                lambda k=k: G.at[c, g0:g1, to_z[k]],
                lambda k=k: ZQ.at[k, local[p] : local[p] + g1 - g0],
                dev_z[k],
                at_rz[p] + k,
            )

    def plane_a(p):
        g0, g1 = parts[p][:2]
        i0, i1 = local[p], local[p] + g1 - g0
        for k in range(NZ - 1):
            arrived(ZQ.at[k, i0:i1], at_rz[p] + k)
        for i in range(i0, i1):
            total = G[c, g0 + i - i0, z].astype(f32) + ZQ[0, i].astype(f32)
            PS[i] = (total + (ZQ[1, i].astype(f32) + ZQ[2, i].astype(f32))).astype(bf16)
        send(lambda: PS.at[i0:i1, :, far_x, :, 0:128], lambda: QX.at[i0:i1], dev_x, at_ra[p])
        send(lambda: PS.at[i0:i1, far_y, :, :, 128:256], lambda: QY.at[i0:i1], dev_y, at_ra[p] + 1)

    def plane_b(p):
        g0, g1 = parts[p][:2]
        i0, i1 = local[p], local[p] + g1 - g0
        arrived(QX.at[i0:i1], at_ra[p])
        arrived(QY.at[i0:i1], at_ra[p] + 1)
        for i in range(i0, i1):
            QS[0, i] = (PS[i, y, far_x, :, 128:256].astype(f32) + QY[i, far_x].astype(f32)).astype(bf16)
            QS[1, i] = (PS[i, far_y, x, :, 0:128].astype(f32) + QX[i, far_y].astype(f32)).astype(bf16)
        send(lambda: QS.at[0, i0:i1], lambda: QB.at[0, i0:i1], dev_x, at_rb[p])
        send(lambda: QS.at[1, i0:i1], lambda: QB.at[1, i0:i1], dev_y, at_rb[p] + 1)

    def plane_end(p):
        g0, g1 = parts[p][:2]
        i0, i1 = local[p], local[p] + g1 - g0
        arrived(QB.at[0, i0:i1], at_rb[p])
        arrived(QB.at[1, i0:i1], at_rb[p] + 1)
        for i in range(i0, i1):
            base = PS[i, y, x].astype(f32)
            left = base[:, 0:128] + (QX[i, y].astype(f32) + QB[1, i].astype(f32))
            right = base[:, 128:256] + (QY[i, x].astype(f32) + QB[0, i].astype(f32))
            GF[g0 + i - i0, :, 0:128] = left
            GF[g0 + i - i0, :, 128:256] = right

    sets = (((4, 12), (2, 3, 4, 5), STA), ((0, 4), (0, 1), STB))
    at_rows = [place() for q in sets]
    at_quad = [place(3) for q in sets]
    at_line = [place(3) for q in sets]
    at_norm = [place() for q in sets]
    beta = 1.0 - STEP ** (-0.8)

    def row_sums(q):
        (g0, g1), _, _ = sets[q]

        @pl.loop(g0, g1)
        def _(g):
            grad = GF[g]
            RSUM[0, g] = jnp.broadcast_to(jnp.sum(grad * grad + square_floor, axis=1, keepdims=True), (BLOCK, 128))

        send(lambda: RSUM.at[0, g0:g1], lambda: RSUM.at[1, g0:g1], dev_peer, at_rows[q])
        pltpu.make_async_copy(GF.at[g0:g1], grads_hbm.at[g0:g1], lsem.at[5 + q]).start()

    def statistics(q):
        (g0, g1), members, SUMS = sets[q]
        arrived(RSUM.at[1, g0:g1], at_rows[q])
        lane_at = lax.broadcasted_iota(jnp.int32, (1, 128), 1)
        packed = jnp.zeros((1, 128), f32)
        n = len(members)
        SUMS[0] = jnp.zeros(SUMS.shape[1:], f32)
        for j, i in enumerate(members):
            squares, weighted, rows = 0.0, 0.0, 0.0
            for g in range(*MATRICES[i]):
                if g < 3:
                    row = conv_rows[g, 0:1]
                elif g >= 9:
                    row = conv_rows[g - 9, 1:2]
                elif g in (3, 8):
                    row = proj_rows[g // 8 : g // 8 + 1]
                else:
                    level, t = (g - 4) // 2, g % 2
                    row = book_rows[level : level + 1, BLOCK * t : BLOCK * (t + 1)]
                old = jnp.broadcast_to(row, (128, BLOCK)).T
                rowstat = beta * old + (1.0 - beta) * (RSUM[0, g] + RSUM[1, g])
                ROWSTAT[g] = rowstat
                square = GF[g] * GF[g]
                squares = squares + (square + square_floor)
                weighted = weighted + square / lanes(rowstat, 2)
                rows = rows + rowstat
            SUMS[0, j : j + 1, :] = jnp.sum(squares, axis=0, keepdims=True)
            SUMS[0, n + j : n + j + 1, :] = jnp.sum(weighted, axis=0, keepdims=True)
            packed = jnp.where(lane_at == j, jnp.sum(rows, axis=0, keepdims=True), packed)
        SUMS[0, 2 * n : 2 * n + 1, 0:128] = packed
        for k, dev in enumerate((dev_x, dev_y, dev_diagonal)):
            send(lambda: SUMS.at[0], lambda k=k: SUMS.at[1 + k], dev, at_quad[q] + k)
        pltpu.make_async_copy(ROWSTAT.at[g0:g1], rows_hbm.at[g0:g1], lsem.at[7 + q]).start()

    def quad_sums(q):
        SUMS = sets[q][2]
        for k in range(3):
            arrived(SUMS.at[1 + k], at_quad[q] + k)
        SUMS[4] = (SUMS[0] + SUMS[1]) + (SUMS[2] + SUMS[3])
        for k in range(NZ - 1):
            send(lambda: SUMS.at[4], lambda k=k: SUMS.at[5 + k], dev_z[k], at_line[q] + k)

    def line_sums(q):
        _, members, SUMS = sets[q]
        for k in range(NZ - 1):
            arrived(SUMS.at[5 + k], at_line[q] + k)
        sums = (SUMS[4] + SUMS[5]) + (SUMS[6] + SUMS[7])
        lane_at = lax.broadcasted_iota(jnp.int32, (1, 128), 1)
        old_cols = (conv_cols[0:1], proj_cols[0:1], book_cols[0:1], book_cols[1:2], proj_cols[1:2], conv_cols[1:2])
        n = len(members)
        NM[0, q] = jnp.zeros((8, 128), f32)
        for j, i in enumerate(members):
            colstat = beta * old_cols[i] + (1.0 - beta) * sums[j : j + 1]
            COLSTAT[i : i + 1, :] = colstat
            total = jnp.sum(jnp.where(lane_at == j, sums[2 * n : 2 * n + 1, 0:128], 0.0), axis=1, keepdims=True)
            norm = total * jnp.sum(sums[n + j : n + j + 1] / colstat, axis=1, keepdims=True)
            SCALARS[i : i + 1, :] = jnp.broadcast_to(total, (1, 128))
            NM[0, q, i : i + 1, :] = jnp.broadcast_to(norm, (1, 128))
        send(lambda: NM.at[0, q], lambda: NM.at[1, q], dev_peer, at_norm[q])

    operations = {
        "z": gather_z,
        "l": gather_line,
        "d": gather_diagonal,
        "q": gather_peer,
        "P": reduce_peer,
        "A": reduce_a,
        "B": reduce_b,
        "Z": reduce_z,
        "E": reduce_end,
        "a": plane_own,
        "b": plane_diagonal,
        "e": plane_line,
        "h": plane_peer,
        "U": plane_reduce,
        "V": plane_a,
        "X": plane_b,
        "F": plane_end,
        "R": row_sums,
        "S": statistics,
        "T": quad_sums,
        "N": line_sums,
    }

    def perform(steps):
        for operation, p in steps:
            operations[operation](p)

    def after(phase, b):
        for k, steps in SCHEDULE.get(phase, {}).items():

            @pl.when(b == k)
            def _():
                perform(steps)

    def once(phase):
        perform(SCHEDULE.get(phase, {}).get(0, ()))

    waited = set()

    def need(a, b):
        for p, (g0, g1, _) in enumerate(pieces):
            if g0 < b and a < g1 and p not in waited:
                waited.add(p)
                gathered(p)

    def w(a, b):
        return W[a:b].reshape((b - a) * D, D)

    def each(phase, step):

        @pl.loop(0, CLIPS)
        def _(b):
            step(b, pl.multiple_of(b * MAXLEN, MAXLEN))
            after(phase, b)

    def put(half, group, value):
        G[half, group] = value.astype(bf16).reshape(NZ, NY, NX, BLOCK, HALF)

    once("start")
    lane_row = lax.broadcasted_iota(jnp.int32, (1, MAXLEN), 1)
    count = jnp.zeros((1, MAXLEN), f32)
    for core in range(2):
        for b in range(CLIPS):
            live = (lane_row < lengths[core * CLIPS + b]) & (frame_mask[core, b] > 0)
            count = count + jnp.where(live, 1.0, 0.0)
    CN[0] = jnp.broadcast_to(jnp.sum(count, axis=1, keepdims=True), (8, 128))
    for k, dev in enumerate((dev_x, dev_y, dev_diagonal)):
        send(lambda: CN.at[0], lambda k=k: CN.at[1 + k], dev, at_count + k)
    send(lambda: index_hbm.at[:, other], lambda: IDX.at[:, c], dev_peer, at_idx)
    send(lambda: cot_hbm.at[theirs, :], lambda: OB.at[:, cols], dev_peer, at_cot)

    @pl.loop(0, CLIPS)
    def _(b):
        live = (lane_row < lengths[c * CLIPS + b]) & (frame_mask[c, b] > 0)
        row = jnp.where(live, 1.0, 0.0)
        MASK[pl.ds(pl.multiple_of(b * MAXLEN, MAXLEN), MAXLEN), :] = jnp.broadcast_to(row, (128, MAXLEN)).T

    frames_in.wait()

    def activate(b, r0):
        rows = pl.ds(r0, MAXLEN)
        for k in range(0, D, 128):
            a = gelu_pair(FR[rows, k : k + 128].astype(f32))[0] * MASK[rows, :]
            S[rows, k : k + 128], S[rows, 2 * D + k : 2 * D + k + 128] = neighbours(a)
            a = a.astype(bf16)
            S[rows, D + k : D + k + 128] = a
            AT[k : k + 128, rows] = a.T

    each("activate", activate)
    for k in range(3):
        arrived(CN.at[1 + k], at_count + k)
    CN[4] = (CN[0] + CN[1]) + (CN[2] + CN[3])
    for k in range(NZ - 1):
        send(lambda: CN.at[4], lambda k=k: CN.at[5 + k], dev_z[k], at_count + 3 + k)
    cot_in.wait()
    index_in.wait()
    arrived(OB.at[:, cols_other], at_cot)
    arrived(IDX.at[:, other], at_idx)

    def upstream(b, r0):
        rows = pl.ds(r0, MAXLEN)
        for k in range(0, D, 128):
            ob = OB[rows, k : k + 128].astype(f32) * MASK[rows, :]
            O[rows, 2 * D + k : 2 * D + k + 128], O[rows, k : k + 128] = neighbours(ob)
            O[rows, D + k : D + k + 128] = ob.astype(bf16)

    each("upstream", upstream)
    for k in range(NZ - 1):
        arrived(CN.at[5 + k], at_count + 3 + k)
    scale = 2.0 / ((CN[4, 0:1] + CN[5, 0:1]) + (CN[6, 0:1] + CN[7, 0:1]))
    need(0, 3)

    def encode(b, r0):
        m = lanes(MASK[pl.ds(r0, MAXLEN), :], 4)
        branch = dot_nn(S[pl.ds(r0, MAXLEN), :], w(0, 3))
        enc = ((FR[pl.ds(r0, MAXLEN), :].astype(f32) + branch) * m).astype(bf16)
        STR[pl.ds(r0, MAXLEN), :] = enc
        ENCT[:, pl.ds(r0, MAXLEN)] = enc.T

    each("encode", encode)

    def project(b, r0):
        LAT[pl.ds(r0, MAXLEN), :] = dot_nn(STR[pl.ds(r0, MAXLEN), :], w(3, 4))

    need(3, 4)
    each("project", project)

    def slot(row):
        return ((row >> 5) & 1) * 512 + (row >> 6) * BLOCK + (row & 31)

    def onehot_rows(l, g, b):
        lane = lax.broadcasted_iota(jnp.int32, (MAXLEN, 128), 1)
        col = jnp.broadcast_to(slot(IDX[l, g, b]), (128, MAXLEN)).T
        return jnp.concatenate(
            [jnp.where(col == lane + 128 * k, 1.0, 0.0).astype(bf16) for k in range(CODES // 128)], axis=1
        )

    def chosen(l, g, b):
        book = W[4 + 2 * l : 6 + 2 * l, :, :, :, :, HALF * g : HALF * (g + 1)].reshape(CODES, HALF)
        return dot_nn(onehot_rows(l, g, b), book)

    def level_one(b, r0):
        for g in range(2):
            DEC[pl.ds(r0, MAXLEN), HALF * g : HALF * (g + 1)] = chosen(0, g, b)

    need(4, 6)
    each("level_one", level_one)

    def quantize(b, r0):
        m = lanes(MASK[pl.ds(r0, MAXLEN), :], 2)
        sc = lanes(scale, 2) * m
        for g in range(2):
            gc = slice(HALF * g, HALF * (g + 1))
            level = (DEC[pl.ds(r0, MAXLEN), gc], chosen(1, g, b))
            latent = LAT[pl.ds(r0, MAXLEN), gc]
            quantized = level[0] + level[1]
            straight = (latent + (quantized - latent)).astype(bf16)
            resid_one = latent - level[0]
            resid_two = resid_one - level[1]
            pulled = sc * (resid_one + resid_two)
            STR[pl.ds(r0, MAXLEN), gc] = straight
            STRT[gc, pl.ds(r0, MAXLEN)] = straight.T
            LAT[pl.ds(r0, MAXLEN), gc] = pulled
            B1[pl.ds(r0, MAXLEN), gc] = (-pulled).astype(bf16)
            B2[pl.ds(r0, MAXLEN), gc] = (-(sc * resid_two)).astype(bf16)

    need(6, 8)
    each("quantize", quantize)

    def halves_of_grad(phase, count, step):
        @pl.loop(0, 2 * count)
        def _(t):
            half = lax.rem(t + other, 2)
            step(t // 2, half, pl.ds(pl.multiple_of(half * HALF, HALF), HALF))
            after(phase, t)

    def book_grads(phase, l, back):
        def step(_, g, hc):
            code = lax.broadcasted_iota(jnp.int32, (CODES, MAXLEN), 0)
            onehot = jnp.concatenate(
                [
                    jnp.where(jnp.broadcast_to(slot(IDX[l, g, b]), (CODES, MAXLEN)) == code, 1.0, 0.0).astype(bf16)
                    for b in range(CLIPS)
                ],
                axis=1,
            )
            value = dot_nn(onehot, back[:, hc]).astype(bf16)
            G[g, 4 + 2 * l : 6 + 2 * l] = value.reshape(2, NZ, NY, NX, BLOCK, HALF)

        halves_of_grad(phase, 1, step)

    book_grads("book0", 0, B1)
    book_grads("book1", 1, B2)

    def decode(b, r0):
        rows = pl.ds(r0, MAXLEN)
        DEC[rows, :] = dot_nn(STR[rows, :], w(8, 9))
        for k in range(0, D, 128):
            value, slope = gelu_pair(DEC[rows, k : k + 128])
            value = value * MASK[rows, :]
            DGD[rows, k : k + 128] = slope * MASK[rows, :]
            S[rows, k : k + 128], S[rows, 2 * D + k : 2 * D + k + 128] = neighbours(value)
            value = value.astype(bf16)
            S[rows, D + k : D + k + 128] = value
            DINT[k : k + 128, rows] = value.T

    need(8, 9)
    each("decode", decode)

    def kernel_grad(phase, left, base):
        def step(k, half, _):
            put(half, base + k, dot_nn(left[...], O[:, pl.ds(pl.multiple_of(k * D + half * HALF, HALF), HALF)]))

        halves_of_grad(phase, KERNEL, step)

    kernel_grad("kg9", DINT, 9)

    def decode_back(b, r0):
        total = None
        for k in range(KERNEL):
            term = dot_nt(O[pl.ds(r0, MAXLEN), k * D : (k + 1) * D], w(9 + k, 10 + k))
            total = term if total is None else total + term
        back = O[pl.ds(r0, MAXLEN), D : 2 * D].astype(f32) + DGD[pl.ds(r0, MAXLEN), :] * total
        back = back.astype(bf16)
        DB[pl.ds(r0, MAXLEN), :] = back
        LB[pl.ds(r0, MAXLEN), :] = (dot_nt(back, w(8, 9)) + LAT[pl.ds(r0, MAXLEN), :]).astype(bf16)

    need(9, 12)
    each("decode_back", decode_back)

    def proj_grads(phase, left, right, group):
        def step(_, half, hc):
            put(half, group, dot_nn(left[...], right[:, hc]))

        halves_of_grad(phase, 1, step)

    proj_grads("pg8", STRT, DB, 8)

    def encode_back(b, r0):
        rows = pl.ds(r0, MAXLEN)
        DGD[rows, :] = dot_nt(LB[rows, :], w(3, 4)) * lanes(MASK[rows, :], 4)
        for k in range(0, D, 128):
            low = DGD[rows, k : k + 128].astype(bf16)
            O[rows, 2 * D + k : 2 * D + k + 128], O[rows, k : k + 128] = neighbours(low.astype(f32))
            O[rows, D + k : D + k + 128] = low

    each("encode_back", encode_back)
    proj_grads("pg3", ENCT, LB, 3)
    kernel_grad("kg0", AT, 0)

    def halves(phase, step):

        @pl.loop(0, 2 * CLIPS)
        def _(t):
            h = t % 2
            step(pl.multiple_of((t // 2) * MAXLEN, MAXLEN), h, pl.ds(pl.multiple_of(h * HALF, HALF), HALF))
            after(phase, t)

    def decoded_result(r0, h, hc):
        m = lanes(MASK[pl.ds(r0, MAXLEN), :], 2)
        kernel = W[9:12, :, :, :, :, hc].reshape(KERNEL * D, HALF)
        value = (DEC[pl.ds(r0, MAXLEN), hc] + dot_nn(S[pl.ds(r0, MAXLEN), :], kernel)) * m
        OB[pl.ds(r0, MAXLEN), hc] = value.astype(bf16)

    def input_back(r0, h, hc):
        m = lanes(MASK[pl.ds(r0, MAXLEN), :], 2)
        total = None
        for k in range(KERNEL):
            kernel = W[k, pl.ds(2 * h, 2)].reshape(HALF, D)
            term = dot_nt(O[pl.ds(r0, MAXLEN), k * D : (k + 1) * D], kernel)
            total = term if total is None else total + term
        slope = gelu_pair(FR[pl.ds(r0, MAXLEN), hc].astype(f32))[1]
        STR[pl.ds(r0, MAXLEN), hc] = (DGD[pl.ds(r0, MAXLEN), hc] + slope * m * total).astype(bf16)

    halves("decoded", decoded_result)
    out_own = pltpu.make_async_copy(OB.at[:, cols], out_hbm.at[mine, :], lsem.at[3])
    out_own.start()
    at_out = place()
    send(lambda: OB.at[:, cols_other], lambda: out_hbm.at[mine, :], dev_peer, at_out)
    halves("input", input_back)
    in_own = pltpu.make_async_copy(STR.at[:, cols], input_hbm.at[mine, :], lsem.at[4])
    in_own.start()
    at_in = place()
    send(lambda: STR.at[:, cols_other], lambda: input_hbm.at[mine, :], dev_peer, at_in)

    once("end")

    for q in range(len(sets)):
        arrived(NM.at[1, q], at_norm[q])
    COLSTAT[6:8, :] = jnp.zeros((2, HALF), f32)
    SCALARS[6:8, :] = jnp.zeros((2, 128), f32)
    SCALARS[8:16, :] = (NM[0, 0] + NM[1, 0]) + (NM[0, 1] + NM[1, 1])

    assert counter[0] <= SEMAPHORES

    arrived(out_hbm.at[theirs, :], at_out)
    arrived(input_hbm.at[theirs, :], at_in)
    out_own.wait()
    in_own.wait()
    for q, ((g0, g1), _, _) in enumerate(sets):
        pltpu.make_async_copy(GF.at[g0:g1], grads_hbm.at[g0:g1], lsem.at[5 + q]).wait()
        pltpu.make_async_copy(ROWSTAT.at[g0:g1], rows_hbm.at[g0:g1], lsem.at[7 + q]).wait()
    for src, at in unsent:
        remote(src(), src(), dev_peer, at).wait_send()


def final_kernel(
    decoded_hbm,
    back_hbm,
    grads_hbm,
    rows_hbm,
    colstat_hbm,
    scalars_hbm,
    conv_hbm,
    proj_hbm,
    books_hbm,
    out_hbm,
    input_hbm,
    conv_grad,
    proj_grad,
    book_grad,
    conv_rows_out,
    conv_cols_out,
    proj_rows_out,
    proj_cols_out,
    book_rows_out,
    book_cols_out,
    conv_new,
    proj_new,
    book_new,
    buffer,
    grads,
    rowstat,
    colstat,
    scalars,
    conv_weight,
    proj_weight,
    codebooks,
    conv_next,
    proj_next,
    books_next,
    sem,
):
    used = [0]

    def copy(src, dst):
        used[0] += 1
        made = pltpu.make_async_copy(src, dst, sem.at[used[0] - 1])
        made.start()
        return made

    small = [
        copy(src, dst)
        for src, dst in (
            (scalars_hbm, scalars),
            (colstat_hbm, colstat),
            (rows_hbm, rowstat),
            (grads_hbm, grads),
            (conv_hbm, conv_weight),
            (proj_hbm, proj_weight),
            (books_hbm, codebooks),
        )
    ]
    chunks = 2
    rows = decoded_hbm.shape[0] // chunks
    loads, stores = [], []
    for i, (src, dst) in enumerate(((decoded_hbm, out_hbm), (back_hbm, input_hbm))):
        for k in range(chunks):
            at = pl.ds(k * rows, rows)
            loads.append((copy(src.at[at, :], buffer.at[i, at, :]), buffer.at[i, at, :], dst.at[at, :]))
    for load in small:
        load.wait()
    for i in range(2):
        stores.append(copy(grads.at[9 * i : 9 * i + 3], conv_grad.at[i]))
        stores.append(copy(grads.at[3 + 5 * i], proj_grad.at[i]))
        for t in range(2):
            stores.append(copy(grads.at[4 + 2 * i + t], book_grad.at[i, BLOCK * t : BLOCK * (t + 1)]))
    size = grads.shape[1] * NZ * NY * NX * D
    for i, (g0, g1) in enumerate(MATRICES):
        factor = jnp.maximum(1.0, jnp.sqrt(scalars[8 + i : 9 + i] / ((g1 - g0) * size)) / clip_level)
        total = lanes(scalars[i : i + 1], 2)
        rate = (2.0 / math.sqrt(KERNEL * D), 2.0 / math.sqrt(D), 2.0)[(0, 1, 2, 2, 1, 0)[i]]
        for g in range(g0, g1):
            update = grads[g] * lax.rsqrt(lanes(rowstat[g], 2) * colstat[i : i + 1] / total)
            step = rate * (update / lanes(factor, 2))
            row = rowstat[g].T[0:1]
            k = g - g0
            if i in (0, 5):
                conv_next[i // 5, k] = conv_weight[i // 5, k] - step
                conv_rows_out[k, i // 5 : i // 5 + 1] = row
            elif i in (1, 4):
                proj_next[i // 4] = proj_weight[i // 4] - step
                proj_rows_out[i // 4 : i // 4 + 1] = row
            else:
                part = slice(BLOCK * k, BLOCK * (k + 1))
                books_next[i - 2, part] = codebooks[i - 2, part] - step
                book_rows_out[i - 2 : i - 1, part] = row
    conv_cols_out[0:1] = colstat[0:1]
    conv_cols_out[1:2] = colstat[5:6]
    proj_cols_out[0:1] = colstat[1:2]
    proj_cols_out[1:2] = colstat[4:5]
    book_cols_out[...] = colstat[2:4]
    stores.append(copy(conv_next, conv_new))
    stores.append(copy(proj_next, proj_new))
    stores.append(copy(books_next, book_new))
    for load, src, dst in loads:
        load.wait()
        stores.append(copy(src, dst))
    for store in stores:
        store.wait()


def fused_body(
    frames,
    cotangent,
    lengths,
    frame_mask,
    code_index,
    conv_weight,
    proj_weight,
    codebooks,
    conv_rows,
    conv_cols,
    proj_rows,
    proj_cols,
    book_rows,
    book_cols,
):
    vmem = pl.BlockSpec(memory_space=pltpu.VMEM)
    hbm = pl.BlockSpec(memory_space=pl.ANY)
    shape = jax.ShapeDtypeStruct
    quad = (NZ, NY, NX, BLOCK)
    part = pl.pallas_call(
        fused_kernel,
        out_shape=(
            shape(cotangent.shape, bf16),
            shape(cotangent.shape, bf16),
            shape((GROUPS12, BLOCK, HALF), f32),
            shape((GROUPS12, BLOCK, 128), f32),
            shape((8, HALF), f32),
            shape((16, 128), f32),
        ),
        in_specs=[pl.BlockSpec(memory_space=pltpu.SMEM)] + [hbm] * 6 + [vmem] * 7,
        out_specs=(hbm,) * 4 + (vmem,) * 2,
        scratch_shapes=[
            pltpu.VMEM((GROUPS12,) + quad + (D,), bf16),
            pltpu.VMEM((2, GROUPS12) + quad + (HALF,), bf16),
            pltpu.VMEM((GROUPS12,) + quad + (HALF,), bf16),
            pltpu.VMEM((GROUPS12, NZ, NY, BLOCK, 128), bf16),
            pltpu.VMEM((GROUPS12, NZ, NX, BLOCK, 128), bf16),
            pltpu.VMEM((GROUPS12, NZ, BLOCK, 128), bf16),
            pltpu.VMEM((GROUPS12, NZ, BLOCK, 128), bf16),
            pltpu.VMEM((GROUPS12, NZ, BLOCK, 128), bf16),
            pltpu.VMEM((GROUPS12, NZ, BLOCK, 128), bf16),
            pltpu.VMEM((GROUPS12, NZ, BLOCK, HALF), bf16),
            pltpu.VMEM((NZ - 1, GROUPS12, BLOCK, HALF), bf16),
            pltpu.VMEM((ROWS, D), bf16),
            pltpu.VMEM((ROWS, 3 * D), bf16),
            pltpu.VMEM((ROWS, 3 * D), bf16),
            pltpu.VMEM((D, ROWS), bf16),
            pltpu.VMEM((D, ROWS), bf16),
            pltpu.VMEM((D, ROWS), bf16),
            pltpu.VMEM((D, ROWS), bf16),
            pltpu.VMEM((ROWS, D), f32),
            pltpu.VMEM((ROWS, D), f32),
            pltpu.VMEM((ROWS, D), f32),
            pltpu.VMEM((ROWS, D), bf16),
            pltpu.VMEM((ROWS, D), bf16),
            pltpu.VMEM((ROWS, D), bf16),
            pltpu.VMEM((ROWS, D), bf16),
            pltpu.VMEM((ROWS, D), bf16),
            pltpu.VMEM((ROWS, D), bf16),
            pltpu.VMEM((NZ - 1, PLANES, NY, NX, BLOCK, HALF), bf16),
            pltpu.VMEM((PLANES, NY, NX, BLOCK, HALF), bf16),
            pltpu.VMEM((PLANES, NY, BLOCK, 128), bf16),
            pltpu.VMEM((PLANES, NX, BLOCK, 128), bf16),
            pltpu.VMEM((2, PLANES, BLOCK, 128), bf16),
            pltpu.VMEM((2, PLANES, BLOCK, 128), bf16),
            pltpu.VMEM(conv_weight.shape, f32),
            pltpu.VMEM(proj_weight.shape, f32),
            pltpu.VMEM(codebooks.shape, f32),
            pltpu.VMEM((ROWS, 128), f32),
            pltpu.VMEM((2, 2, CLIPS, 1, MAXLEN), jnp.int32),
            pltpu.VMEM((8, 8, 128), f32),
            pltpu.VMEM((GROUPS12, BLOCK, HALF), f32),
            pltpu.VMEM((GROUPS12, BLOCK, 128), f32),
            pltpu.VMEM((8, 16, HALF), f32),
            pltpu.VMEM((8, 8, HALF), f32),
            pltpu.VMEM((2, 2, 8, 128), f32),
            pltpu.VMEM((2, GROUPS12, BLOCK, 128), f32),
            pltpu.SemaphoreType.DMA((SEMAPHORES,)),
            pltpu.SemaphoreType.DMA((SEMAPHORES,)),
            pltpu.SemaphoreType.DMA((16,)),
        ],
        compiler_params=pltpu.CompilerParams(
            collective_id=0, has_side_effects=True, vmem_limit_bytes=63 * 2**20
        ),
        name="step",
    )(
        lengths,
        frames,
        cotangent,
        code_index.reshape(2, 2, CLIPS, 1, MAXLEN),
        conv_weight,
        proj_weight,
        codebooks,
        frame_mask.reshape(2, CLIPS, 1, MAXLEN),
        jnp.swapaxes(conv_rows, 0, 1),
        proj_rows,
        book_rows,
        conv_cols,
        proj_cols,
        book_cols,
    )
    out = pl.pallas_call(
        final_kernel,
        out_shape=(
            shape(cotangent.shape, bf16),
            shape(cotangent.shape, bf16),
            shape(conv_weight.shape, f32),
            shape(proj_weight.shape, f32),
            shape(codebooks.shape, f32),
            shape((KERNEL, 2, BLOCK), f32),
            shape(conv_cols.shape, f32),
            shape(proj_rows.shape, f32),
            shape(proj_cols.shape, f32),
            shape(book_rows.shape, f32),
            shape(book_cols.shape, f32),
            shape(conv_weight.shape, f32),
            shape(proj_weight.shape, f32),
            shape(codebooks.shape, f32),
        ),
        in_specs=[hbm] * 9,
        out_specs=(hbm,) * 5 + (vmem,) * 6 + (hbm,) * 3,
        scratch_shapes=[
            pltpu.VMEM((2,) + cotangent.shape, bf16),
            pltpu.VMEM((GROUPS12, BLOCK, HALF), f32),
            pltpu.VMEM((GROUPS12, BLOCK, 128), f32),
            pltpu.VMEM((8, HALF), f32),
            pltpu.VMEM((16, 128), f32),
            pltpu.VMEM(conv_weight.shape, f32),
            pltpu.VMEM(proj_weight.shape, f32),
            pltpu.VMEM(codebooks.shape, f32),
            pltpu.VMEM(conv_weight.shape, f32),
            pltpu.VMEM(proj_weight.shape, f32),
            pltpu.VMEM(codebooks.shape, f32),
            pltpu.SemaphoreType.DMA((32,)),
        ],
        compiler_params=pltpu.CompilerParams(vmem_limit_bytes=63 * 2**20),
        name="final",
    )(*part, conv_weight, proj_weight, codebooks)
    return out[:5] + (jnp.swapaxes(out[5], 0, 1),) + out[6:]


def solution(mesh):
    placed = (
        P("dp", None),
        P("dp", "chan"),
        P("dp"),
        P("dp"),
        P(None, "dp", "chan"),
        P(None, None, "dp", "chan"),
        P(None, "dp", "chan"),
        P(None, "dp", "chan"),
        P(None, None, "dp"),
        P(None, "chan"),
        P(None, "dp"),
        P(None, "chan"),
        P(None, "dp"),
        P(None, "chan"),
    )
    fits = mesh.shape["dp"] == NZ * NY * NX and mesh.shape["chan"] == 2
    return jax.shard_map(
        fused_body if fits else general_body,
        mesh=mesh,
        in_specs=placed,
        out_specs=(
            P("dp", "chan"),
            P("dp", "chan"),
            P(None, None, "dp", "chan"),
            P(None, "dp", "chan"),
            P(None, "dp", "chan"),
            P(None, None, "dp"),
            P(None, "chan"),
            P(None, "dp"),
            P(None, "chan"),
            P(None, "dp"),
            P(None, "chan"),
            P(None, None, "dp", "chan"),
            P(None, "dp", "chan"),
            P(None, "dp", "chan"),
        ),
        check_vma=False,
    )
```

```python
import functools
import math

import jax
import jax.numpy as jnp
from jax import lax
from jax.experimental import pallas as pl
from jax.experimental.pallas import tpu as pltpu
from jax.sharding import PartitionSpec as P

D = 512
CODES = 1024
KERNEL = 3
STEP = 10
MAXLEN = 512
MICRO = 2


square_floor = 1e-30
clip_level = 0.5
f32 = jnp.float32
bf16 = jnp.bfloat16


def shifted(signal, length):
    channels = signal.shape[-1]
    blocks = signal.reshape(-1, length, channels)
    padded = jnp.pad(blocks, ((0, 0), (1, 1), (0, 0)))
    joined = jnp.concatenate(
        [padded[:, 0:length], padded[:, 1 : length + 1], padded[:, 2 : length + 2]], axis=2
    )
    return joined.reshape(-1, 3 * channels)


def unshift(partial_terms, length):
    channels = partial_terms.shape[-1] // 3
    blocks = partial_terms.reshape(-1, length, 3, channels)
    padded = jnp.pad(blocks, ((0, 0), (1, 1), (0, 0), (0, 0)))
    summed = padded[:, 2 : length + 2, 0] + padded[:, 1 : length + 1, 1] + padded[:, 0:length, 2]
    return summed.reshape(-1, channels)


def gelu_back(values, upstream):
    return jax.vjp(jax.nn.gelu, values)[1](upstream)[0]


def fetch(conv_weight, proj_weight, codebooks):
    return (
        lax.all_gather(conv_weight.astype(bf16), "dp", axis=2, tiled=True),
        lax.all_gather(proj_weight.astype(bf16), "dp", axis=1, tiled=True),
        lax.all_gather(codebooks.astype(bf16), "dp", axis=1, tiled=True),
    )


def reduce_grads(conv_total, proj_total, book_total):
    return (
        lax.psum_scatter(conv_total, "dp", scatter_dimension=2, tiled=True),
        lax.psum_scatter(proj_total, "dp", scatter_dimension=1, tiled=True),
        lax.psum_scatter(book_total, "dp", scatter_dimension=1, tiled=True),
    )


def contract(left, right):
    return jnp.einsum("fc,fd->cd", left, right, preferred_element_type=f32)


def transpose_product(left, right):
    return jnp.einsum("fd,cd->fc", left, right, preferred_element_type=f32)


def general_body(
    frames,
    cotangent,
    lengths,
    frame_mask,
    code_index,
    conv_weight,
    proj_weight,
    codebooks,
    conv_rows,
    conv_cols,
    proj_rows,
    proj_cols,
    book_rows,
    book_cols,
):
    length = MAXLEN
    block_rows = frames.shape[0] // MICRO
    half_width = cotangent.shape[1]
    chan_place = lax.axis_index("chan")
    row_place = jnp.arange(frames.shape[0], dtype=jnp.int32) % length
    live = (row_place < jnp.repeat(lengths, length, total_repeat_length=frames.shape[0])) & (
        frame_mask > 0
    )
    weight_mask = live.astype(f32)[:, None]
    live_total = lax.psum(jnp.sum(weight_mask), "dp")
    vq_scale = 2.0 / live_total
    running = None
    out_pieces = []
    grad_pieces = []
    for block_number in range(MICRO):
        first_row = block_number * block_rows
        last_row = first_row + block_rows
        conv_bank, proj_bank, book_bank = fetch(conv_weight, proj_weight, codebooks)
        conv_enc = conv_bank[0].reshape(-1, half_width)
        conv_dec = conv_bank[1].reshape(-1, half_width)
        frame_part = frames[first_row:last_row]
        frame_wide = frame_part.astype(f32)
        own_part = lax.dynamic_slice_in_dim(frame_wide, chan_place * half_width, half_width, 1)
        masked = weight_mask[first_row:last_row]
        cot_part = jnp.where(masked > 0, cotangent[first_row:last_row], jnp.zeros((), bf16))
        code_range = jnp.arange(book_bank.shape[1], dtype=jnp.int32)
        onehot_one = (code_index[0, first_row:last_row, 0][:, None] == code_range[None, :]).astype(
            bf16
        )
        onehot_two = (code_index[1, first_row:last_row, 0][:, None] == code_range[None, :]).astype(
            bf16
        )
        activated = (jax.nn.gelu(frame_wide) * masked).astype(bf16)
        stack_one = shifted(activated, length)
        branch = jnp.dot(stack_one, conv_enc, preferred_element_type=f32)
        encoded = (own_part + branch) * masked
        enc_full = lax.all_gather(encoded.astype(bf16), "chan", axis=1, tiled=True)
        latent = jnp.dot(enc_full, proj_bank[0], preferred_element_type=f32)
        level_one = jnp.dot(onehot_one, book_bank[0], preferred_element_type=f32)
        level_two = jnp.dot(onehot_two, book_bank[1], preferred_element_type=f32)
        quantized = level_one + level_two
        straight = (latent + (quantized - latent)).astype(bf16)
        straight_full = lax.all_gather(straight, "chan", axis=1, tiled=True)
        decoded = jnp.dot(straight_full, proj_bank[1], preferred_element_type=f32)
        decoder_in = (jax.nn.gelu(decoded) * masked).astype(bf16)
        decoder_full = lax.all_gather(decoder_in, "chan", axis=1, tiled=True)
        stack_two = shifted(decoder_full, length)
        result = (decoded + jnp.dot(stack_two, conv_dec, preferred_element_type=f32)) * masked
        out_pieces.append(result.astype(bf16))
        conv_dec_grad = contract(stack_two, cot_part)
        in_partial = unshift(transpose_product(cot_part, conv_dec), length)
        in_back = lax.psum_scatter(in_partial, "chan", scatter_dimension=1, tiled=True)
        decoded_back = (cot_part.astype(f32) + gelu_back(decoded, masked * in_back)).astype(bf16)
        proj_dec_grad = contract(straight_full, decoded_back)
        straight_back = lax.psum_scatter(
            transpose_product(decoded_back, proj_bank[1]), "chan", scatter_dimension=1, tiled=True
        )
        resid_one = latent - level_one
        resid_two = resid_one - level_two
        pulled = vq_scale * masked * (resid_one + resid_two)
        latent_back = (straight_back + pulled).astype(bf16)
        one_back = (-pulled).astype(bf16)
        two_back = (-(vq_scale * masked * resid_two)).astype(bf16)
        book_one_grad = contract(onehot_one, one_back)
        book_two_grad = contract(onehot_two, two_back)
        proj_enc_grad = contract(enc_full, latent_back)
        encoded_back = lax.psum_scatter(
            transpose_product(latent_back, proj_bank[0]), "chan", scatter_dimension=1, tiled=True
        )
        branch_back = (encoded_back * masked).astype(bf16)
        conv_enc_grad = contract(stack_one, branch_back)
        activated_back = unshift(transpose_product(branch_back, conv_enc), length)
        input_partial = gelu_back(frame_wide, masked * activated_back)
        input_own = lax.psum_scatter(input_partial, "chan", scatter_dimension=1, tiled=True)
        grad_pieces.append((encoded_back * masked + input_own).astype(bf16))
        conv_blockgrad = jnp.stack(
            [
                conv_enc_grad.reshape(KERNEL, -1, half_width),
                conv_dec_grad.reshape(KERNEL, -1, half_width),
            ]
        )
        proj_blockgrad = jnp.stack([proj_enc_grad, proj_dec_grad])
        book_blockgrad = jnp.stack([book_one_grad, book_two_grad])
        reduced = reduce_grads(conv_blockgrad, proj_blockgrad, book_blockgrad)
        running = (
            reduced
            if running is None
            else (running[0] + reduced[0], running[1] + reduced[1], running[2] + reduced[2])
        )
    conv_grad, proj_grad, book_grad = running
    decoded_out = jnp.concatenate(out_pieces, axis=0)
    input_grad = jnp.concatenate(grad_pieces, axis=0)
    beta_two = 1.0 - STEP ** (-0.8)
    squares_conv = conv_grad * conv_grad + square_floor
    squares_proj = proj_grad * proj_grad + square_floor
    squares_book = book_grad * book_grad + square_floor
    row_sums = lax.psum(
        (
            jnp.sum(squares_conv, axis=3),
            jnp.sum(squares_proj, axis=2),
            jnp.sum(squares_book, axis=2),
        ),
        "chan",
    )
    rowstat_conv = beta_two * conv_rows + (1.0 - beta_two) * row_sums[0]
    rowstat_proj = beta_two * proj_rows + (1.0 - beta_two) * row_sums[1]
    rowstat_book = beta_two * book_rows + (1.0 - beta_two) * row_sums[2]
    col_sums = lax.psum(
        (
            jnp.sum(squares_conv, axis=(1, 2)),
            jnp.sum(squares_proj, axis=1),
            jnp.sum(squares_book, axis=1),
            jnp.sum(rowstat_conv, axis=(1, 2)),
            jnp.sum(rowstat_proj, axis=1),
            jnp.sum(rowstat_book, axis=1),
        ),
        "dp",
    )
    colstat_conv = beta_two * conv_cols + (1.0 - beta_two) * col_sums[0]
    colstat_proj = beta_two * proj_cols + (1.0 - beta_two) * col_sums[1]
    colstat_book = beta_two * book_cols + (1.0 - beta_two) * col_sums[2]
    update_conv = conv_grad * lax.rsqrt(
        rowstat_conv[..., None] * colstat_conv[:, None, None, :] / col_sums[3][:, None, None, None]
    )
    update_proj = proj_grad * lax.rsqrt(
        rowstat_proj[..., None] * colstat_proj[:, None, :] / col_sums[4][:, None, None]
    )
    update_book = book_grad * lax.rsqrt(
        rowstat_book[..., None] * colstat_book[:, None, :] / col_sums[5][:, None, None]
    )
    norm_sums = lax.psum(
        (
            jnp.sum(update_conv * update_conv, axis=(1, 2, 3)),
            jnp.sum(update_proj * update_proj, axis=(1, 2)),
            jnp.sum(update_book * update_book, axis=(1, 2)),
        ),
        ("dp", "chan"),
    )
    factor_conv = jnp.maximum(1.0, jnp.sqrt(norm_sums[0] / (KERNEL * D * D)) / clip_level)
    factor_proj = jnp.maximum(1.0, jnp.sqrt(norm_sums[1] / (D * D)) / clip_level)
    factor_book = jnp.maximum(1.0, jnp.sqrt(norm_sums[2] / (CODES * D)) / clip_level)
    rate_conv = 2.0 / math.sqrt(KERNEL * D)
    rate_proj = 2.0 / math.sqrt(D)
    updated_conv = conv_weight - rate_conv * (update_conv / factor_conv[:, None, None, None])
    updated_proj = proj_weight - rate_proj * (update_proj / factor_proj[:, None, None])
    updated_book = codebooks - 2.0 * (update_book / factor_book[:, None, None])
    return (
        decoded_out,
        input_grad,
        conv_grad,
        proj_grad,
        book_grad,
        rowstat_conv,
        colstat_conv,
        rowstat_proj,
        colstat_proj,
        rowstat_book,
        colstat_book,
        updated_conv,
        updated_proj,
        updated_book,
    )


MESH = pl.DeviceIdType.MESH
CLIPS = 3
ROWS = CLIPS * MAXLEN
GROUPS12 = 12
NZ, NY, NX = 4, 2, 2
BLOCK = 32
SEMAPHORES = 256
HALF = 256
GELU_A = math.sqrt(2.0 / math.pi)
GELU_B = 0.044715
MATRICES = ((0, 3), (3, 4), (4, 6), (6, 8), (8, 9), (9, 12))


def gelu_pair(x):
    x2 = x * x
    t = jnp.tanh(x * (GELU_A + GELU_A * GELU_B * x2))
    half = 0.5 + 0.5 * t
    value = x * half
    return value, half + value * (1.0 - t) * (GELU_A + 3.0 * GELU_A * GELU_B * x2)


def lanes(m, n):
    return jnp.concatenate([m] * n, axis=1)


def dot_nn(a, b):
    return jnp.dot(a, b, preferred_element_type=f32)


def dot_nt(a, b):
    return lax.dot_general(a, b, (((1,), (1,)), ((), ())), preferred_element_type=f32)


def neighbours(v):
    rows = v.shape[0]
    row = lax.broadcasted_iota(jnp.int32, (8, v.shape[1]), 0)
    before, after = pltpu.roll(v, 1, 0), pltpu.roll(v, rows - 1, 0)
    before = jnp.concatenate([jnp.where(row == 0, 0.0, before[:8]), before[8:]], axis=0)
    after = jnp.concatenate([after[:-8], jnp.where(row == 7, 0.0, after[-8:])], axis=0)
    return before.astype(bf16), after.astype(bf16)


PIECES = ((0, 1, "f"), (1, 2, "f"), (2, 3, "f"), (3, 4, "f"), (4, 6, "f"), (6, 8, "f"), (8, 9, "f"), (9, 11, "f"), (11, 12, "f"))
PARTS = ((4, 6, "f"), (6, 8, "f"), (9, 10, "f"), (10, 12, "f"), (8, 9, "l"), (3, 4, "f"), (0, 1, "f"), (1, 2, "f"), (2, 3, "f"))
PLANES = max(1, sum((g1 - g0) * (kind == "l") for g0, g1, kind in PARTS))
SCHEDULE = {
    "start": {
        0: (("z", 0), ("z", 1), ("z", 2), ("z", 3), ("z", 4), ("z", 5), ("z", 7), ("z", 6),),
    },
    "upstream": {
        1: (("l", 0),),
        2: (("l", 1), ("l", 2), ("d", 0), ("d", 1), ("l", 3), ("d", 2), ("l", 4), ("q", 0), ("q", 1), ("l", 5), ("d", 3), ("q", 2),),
    },
    "encode": {
        1: (("d", 4),),
        2: (("d", 5), ("l", 7), ("l", 6), ("z", 8), ("q", 3),),
    },
    "project": {
        1: (("q", 4),),
        2: (("q", 5), ("l", 8),),
    },
    "quantize": {
        2: (("d", 6),),
    },
    "book0": {
        0: (("d", 8), ("d", 7),),
        1: (("P", 0),),
    },
    "book1": {
        0: (("q", 6),),
        1: (("q", 8), ("P", 1), ("A", 0),),
    },
    "decode": {
        0: (("q", 7),),
        2: (("A", 1),),
    },
    "kg9": {
        1: (("P", 2),),
        3: (("B", 0),),
        4: (("A", 2),),
        5: (("P", 3),),
    },
    "decode_back": {
        0: (("B", 1),),
        1: (("A", 3), ("Z", 0),),
        2: (("B", 2),),
    },
    "pg8": {
        1: (("Z", 1), ("P", 4),),
    },
    "pg3": {
        0: (("U", 4),),
        1: (("B", 3), ("P", 5), ("E", 0),),
    },
    "kg0": {
        0: (("Z", 2),),
        1: (("P", 6),),
        2: (("A", 5),),
        3: (("P", 7), ("E", 1),),
        4: (("A", 6),),
        5: (("Z", 3), ("P", 8),),
    },
    "decoded": {
        0: (("A", 7),),
        2: (("B", 5), ("A", 8),),
        5: (("B", 6), ("V", 4),),
    },
    "input": {
        1: (("B", 7), ("Z", 5), ("E", 2),),
        3: (("B", 8),),
        4: (("Z", 6), ("E", 3), ("X", 4),),
        5: (("Z", 7),),
    },
    "end": {
        0: (("Z", 8), ("F", 4), ("R", 0), ("E", 6), ("S", 0), ("E", 5), ("E", 7), ("E", 8), ("R", 1), ("S", 1), ("T", 0), ("T", 1), ("N", 0), ("N", 1),),
    },
}


def fused_kernel(
    lengths_hbm,
    frames_hbm,
    cot_hbm,
    index_hbm,
    conv_hbm,
    proj_hbm,
    books_hbm,
    mask_hbm,
    conv_rows_hbm,
    proj_rows_hbm,
    book_rows_hbm,
    conv_cols_hbm,
    proj_cols_hbm,
    book_cols_hbm,
    out_hbm,
    input_hbm,
    conv_grad,
    proj_grad,
    book_grad,
    conv_rows_out,
    conv_cols_out,
    proj_rows_out,
    proj_cols_out,
    book_rows_out,
    book_cols_out,
    conv_new,
    proj_new,
    book_new,
    W,
    G,
    RP,
    AX,
    AY,
    BX,
    BY,
    BXS,
    BYS,
    TS,
    ZR,
    FR,
    S,
    O,
    AT,
    ENCT,
    STRT,
    DINT,
    DEC,
    DGD,
    B1,
    B2,
    STR,
    OB,
    ZQ,
    PS,
    QX,
    QY,
    QS,
    QB,
    conv_weight,
    proj_weight,
    codebooks,
    lengths,
    frame_mask,
    conv_rows,
    proj_rows,
    book_rows,
    conv_cols,
    proj_cols,
    book_cols,
    OLD,
    MASK,
    IDX,
    CN,
    GF,
    ROWSTAT,
    STA,
    STB,
    RSUM,
    ssem,
    rsem,
    lsem,
):
    DB, LB = OB, B1
    me = lax.axis_index("dp")
    c = lax.axis_index("chan")
    z, y, x = me // (NY * NX), (me // NX) % NY, me % NX
    far_y, far_x, other = 1 - y, 1 - x, 1 - c

    def dp_of(zz, yy, xx):
        return (zz * (NY * NX) + yy * NX + xx, c)

    dev_x, dev_y, dev_diagonal = dp_of(z, y, far_x), dp_of(z, far_y, x), dp_of(z, far_y, far_x)
    dev_z = [dp_of(lax.rem(z + k, NZ), y, x) for k in range(1, NZ)]
    dev_peer = (me, other)
    to_z = [lax.rem(z + k, NZ) for k in range(1, NZ)]
    from_z = [lax.rem(z + NZ - k, NZ) for k in range(1, NZ)]
    cols = pl.ds(pl.multiple_of(c * HALF, HALF), HALF)
    cols_other = pl.ds(pl.multiple_of(other * HALF, HALF), HALF)
    quarter = (
        pl.ds(pl.multiple_of(c * HALF, HALF), 128),
        pl.ds(pl.multiple_of(c * HALF + 128, 128), 128),
    )
    mine = pl.ds(pl.multiple_of(c * ROWS, ROWS), ROWS)
    theirs = pl.ds(pl.multiple_of(other * ROWS, ROWS), ROWS)

    counter = [0]
    unsent = []

    def place(n=1):
        counter[0] += n
        return counter[0] - n

    def remote(src, dst, dev, at):
        return pltpu.make_async_remote_copy(
            src_ref=src,
            dst_ref=dst,
            send_sem=ssem.at[at],
            recv_sem=rsem.at[at],
            device_id=dev,
            device_id_type=MESH,
        )

    def send(src, dst, dev, at):
        remote(src(), dst(), dev, at).start()
        unsent.append((src, at))

    def arrived(dst, at):
        remote(dst, dst, dev_peer, at).wait_recv()

    barrier = pltpu.get_barrier_semaphore()
    partners = [dev_x, dev_y, dev_diagonal, dev_peer] + dev_z + [(dev[0], other) for dev in dev_z]
    for dev in partners:
        pl.semaphore_signal(barrier, inc=1, device_id=dev, device_id_type=MESH)
    weights_in = [
        pltpu.make_async_copy(src, dst, lsem.at[9 + i])
        for i, (src, dst) in enumerate(((conv_hbm, conv_weight), (proj_hbm, proj_weight), (books_hbm, codebooks)))
    ]
    for load in weights_in:
        load.start()
    index_in = pltpu.make_async_copy(index_hbm.at[:, c], IDX.at[:, c], lsem.at[2])
    index_in.start()
    frames_in = pltpu.make_async_copy(frames_hbm.at[mine, :], FR, lsem.at[0])
    frames_in.start()
    cot_in = pltpu.make_async_copy(cot_hbm.at[mine, :], OB.at[:, cols], lsem.at[1])
    cot_in.start()
    small_in = [
        pltpu.make_async_copy(src, dst, lsem.at[16 + i])
        for i, (src, dst) in enumerate(
            (
                (lengths_hbm, lengths),
                (mask_hbm, frame_mask),
                (conv_rows_hbm, conv_rows),
                (proj_rows_hbm, proj_rows),
                (book_rows_hbm, book_rows),
                (conv_cols_hbm, conv_cols.at[c]),
                (proj_cols_hbm, proj_cols.at[c]),
                (book_cols_hbm, book_cols.at[c]),
            )
        )
    ]
    for load in small_in:
        load.start()
    for load in weights_in:
        load.wait()

    for k in range(3):
        W[k, z, y, x, :, cols] = conv_weight[0, k].astype(bf16)
        W[9 + k, z, y, x, :, cols] = conv_weight[1, k].astype(bf16)
    W[3, z, y, x, :, cols] = proj_weight[0].astype(bf16)
    W[8, z, y, x, :, cols] = proj_weight[1].astype(bf16)
    for level in range(2):
        for t in range(2):
            W[4 + 2 * level + t, z, y, x, :, cols] = codebooks[level, BLOCK * t : BLOCK * (t + 1)].astype(bf16)
    pl.semaphore_wait(barrier, len(partners))

    pieces = PIECES
    at_z = [place(3) for p in pieces]
    at_l = [place(2) for p in pieces]
    at_d = [place(2) for p in pieces]
    at_p = [place(2) for p in pieces]
    at_cot, at_idx, at_count = place(), place(), place(6)

    def gather_z(p):
        g0, g1 = pieces[p][:2]
        for k in range(NZ - 1):
            own = lambda: W.at[g0:g1, z, y, x, :, cols]
            send(own, own, dev_z[k], at_z[p] + k)

    def gather_line(p):
        g0, g1 = pieces[p][:2]
        for k in range(NZ - 1):
            arrived(W.at[g0:g1, from_z[k], y, x, :, cols], at_z[p] + k)
        line = lambda: W.at[g0:g1, :, y, x, :, cols]
        send(line, line, dev_x, at_l[p])
        send(line, line, dev_y, at_l[p] + 1)

    def gather_diagonal(p):
        g0, g1 = pieces[p][:2]
        arrived(W.at[g0:g1, :, y, far_x, :, cols], at_l[p])
        arrived(W.at[g0:g1, :, far_y, x, :, cols], at_l[p] + 1)
        part_y = lambda: W.at[g0:g1, :, far_y, x, :, quarter[0]]
        send(part_y, part_y, dev_x, at_d[p])
        part_x = lambda: W.at[g0:g1, :, y, far_x, :, quarter[1]]
        send(part_x, part_x, dev_y, at_d[p] + 1)
        near = lambda: W.at[g0:g1, :, y, :, :, cols]
        send(near, near, dev_peer, at_p[p])

    def gather_peer(p):
        g0, g1 = pieces[p][:2]
        arrived(W.at[g0:g1, :, far_y, far_x, :, quarter[0]], at_d[p])
        arrived(W.at[g0:g1, :, far_y, far_x, :, quarter[1]], at_d[p] + 1)
        far = lambda: W.at[g0:g1, :, far_y, :, :, cols]
        send(far, far, dev_peer, at_p[p] + 1)

    def plane_own(p):
        g0, g1 = pieces[p][:2]
        own = lambda: W.at[g0:g1, z, y, x, :, cols]
        send(own, own, dev_x, at_l[p])
        send(own, own, dev_y, at_l[p] + 1)

    def plane_diagonal(p):
        g0, g1 = pieces[p][:2]
        arrived(W.at[g0:g1, z, y, far_x, :, cols], at_l[p])
        arrived(W.at[g0:g1, z, far_y, x, :, cols], at_l[p] + 1)
        part_y = lambda: W.at[g0:g1, z, far_y, x, :, quarter[0]]
        send(part_y, part_y, dev_x, at_d[p])
        part_x = lambda: W.at[g0:g1, z, y, far_x, :, quarter[1]]
        send(part_x, part_x, dev_y, at_d[p] + 1)

    def plane_line(p):
        g0, g1 = pieces[p][:2]
        arrived(W.at[g0:g1, z, far_y, far_x, :, quarter[0]], at_d[p])
        arrived(W.at[g0:g1, z, far_y, far_x, :, quarter[1]], at_d[p] + 1)
        plane = lambda: W.at[g0:g1, z, :, :, :, cols]
        for k in range(NZ - 1):
            send(plane, plane, dev_z[k], at_z[p] + k)

    def plane_peer(p):
        g0, g1 = pieces[p][:2]
        for k in range(NZ - 1):
            arrived(W.at[g0:g1, from_z[k], :, :, :, cols], at_z[p] + k)
        whole = lambda: W.at[g0:g1, :, :, :, :, cols]
        send(whole, whole, dev_peer, at_p[p])

    def gathered(p):
        g0, g1 = pieces[p][:2]
        if pieces[p][2] == "l":
            arrived(W.at[g0:g1, :, :, :, :, cols_other], at_p[p])
            return
        arrived(W.at[g0:g1, :, y, :, :, cols_other], at_p[p])
        arrived(W.at[g0:g1, :, far_y, :, :, cols_other], at_p[p] + 1)

    parts = PARTS
    local, planes = [], 0
    for g0, g1, kind in parts:
        local.append(planes)
        planes += (g1 - g0) * (kind == "l")
    at_rp = [place() for p in parts]
    at_ra = [place(2) for p in parts]
    at_rb = [place(2) for p in parts]
    at_rz = [place(3) for p in parts]

    def reduce_peer(p):
        g0, g1 = parts[p][:2]
        send(lambda: G.at[other, g0:g1], lambda: RP.at[g0:g1], dev_peer, at_rp[p])

    def reduce_a(p):
        g0, g1 = parts[p][:2]
        arrived(RP.at[g0:g1], at_rp[p])

        @pl.loop(g0, g1)
        def _(g):
            G[c, g] = (G[c, g].astype(f32) + RP[g].astype(f32)).astype(bf16)

        send(lambda: G.at[c, g0:g1, :, :, far_x, :, 0:128], lambda: AX.at[g0:g1], dev_x, at_ra[p])
        send(lambda: G.at[c, g0:g1, :, far_y, :, :, 128:256], lambda: AY.at[g0:g1], dev_y, at_ra[p] + 1)

    def reduce_b(p):
        g0, g1 = parts[p][:2]
        arrived(AX.at[g0:g1], at_ra[p])
        arrived(AY.at[g0:g1], at_ra[p] + 1)

        @pl.loop(g0, g1)
        def _(g):
            BXS[g] = (G[c, g, :, y, far_x, :, 128:256].astype(f32) + AY[g, :, far_x].astype(f32)).astype(bf16)
            BYS[g] = (G[c, g, :, far_y, x, :, 0:128].astype(f32) + AX[g, :, far_y].astype(f32)).astype(bf16)

        send(lambda: BXS.at[g0:g1], lambda: BX.at[g0:g1], dev_x, at_rb[p])
        send(lambda: BYS.at[g0:g1], lambda: BY.at[g0:g1], dev_y, at_rb[p] + 1)

    def reduce_z(p):
        g0, g1 = parts[p][:2]
        arrived(BX.at[g0:g1], at_rb[p])
        arrived(BY.at[g0:g1], at_rb[p] + 1)

        @pl.loop(g0, g1)
        def _(g):
            base = G[c, g, :, y, x].astype(f32)
            left = base[:, :, 0:128] + (AX[g, :, y].astype(f32) + BY[g].astype(f32))
            right = base[:, :, 128:256] + (AY[g, :, x].astype(f32) + BX[g].astype(f32))
            TS[g, :, :, 0:128] = left.astype(bf16)
            TS[g, :, :, 128:256] = right.astype(bf16)

        for k in range(NZ - 1):
            send(
                lambda k=k: TS.at[g0:g1, to_z[k]],
                lambda k=k: ZR.at[k, g0:g1],
                dev_z[k],
                at_rz[p] + k,
            )

    def reduce_end(p):
        g0, g1 = parts[p][:2]
        for k in range(NZ - 1):
            arrived(ZR.at[k, g0:g1], at_rz[p] + k)

        @pl.loop(g0, g1)
        def _(g):
            GF[g] = (TS[g, z].astype(f32) + ZR[0, g].astype(f32)) + (ZR[1, g].astype(f32) + ZR[2, g].astype(f32))

    def plane_reduce(p):
        g0, g1 = parts[p][:2]
        arrived(RP.at[g0:g1], at_rp[p])

        @pl.loop(g0, g1)
        def _(g):
            G[c, g] = (G[c, g].astype(f32) + RP[g].astype(f32)).astype(bf16)

        for k in range(NZ - 1):
            send(
                lambda k=k: G.at[c, g0:g1, to_z[k]],
                lambda k=k: ZQ.at[k, local[p] : local[p] + g1 - g0],
                dev_z[k],
                at_rz[p] + k,
            )

    def plane_a(p):
        g0, g1 = parts[p][:2]
        i0, i1 = local[p], local[p] + g1 - g0
        for k in range(NZ - 1):
            arrived(ZQ.at[k, i0:i1], at_rz[p] + k)
        for i in range(i0, i1):
            total = G[c, g0 + i - i0, z].astype(f32) + ZQ[0, i].astype(f32)
            PS[i] = (total + (ZQ[1, i].astype(f32) + ZQ[2, i].astype(f32))).astype(bf16)
        send(lambda: PS.at[i0:i1, :, far_x, :, 0:128], lambda: QX.at[i0:i1], dev_x, at_ra[p])
        send(lambda: PS.at[i0:i1, far_y, :, :, 128:256], lambda: QY.at[i0:i1], dev_y, at_ra[p] + 1)

    def plane_b(p):
        g0, g1 = parts[p][:2]
        i0, i1 = local[p], local[p] + g1 - g0
        arrived(QX.at[i0:i1], at_ra[p])
        arrived(QY.at[i0:i1], at_ra[p] + 1)
        for i in range(i0, i1):
            QS[0, i] = (PS[i, y, far_x, :, 128:256].astype(f32) + QY[i, far_x].astype(f32)).astype(bf16)
            QS[1, i] = (PS[i, far_y, x, :, 0:128].astype(f32) + QX[i, far_y].astype(f32)).astype(bf16)
        send(lambda: QS.at[0, i0:i1], lambda: QB.at[0, i0:i1], dev_x, at_rb[p])
        send(lambda: QS.at[1, i0:i1], lambda: QB.at[1, i0:i1], dev_y, at_rb[p] + 1)

    def plane_end(p):
        g0, g1 = parts[p][:2]
        i0, i1 = local[p], local[p] + g1 - g0
        arrived(QB.at[0, i0:i1], at_rb[p])
        arrived(QB.at[1, i0:i1], at_rb[p] + 1)
        for i in range(i0, i1):
            base = PS[i, y, x].astype(f32)
            left = base[:, 0:128] + (QX[i, y].astype(f32) + QB[1, i].astype(f32))
            right = base[:, 128:256] + (QY[i, x].astype(f32) + QB[0, i].astype(f32))
            GF[g0 + i - i0, :, 0:128] = left
            GF[g0 + i - i0, :, 128:256] = right

    sets = (((4, 12), (2, 3, 4, 5), STA), ((0, 4), (0, 1), STB))
    at_rows = [place() for q in sets]
    at_quad = [place(3) for q in sets]
    at_line = [place(3) for q in sets]
    at_both = [place(4) for q in sets]
    at_cols = place(3)
    beta = 1.0 - STEP ** (-0.8)

    def row_sums(q):
        (g0, g1), _, _ = sets[q]

        @pl.loop(g0, g1)
        def _(g):
            grad = GF[g]
            RSUM[0, g] = jnp.broadcast_to(jnp.sum(grad * grad + square_floor, axis=1, keepdims=True), (BLOCK, 128))

        send(lambda: RSUM.at[0, g0:g1], lambda: RSUM.at[1, g0:g1], dev_peer, at_rows[q])

    def statistics(q):
        (g0, g1), members, SUMS = sets[q]
        arrived(RSUM.at[1, g0:g1], at_rows[q])
        lane_at = lax.broadcasted_iota(jnp.int32, (1, 128), 1)
        packed = jnp.zeros((1, 128), f32)
        n = len(members)
        SUMS[0] = jnp.zeros(SUMS.shape[1:], f32)
        for j, i in enumerate(members):
            squares, weighted, rows = 0.0, 0.0, 0.0
            for g in range(*MATRICES[i]):
                rowstat = OLD[g] + (1.0 - beta) * (RSUM[0, g] + RSUM[1, g])
                ROWSTAT[g] = rowstat
                square = GF[g] * GF[g]
                squares = squares + (square + square_floor)
                weighted = weighted + square / lanes(rowstat, 2)
                rows = rows + rowstat
            SUMS[0, j : j + 1, :] = jnp.sum(squares, axis=0, keepdims=True)
            SUMS[0, n + j : n + j + 1, :] = jnp.sum(weighted, axis=0, keepdims=True)
            packed = jnp.where(lane_at == j, jnp.sum(rows, axis=0, keepdims=True), packed)
        SUMS[0, 2 * n : 2 * n + 1, 0:128] = packed
        for k, dev in enumerate((dev_x, dev_y, dev_diagonal)):
            send(lambda: SUMS.at[0], lambda k=k: SUMS.at[1 + k], dev, at_quad[q] + k)

    def quad_sums(q):
        SUMS = sets[q][2]
        for k in range(3):
            arrived(SUMS.at[1 + k], at_quad[q] + k)
        SUMS[4] = (SUMS[0] + SUMS[1]) + (SUMS[2] + SUMS[3])
        for k in range(NZ - 1):
            send(lambda: SUMS.at[4], lambda k=k: SUMS.at[5 + k], dev_z[k], at_line[q] + k)
        send(lambda: SUMS.at[4], lambda: SUMS.at[8], dev_peer, at_both[q])
        for k in range(NZ - 1):
            send(lambda: SUMS.at[4], lambda k=k: SUMS.at[9 + k], (dev_z[k][0], other), at_both[q] + 1 + k)

    def line_sums(q):
        _, members, SUMS = sets[q]
        for k in range(NZ - 1):
            arrived(SUMS.at[5 + k], at_line[q] + k)
        for k in range(NZ):
            arrived(SUMS.at[8 + k], at_both[q] + k)
        lane_at = lax.broadcasted_iota(jnp.int32, (1, 128), 1)
        n = len(members)
        totals, norms = [0.0] * n, [0.0] * n
        for slot0, core in ((4, c), (8, other)):
            sums = (SUMS[slot0] + SUMS[slot0 + 1]) + (SUMS[slot0 + 2] + SUMS[slot0 + 3])
            for j, i in enumerate(members):
                cols_ref, at = (
                    (conv_cols, 0),
                    (proj_cols, 0),
                    (book_cols, 0),
                    (book_cols, 1),
                    (proj_cols, 1),
                    (conv_cols, 1),
                )[i]
                colstat = beta * cols_ref[core, at : at + 1] + (1.0 - beta) * sums[j : j + 1]
                if slot0 == 4:
                    cols_out = (
                        conv_cols_out,
                        proj_cols_out,
                        book_cols_out,
                        book_cols_out,
                        proj_cols_out,
                        conv_cols_out,
                    )[i]
                    cols_out[at : at + 1] = colstat
                    totals[j] = jnp.sum(
                        jnp.where(lane_at == j, sums[2 * n : 2 * n + 1, 0:128], 0.0), axis=1, keepdims=True
                    )
                norms[j] = norms[j] + jnp.sum(sums[n + j : n + j + 1] / colstat, axis=1, keepdims=True)
        for j, i in enumerate(members):
            g0, g1 = MATRICES[i]
            size = (g1 - g0) * BLOCK * NZ * NY * NX * D
            factor = jnp.maximum(1.0, jnp.sqrt(totals[j] * norms[j] / size) / clip_level)
            rate = (2.0 / math.sqrt(KERNEL * D), 2.0 / math.sqrt(D), 2.0)[(0, 1, 2, 2, 1, 0)[i]]
            for k in range(g1 - g0):
                grad, rowstat = GF[g0 + k], ROWSTAT[g0 + k]
                row = rowstat.T[0:1]
                if i in (0, 5):
                    m = i // 5
                    colstat = conv_cols_out[m : m + 1]
                elif i in (1, 4):
                    m = i // 4
                    colstat = proj_cols_out[m : m + 1]
                else:
                    m = i - 2
                    colstat = book_cols_out[m : m + 1]
                update = grad * lax.rsqrt(lanes(rowstat, 2) * colstat / totals[j])
                step = rate * (update / factor)
                if i in (0, 5):
                    conv_grad[m, k] = grad
                    conv_new[m, k] = conv_weight[m, k] - step
                    conv_rows_out[k, m : m + 1] = row
                elif i in (1, 4):
                    proj_grad[m] = grad
                    proj_new[m] = proj_weight[m] - step
                    proj_rows_out[m : m + 1] = row
                else:
                    part = slice(BLOCK * k, BLOCK * (k + 1))
                    book_grad[m, part] = grad
                    book_new[m, part] = codebooks[m, part] - step
                    book_rows_out[m : m + 1, part] = row

    operations = {
        "z": gather_z,
        "l": gather_line,
        "d": gather_diagonal,
        "q": gather_peer,
        "P": reduce_peer,
        "A": reduce_a,
        "B": reduce_b,
        "Z": reduce_z,
        "E": reduce_end,
        "a": plane_own,
        "b": plane_diagonal,
        "e": plane_line,
        "h": plane_peer,
        "U": plane_reduce,
        "V": plane_a,
        "X": plane_b,
        "F": plane_end,
        "R": row_sums,
        "S": statistics,
        "T": quad_sums,
        "N": line_sums,
    }

    def perform(steps):
        for operation, p in steps:
            operations[operation](p)

    def after(phase, b):
        for k, steps in SCHEDULE.get(phase, {}).items():

            @pl.when(b == k)
            def _():
                perform(steps)

    def once(phase):
        perform(SCHEDULE.get(phase, {}).get(0, ()))

    waited = set()

    def need(a, b):
        for p, (g0, g1, _) in enumerate(pieces):
            if g0 < b and a < g1 and p not in waited:
                waited.add(p)
                gathered(p)

    def w(a, b):
        return W[a:b].reshape((b - a) * D, D)

    def each(phase, step):

        @pl.loop(0, CLIPS)
        def _(b):
            step(b, pl.multiple_of(b * MAXLEN, MAXLEN))
            after(phase, b)

    def put(half, group, value):
        G[half, group] = value.astype(bf16).reshape(NZ, NY, NX, BLOCK, HALF)

    once("start")
    for load in small_in:
        load.wait()
    lane_row = lax.broadcasted_iota(jnp.int32, (1, MAXLEN), 1)
    count = jnp.zeros((1, MAXLEN), f32)
    for core in range(2):
        for b in range(CLIPS):
            live = (lane_row < lengths[core * CLIPS + b]) & (frame_mask[core, b] > 0)
            count = count + jnp.where(live, 1.0, 0.0)
    CN[0] = jnp.broadcast_to(jnp.sum(count, axis=1, keepdims=True), (8, 128))
    for k, dev in enumerate((dev_x, dev_y, dev_diagonal)):
        send(lambda: CN.at[0], lambda k=k: CN.at[1 + k], dev, at_count + k)
    for k, old in enumerate((conv_cols, proj_cols, book_cols)):
        send(lambda old=old: old.at[c], lambda old=old: old.at[c], dev_peer, at_cols + k)
    send(lambda: index_hbm.at[:, other], lambda: IDX.at[:, c], dev_peer, at_idx)
    send(lambda: cot_hbm.at[theirs, :], lambda: OB.at[:, cols], dev_peer, at_cot)

    @pl.loop(0, CLIPS)
    def _(b):
        live = (lane_row < lengths[c * CLIPS + b]) & (frame_mask[c, b] > 0)
        row = jnp.where(live, 1.0, 0.0)
        MASK[pl.ds(pl.multiple_of(b * MAXLEN, MAXLEN), MAXLEN), :] = jnp.broadcast_to(row, (128, MAXLEN)).T

    for g in range(GROUPS12):
        if g < 3:
            row = conv_rows[g, 0:1]
        elif g >= 9:
            row = conv_rows[g - 9, 1:2]
        elif g in (3, 8):
            row = proj_rows[g // 8 : g // 8 + 1]
        else:
            level, t = (g - 4) // 2, g % 2
            row = book_rows[level : level + 1, BLOCK * t : BLOCK * (t + 1)]
        OLD[g] = beta * jnp.broadcast_to(row, (128, BLOCK)).T
    frames_in.wait()

    def activate(b, r0):
        rows = pl.ds(r0, MAXLEN)
        for k in range(0, D, 128):
            a = gelu_pair(FR[rows, k : k + 128].astype(f32))[0] * MASK[rows, :]
            S[rows, k : k + 128], S[rows, 2 * D + k : 2 * D + k + 128] = neighbours(a)
            a = a.astype(bf16)
            S[rows, D + k : D + k + 128] = a
            AT[k : k + 128, rows] = a.T

    each("activate", activate)
    for k in range(3):
        arrived(CN.at[1 + k], at_count + k)
    CN[4] = (CN[0] + CN[1]) + (CN[2] + CN[3])
    for k in range(NZ - 1):
        send(lambda: CN.at[4], lambda k=k: CN.at[5 + k], dev_z[k], at_count + 3 + k)
    cot_in.wait()
    index_in.wait()
    arrived(OB.at[:, cols_other], at_cot)
    arrived(IDX.at[:, other], at_idx)
    for k, old in enumerate((conv_cols, proj_cols, book_cols)):
        arrived(old.at[other], at_cols + k)

    def upstream(b, r0):
        rows = pl.ds(r0, MAXLEN)
        for k in range(0, D, 128):
            ob = OB[rows, k : k + 128].astype(f32) * MASK[rows, :]
            O[rows, 2 * D + k : 2 * D + k + 128], O[rows, k : k + 128] = neighbours(ob)
            O[rows, D + k : D + k + 128] = ob.astype(bf16)

    each("upstream", upstream)
    for k in range(NZ - 1):
        arrived(CN.at[5 + k], at_count + 3 + k)
    scale = 2.0 / ((CN[4, 0:1] + CN[5, 0:1]) + (CN[6, 0:1] + CN[7, 0:1]))
    need(0, 3)

    def encode(b, r0):
        m = lanes(MASK[pl.ds(r0, MAXLEN), :], 4)
        branch = dot_nn(S[pl.ds(r0, MAXLEN), :], w(0, 3))
        enc = ((FR[pl.ds(r0, MAXLEN), :].astype(f32) + branch) * m).astype(bf16)
        STR[pl.ds(r0, MAXLEN), :] = enc
        ENCT[:, pl.ds(r0, MAXLEN)] = enc.T

    each("encode", encode)

    def project(b, r0):
        DGD[pl.ds(r0, MAXLEN), :] = dot_nn(STR[pl.ds(r0, MAXLEN), :], w(3, 4))

    need(3, 4)
    each("project", project)

    def slot(row):
        return ((row >> 5) & 1) * 512 + (row >> 6) * BLOCK + (row & 31)

    def onehot_rows(l, g, b):
        lane = lax.broadcasted_iota(jnp.int32, (MAXLEN, 128), 1)
        col = jnp.broadcast_to(slot(IDX[l, g, b]), (128, MAXLEN)).T
        return jnp.concatenate(
            [jnp.where(col == lane + 128 * k, 1.0, 0.0).astype(bf16) for k in range(CODES // 128)], axis=1
        )

    def chosen(l, g, b):
        book = W[4 + 2 * l : 6 + 2 * l, :, :, :, :, HALF * g : HALF * (g + 1)].reshape(CODES, HALF)
        return dot_nn(onehot_rows(l, g, b), book)

    def level_one(b, r0):
        for g in range(2):
            DEC[pl.ds(r0, MAXLEN), HALF * g : HALF * (g + 1)] = chosen(0, g, b)

    need(4, 6)
    each("level_one", level_one)

    def quantize(b, r0):
        m = lanes(MASK[pl.ds(r0, MAXLEN), :], 2)
        sc = lanes(scale, 2) * m
        for g in range(2):
            gc = slice(HALF * g, HALF * (g + 1))
            level = (DEC[pl.ds(r0, MAXLEN), gc], chosen(1, g, b))
            latent = DGD[pl.ds(r0, MAXLEN), gc]
            quantized = level[0] + level[1]
            straight = (latent + (quantized - latent)).astype(bf16)
            resid_one = latent - level[0]
            resid_two = resid_one - level[1]
            pulled = sc * (resid_one + resid_two)
            STR[pl.ds(r0, MAXLEN), gc] = straight
            STRT[gc, pl.ds(r0, MAXLEN)] = straight.T
            B1[pl.ds(r0, MAXLEN), gc] = (-pulled).astype(bf16)
            B2[pl.ds(r0, MAXLEN), gc] = (-(sc * resid_two)).astype(bf16)

    need(6, 8)
    each("quantize", quantize)

    def halves_of_grad(phase, count, step):
        @pl.loop(0, 2 * count)
        def _(t):
            half = lax.rem(t + other, 2)
            step(t // 2, half, pl.ds(pl.multiple_of(half * HALF, HALF), HALF))
            after(phase, t)

    def book_grads(phase, l, back):
        def step(_, g, hc):
            code = lax.broadcasted_iota(jnp.int32, (CODES, MAXLEN), 0)
            onehot = jnp.concatenate(
                [
                    jnp.where(jnp.broadcast_to(slot(IDX[l, g, b]), (CODES, MAXLEN)) == code, 1.0, 0.0).astype(bf16)
                    for b in range(CLIPS)
                ],
                axis=1,
            )
            value = dot_nn(onehot, back[:, hc]).astype(bf16)
            G[g, 4 + 2 * l : 6 + 2 * l] = value.reshape(2, NZ, NY, NX, BLOCK, HALF)

        halves_of_grad(phase, 1, step)

    book_grads("book0", 0, B1)
    book_grads("book1", 1, B2)

    def decode(b, r0):
        rows = pl.ds(r0, MAXLEN)
        DEC[rows, :] = dot_nn(STR[rows, :], w(8, 9))
        for k in range(0, D, 128):
            value, slope = gelu_pair(DEC[rows, k : k + 128])
            value = value * MASK[rows, :]
            DGD[rows, k : k + 128] = slope * MASK[rows, :]
            S[rows, k : k + 128], S[rows, 2 * D + k : 2 * D + k + 128] = neighbours(value)
            value = value.astype(bf16)
            S[rows, D + k : D + k + 128] = value
            DINT[k : k + 128, rows] = value.T

    need(8, 9)
    each("decode", decode)

    def kernel_grad(phase, left, base):
        def step(k, half, _):
            put(half, base + k, dot_nn(left[...], O[:, pl.ds(pl.multiple_of(k * D + half * HALF, HALF), HALF)]))

        halves_of_grad(phase, KERNEL, step)

    kernel_grad("kg9", DINT, 9)

    def decode_back(b, r0):
        total = None
        for k in range(KERNEL):
            term = dot_nt(O[pl.ds(r0, MAXLEN), k * D : (k + 1) * D], w(9 + k, 10 + k))
            total = term if total is None else total + term
        back = O[pl.ds(r0, MAXLEN), D : 2 * D].astype(f32) + DGD[pl.ds(r0, MAXLEN), :] * total
        back = back.astype(bf16)
        DB[pl.ds(r0, MAXLEN), :] = back
        pulled = B1[pl.ds(r0, MAXLEN), :].astype(f32)
        LB[pl.ds(r0, MAXLEN), :] = (dot_nt(back, w(8, 9)) - pulled).astype(bf16)

    need(9, 12)
    each("decode_back", decode_back)

    def proj_grads(phase, left, right, group):
        def step(_, half, hc):
            put(half, group, dot_nn(left[...], right[:, hc]))

        halves_of_grad(phase, 1, step)

    proj_grads("pg8", STRT, DB, 8)

    def encode_back(b, r0):
        rows = pl.ds(r0, MAXLEN)
        DGD[rows, :] = dot_nt(LB[rows, :], w(3, 4)) * lanes(MASK[rows, :], 4)
        for k in range(0, D, 128):
            low = DGD[rows, k : k + 128].astype(bf16)
            O[rows, 2 * D + k : 2 * D + k + 128], O[rows, k : k + 128] = neighbours(low.astype(f32))
            O[rows, D + k : D + k + 128] = low

    each("encode_back", encode_back)
    proj_grads("pg3", ENCT, LB, 3)
    kernel_grad("kg0", AT, 0)

    def halves(phase, step):

        @pl.loop(0, 2 * CLIPS)
        def _(t):
            h = t % 2
            step(pl.multiple_of((t // 2) * MAXLEN, MAXLEN), h, pl.ds(pl.multiple_of(h * HALF, HALF), HALF))
            after(phase, t)

    def decoded_result(r0, h, hc):
        m = lanes(MASK[pl.ds(r0, MAXLEN), :], 2)
        kernel = W[9:12, :, :, :, :, hc].reshape(KERNEL * D, HALF)
        value = (DEC[pl.ds(r0, MAXLEN), hc] + dot_nn(S[pl.ds(r0, MAXLEN), :], kernel)) * m
        OB[pl.ds(r0, MAXLEN), hc] = value.astype(bf16)

    def input_back(r0, h, hc):
        m = lanes(MASK[pl.ds(r0, MAXLEN), :], 2)
        total = None
        for k in range(KERNEL):
            kernel = W[k, pl.ds(2 * h, 2)].reshape(HALF, D)
            term = dot_nt(O[pl.ds(r0, MAXLEN), k * D : (k + 1) * D], kernel)
            total = term if total is None else total + term
        slope = gelu_pair(FR[pl.ds(r0, MAXLEN), hc].astype(f32))[1]
        STR[pl.ds(r0, MAXLEN), hc] = (DGD[pl.ds(r0, MAXLEN), hc] + slope * m * total).astype(bf16)

    halves("decoded", decoded_result)
    out_own = pltpu.make_async_copy(OB.at[:, cols], out_hbm.at[mine, :], lsem.at[3])
    out_own.start()
    at_out = place()
    send(lambda: OB.at[:, cols_other], lambda: out_hbm.at[mine, :], dev_peer, at_out)
    halves("input", input_back)
    in_own = pltpu.make_async_copy(STR.at[:, cols], input_hbm.at[mine, :], lsem.at[4])
    in_own.start()
    at_in = place()
    send(lambda: STR.at[:, cols_other], lambda: input_hbm.at[mine, :], dev_peer, at_in)

    once("end")

    assert counter[0] <= SEMAPHORES

    arrived(out_hbm.at[theirs, :], at_out)
    arrived(input_hbm.at[theirs, :], at_in)
    out_own.wait()
    in_own.wait()
    for src, at in unsent:
        remote(src(), src(), dev_peer, at).wait_send()


def write_kernel(*refs):
    count = len(refs) // 2
    copies = [pltpu.make_async_copy(refs[i], refs[count + i], refs[-1].at[i]) for i in range(count)]
    for copy in copies:
        copy.start()
    for copy in copies:
        copy.wait()


def fused_body(
    frames,
    cotangent,
    lengths,
    frame_mask,
    code_index,
    conv_weight,
    proj_weight,
    codebooks,
    conv_rows,
    conv_cols,
    proj_rows,
    proj_cols,
    book_rows,
    book_cols,
):
    vmem = pl.BlockSpec(memory_space=pltpu.VMEM)
    hbm = pl.BlockSpec(memory_space=pl.ANY)
    quad = (NZ, NY, NX, BLOCK)
    out = pl.pallas_call(
        fused_kernel,
        out_shape=(
            pltpu.VMEM(cotangent.shape, bf16),
            pltpu.VMEM(cotangent.shape, bf16),
            pltpu.VMEM(conv_weight.shape, f32),
            pltpu.VMEM(proj_weight.shape, f32),
            pltpu.VMEM(codebooks.shape, f32),
            pltpu.VMEM((KERNEL, 2, BLOCK), f32),
            pltpu.VMEM(conv_cols.shape, f32),
            pltpu.VMEM(proj_rows.shape, f32),
            pltpu.VMEM(proj_cols.shape, f32),
            pltpu.VMEM(book_rows.shape, f32),
            pltpu.VMEM(book_cols.shape, f32),
            pltpu.VMEM(conv_weight.shape, f32),
            pltpu.VMEM(proj_weight.shape, f32),
            pltpu.VMEM(codebooks.shape, f32),
        ),
        in_specs=[hbm] * 14,
        out_specs=(vmem,) * 14,
        scratch_shapes=[
            pltpu.VMEM((GROUPS12,) + quad + (D,), bf16),
            pltpu.VMEM((2, GROUPS12) + quad + (HALF,), bf16),
            pltpu.VMEM((GROUPS12,) + quad + (HALF,), bf16),
            pltpu.VMEM((GROUPS12, NZ, NY, BLOCK, 128), bf16),
            pltpu.VMEM((GROUPS12, NZ, NX, BLOCK, 128), bf16),
            pltpu.VMEM((GROUPS12, NZ, BLOCK, 128), bf16),
            pltpu.VMEM((GROUPS12, NZ, BLOCK, 128), bf16),
            pltpu.VMEM((GROUPS12, NZ, BLOCK, 128), bf16),
            pltpu.VMEM((GROUPS12, NZ, BLOCK, 128), bf16),
            pltpu.VMEM((GROUPS12, NZ, BLOCK, HALF), bf16),
            pltpu.VMEM((NZ - 1, GROUPS12, BLOCK, HALF), bf16),
            pltpu.VMEM((ROWS, D), bf16),
            pltpu.VMEM((ROWS, 3 * D), bf16),
            pltpu.VMEM((ROWS, 3 * D), bf16),
            pltpu.VMEM((D, ROWS), bf16),
            pltpu.VMEM((D, ROWS), bf16),
            pltpu.VMEM((D, ROWS), bf16),
            pltpu.VMEM((D, ROWS), bf16),
            pltpu.VMEM((ROWS, D), f32),
            pltpu.VMEM((ROWS, D), f32),
            pltpu.VMEM((ROWS, D), bf16),
            pltpu.VMEM((ROWS, D), bf16),
            pltpu.VMEM((ROWS, D), bf16),
            pltpu.VMEM((ROWS, D), bf16),
            pltpu.VMEM((NZ - 1, PLANES, NY, NX, BLOCK, HALF), bf16),
            pltpu.VMEM((PLANES, NY, NX, BLOCK, HALF), bf16),
            pltpu.VMEM((PLANES, NY, BLOCK, 128), bf16),
            pltpu.VMEM((PLANES, NX, BLOCK, 128), bf16),
            pltpu.VMEM((2, PLANES, BLOCK, 128), bf16),
            pltpu.VMEM((2, PLANES, BLOCK, 128), bf16),
            pltpu.VMEM(conv_weight.shape, f32),
            pltpu.VMEM(proj_weight.shape, f32),
            pltpu.VMEM(codebooks.shape, f32),
            pltpu.SMEM(lengths.shape, jnp.int32),
            pltpu.VMEM((2, CLIPS, 1, MAXLEN), jnp.int32),
            pltpu.VMEM((KERNEL, 2, BLOCK), f32),
            pltpu.VMEM(proj_rows.shape, f32),
            pltpu.VMEM(book_rows.shape, f32),
            pltpu.VMEM((2,) + conv_cols.shape, f32),
            pltpu.VMEM((2,) + proj_cols.shape, f32),
            pltpu.VMEM((2,) + book_cols.shape, f32),
            pltpu.VMEM((GROUPS12, BLOCK, 128), f32),
            pltpu.VMEM((ROWS, 128), f32),
            pltpu.VMEM((2, 2, CLIPS, 1, MAXLEN), jnp.int32),
            pltpu.VMEM((8, 8, 128), f32),
            pltpu.VMEM((GROUPS12, BLOCK, HALF), f32),
            pltpu.VMEM((GROUPS12, BLOCK, 128), f32),
            pltpu.VMEM((12, 16, HALF), f32),
            pltpu.VMEM((12, 8, HALF), f32),
            pltpu.VMEM((2, GROUPS12, BLOCK, 128), f32),
            pltpu.SemaphoreType.DMA((SEMAPHORES,)),
            pltpu.SemaphoreType.DMA((SEMAPHORES,)),
            pltpu.SemaphoreType.DMA((24,)),
        ],
        compiler_params=pltpu.CompilerParams(
            collective_id=0, has_side_effects=True, vmem_limit_bytes=58 * 2**20
        ),
        name="step",
    )(
        lengths,
        frames,
        cotangent,
        code_index.reshape(2, 2, CLIPS, 1, MAXLEN),
        conv_weight,
        proj_weight,
        codebooks,
        frame_mask.reshape(2, CLIPS, 1, MAXLEN),
        jnp.swapaxes(conv_rows, 0, 1),
        proj_rows,
        book_rows,
        conv_cols,
        proj_cols,
        book_cols,
    )
    out = pl.pallas_call(
        write_kernel,
        out_shape=tuple(jax.ShapeDtypeStruct(array.shape, array.dtype) for array in out),
        in_specs=[hbm] * len(out),
        out_specs=(hbm,) * len(out),
        scratch_shapes=[pltpu.SemaphoreType.DMA((len(out),))],
        compiler_params=pltpu.CompilerParams(vmem_limit_bytes=2 * 2**20),
        name="write",
    )(*out)
    return out[:5] + (jnp.swapaxes(out[5], 0, 1),) + out[6:]


def solution(mesh):
    placed = (
        P("dp", None),
        P("dp", "chan"),
        P("dp"),
        P("dp"),
        P(None, "dp", "chan"),
        P(None, None, "dp", "chan"),
        P(None, "dp", "chan"),
        P(None, "dp", "chan"),
        P(None, None, "dp"),
        P(None, "chan"),
        P(None, "dp"),
        P(None, "chan"),
        P(None, "dp"),
        P(None, "chan"),
    )
    fits = mesh.shape["dp"] == NZ * NY * NX and mesh.shape["chan"] == 2
    return jax.shard_map(
        fused_body if fits else general_body,
        mesh=mesh,
        in_specs=placed,
        out_specs=(
            P("dp", "chan"),
            P("dp", "chan"),
            P(None, None, "dp", "chan"),
            P(None, "dp", "chan"),
            P(None, "dp", "chan"),
            P(None, None, "dp"),
            P(None, "chan"),
            P(None, "dp"),
            P(None, "chan"),
            P(None, "dp"),
            P(None, "chan"),
            P(None, None, "dp", "chan"),
            P(None, "dp", "chan"),
            P(None, "dp", "chan"),
        ),
        check_vma=False,
    )
```

```python
import functools
import math

import jax
import jax.numpy as jnp
from jax import lax
from jax.experimental import pallas as pl
from jax.experimental.pallas import tpu as pltpu
from jax.sharding import PartitionSpec as P

D = 512
CODES = 1024
KERNEL = 3
STEP = 10
MAXLEN = 512
MICRO = 2


square_floor = 1e-30
clip_level = 0.5
f32 = jnp.float32
bf16 = jnp.bfloat16


def shifted(signal, length):
    channels = signal.shape[-1]
    blocks = signal.reshape(-1, length, channels)
    padded = jnp.pad(blocks, ((0, 0), (1, 1), (0, 0)))
    joined = jnp.concatenate(
        [padded[:, 0:length], padded[:, 1 : length + 1], padded[:, 2 : length + 2]], axis=2
    )
    return joined.reshape(-1, 3 * channels)


def unshift(partial_terms, length):
    channels = partial_terms.shape[-1] // 3
    blocks = partial_terms.reshape(-1, length, 3, channels)
    padded = jnp.pad(blocks, ((0, 0), (1, 1), (0, 0), (0, 0)))
    summed = padded[:, 2 : length + 2, 0] + padded[:, 1 : length + 1, 1] + padded[:, 0:length, 2]
    return summed.reshape(-1, channels)


def gelu_back(values, upstream):
    return jax.vjp(jax.nn.gelu, values)[1](upstream)[0]


def fetch(conv_weight, proj_weight, codebooks):
    return (
        lax.all_gather(conv_weight.astype(bf16), "dp", axis=2, tiled=True),
        lax.all_gather(proj_weight.astype(bf16), "dp", axis=1, tiled=True),
        lax.all_gather(codebooks.astype(bf16), "dp", axis=1, tiled=True),
    )


def reduce_grads(conv_total, proj_total, book_total):
    return (
        lax.psum_scatter(conv_total, "dp", scatter_dimension=2, tiled=True),
        lax.psum_scatter(proj_total, "dp", scatter_dimension=1, tiled=True),
        lax.psum_scatter(book_total, "dp", scatter_dimension=1, tiled=True),
    )


def contract(left, right):
    return jnp.einsum("fc,fd->cd", left, right, preferred_element_type=f32)


def transpose_product(left, right):
    return jnp.einsum("fd,cd->fc", left, right, preferred_element_type=f32)


def general_body(
    frames,
    cotangent,
    lengths,
    frame_mask,
    code_index,
    conv_weight,
    proj_weight,
    codebooks,
    conv_rows,
    conv_cols,
    proj_rows,
    proj_cols,
    book_rows,
    book_cols,
):
    length = MAXLEN
    block_rows = frames.shape[0] // MICRO
    half_width = cotangent.shape[1]
    chan_place = lax.axis_index("chan")
    row_place = jnp.arange(frames.shape[0], dtype=jnp.int32) % length
    live = (row_place < jnp.repeat(lengths, length, total_repeat_length=frames.shape[0])) & (
        frame_mask > 0
    )
    weight_mask = live.astype(f32)[:, None]
    live_total = lax.psum(jnp.sum(weight_mask), "dp")
    vq_scale = 2.0 / live_total
    running = None
    out_pieces = []
    grad_pieces = []
    for block_number in range(MICRO):
        first_row = block_number * block_rows
        last_row = first_row + block_rows
        conv_bank, proj_bank, book_bank = fetch(conv_weight, proj_weight, codebooks)
        conv_enc = conv_bank[0].reshape(-1, half_width)
        conv_dec = conv_bank[1].reshape(-1, half_width)
        frame_part = frames[first_row:last_row]
        frame_wide = frame_part.astype(f32)
        own_part = lax.dynamic_slice_in_dim(frame_wide, chan_place * half_width, half_width, 1)
        masked = weight_mask[first_row:last_row]
        cot_part = jnp.where(masked > 0, cotangent[first_row:last_row], jnp.zeros((), bf16))
        code_range = jnp.arange(book_bank.shape[1], dtype=jnp.int32)
        onehot_one = (code_index[0, first_row:last_row, 0][:, None] == code_range[None, :]).astype(
            bf16
        )
        onehot_two = (code_index[1, first_row:last_row, 0][:, None] == code_range[None, :]).astype(
            bf16
        )
        activated = (jax.nn.gelu(frame_wide) * masked).astype(bf16)
        stack_one = shifted(activated, length)
        branch = jnp.dot(stack_one, conv_enc, preferred_element_type=f32)
        encoded = (own_part + branch) * masked
        enc_full = lax.all_gather(encoded.astype(bf16), "chan", axis=1, tiled=True)
        latent = jnp.dot(enc_full, proj_bank[0], preferred_element_type=f32)
        level_one = jnp.dot(onehot_one, book_bank[0], preferred_element_type=f32)
        level_two = jnp.dot(onehot_two, book_bank[1], preferred_element_type=f32)
        quantized = level_one + level_two
        straight = (latent + (quantized - latent)).astype(bf16)
        straight_full = lax.all_gather(straight, "chan", axis=1, tiled=True)
        decoded = jnp.dot(straight_full, proj_bank[1], preferred_element_type=f32)
        decoder_in = (jax.nn.gelu(decoded) * masked).astype(bf16)
        decoder_full = lax.all_gather(decoder_in, "chan", axis=1, tiled=True)
        stack_two = shifted(decoder_full, length)
        result = (decoded + jnp.dot(stack_two, conv_dec, preferred_element_type=f32)) * masked
        out_pieces.append(result.astype(bf16))
        conv_dec_grad = contract(stack_two, cot_part)
        in_partial = unshift(transpose_product(cot_part, conv_dec), length)
        in_back = lax.psum_scatter(in_partial, "chan", scatter_dimension=1, tiled=True)
        decoded_back = (cot_part.astype(f32) + gelu_back(decoded, masked * in_back)).astype(bf16)
        proj_dec_grad = contract(straight_full, decoded_back)
        straight_back = lax.psum_scatter(
            transpose_product(decoded_back, proj_bank[1]), "chan", scatter_dimension=1, tiled=True
        )
        resid_one = latent - level_one
        resid_two = resid_one - level_two
        pulled = vq_scale * masked * (resid_one + resid_two)
        latent_back = (straight_back + pulled).astype(bf16)
        one_back = (-pulled).astype(bf16)
        two_back = (-(vq_scale * masked * resid_two)).astype(bf16)
        book_one_grad = contract(onehot_one, one_back)
        book_two_grad = contract(onehot_two, two_back)
        proj_enc_grad = contract(enc_full, latent_back)
        encoded_back = lax.psum_scatter(
            transpose_product(latent_back, proj_bank[0]), "chan", scatter_dimension=1, tiled=True
        )
        branch_back = (encoded_back * masked).astype(bf16)
        conv_enc_grad = contract(stack_one, branch_back)
        activated_back = unshift(transpose_product(branch_back, conv_enc), length)
        input_partial = gelu_back(frame_wide, masked * activated_back)
        input_own = lax.psum_scatter(input_partial, "chan", scatter_dimension=1, tiled=True)
        grad_pieces.append((encoded_back * masked + input_own).astype(bf16))
        conv_blockgrad = jnp.stack(
            [
                conv_enc_grad.reshape(KERNEL, -1, half_width),
                conv_dec_grad.reshape(KERNEL, -1, half_width),
            ]
        )
        proj_blockgrad = jnp.stack([proj_enc_grad, proj_dec_grad])
        book_blockgrad = jnp.stack([book_one_grad, book_two_grad])
        reduced = reduce_grads(conv_blockgrad, proj_blockgrad, book_blockgrad)
        running = (
            reduced
            if running is None
            else (running[0] + reduced[0], running[1] + reduced[1], running[2] + reduced[2])
        )
    conv_grad, proj_grad, book_grad = running
    decoded_out = jnp.concatenate(out_pieces, axis=0)
    input_grad = jnp.concatenate(grad_pieces, axis=0)
    beta_two = 1.0 - STEP ** (-0.8)
    squares_conv = conv_grad * conv_grad + square_floor
    squares_proj = proj_grad * proj_grad + square_floor
    squares_book = book_grad * book_grad + square_floor
    row_sums = lax.psum(
        (
            jnp.sum(squares_conv, axis=3),
            jnp.sum(squares_proj, axis=2),
            jnp.sum(squares_book, axis=2),
        ),
        "chan",
    )
    rowstat_conv = beta_two * conv_rows + (1.0 - beta_two) * row_sums[0]
    rowstat_proj = beta_two * proj_rows + (1.0 - beta_two) * row_sums[1]
    rowstat_book = beta_two * book_rows + (1.0 - beta_two) * row_sums[2]
    col_sums = lax.psum(
        (
            jnp.sum(squares_conv, axis=(1, 2)),
            jnp.sum(squares_proj, axis=1),
            jnp.sum(squares_book, axis=1),
            jnp.sum(rowstat_conv, axis=(1, 2)),
            jnp.sum(rowstat_proj, axis=1),
            jnp.sum(rowstat_book, axis=1),
        ),
        "dp",
    )
    colstat_conv = beta_two * conv_cols + (1.0 - beta_two) * col_sums[0]
    colstat_proj = beta_two * proj_cols + (1.0 - beta_two) * col_sums[1]
    colstat_book = beta_two * book_cols + (1.0 - beta_two) * col_sums[2]
    update_conv = conv_grad * lax.rsqrt(
        rowstat_conv[..., None] * colstat_conv[:, None, None, :] / col_sums[3][:, None, None, None]
    )
    update_proj = proj_grad * lax.rsqrt(
        rowstat_proj[..., None] * colstat_proj[:, None, :] / col_sums[4][:, None, None]
    )
    update_book = book_grad * lax.rsqrt(
        rowstat_book[..., None] * colstat_book[:, None, :] / col_sums[5][:, None, None]
    )
    norm_sums = lax.psum(
        (
            jnp.sum(update_conv * update_conv, axis=(1, 2, 3)),
            jnp.sum(update_proj * update_proj, axis=(1, 2)),
            jnp.sum(update_book * update_book, axis=(1, 2)),
        ),
        ("dp", "chan"),
    )
    factor_conv = jnp.maximum(1.0, jnp.sqrt(norm_sums[0] / (KERNEL * D * D)) / clip_level)
    factor_proj = jnp.maximum(1.0, jnp.sqrt(norm_sums[1] / (D * D)) / clip_level)
    factor_book = jnp.maximum(1.0, jnp.sqrt(norm_sums[2] / (CODES * D)) / clip_level)
    rate_conv = 2.0 / math.sqrt(KERNEL * D)
    rate_proj = 2.0 / math.sqrt(D)
    updated_conv = conv_weight - rate_conv * (update_conv / factor_conv[:, None, None, None])
    updated_proj = proj_weight - rate_proj * (update_proj / factor_proj[:, None, None])
    updated_book = codebooks - 2.0 * (update_book / factor_book[:, None, None])
    return (
        decoded_out,
        input_grad,
        conv_grad,
        proj_grad,
        book_grad,
        rowstat_conv,
        colstat_conv,
        rowstat_proj,
        colstat_proj,
        rowstat_book,
        colstat_book,
        updated_conv,
        updated_proj,
        updated_book,
    )


MESH = pl.DeviceIdType.MESH
CLIPS = 3
ROWS = CLIPS * MAXLEN
GROUPS12 = 12
NZ, NY, NX = 4, 2, 2
BLOCK = 32
SEMAPHORES = 256
HALF = 256
GELU_A = math.sqrt(2.0 / math.pi)
GELU_B = 0.044715
MATRICES = ((0, 3), (3, 4), (4, 6), (6, 8), (8, 9), (9, 12))


def gelu_pair(x):
    x2 = x * x
    t = jnp.tanh(x * (GELU_A + GELU_A * GELU_B * x2))
    half = 0.5 + 0.5 * t
    value = x * half
    return value, half + value * (1.0 - t) * (GELU_A + 3.0 * GELU_A * GELU_B * x2)


def lanes(m, n):
    return jnp.concatenate([m] * n, axis=1)


def dot_nn(a, b):
    return jnp.dot(a, b, preferred_element_type=f32)


def dot_nt(a, b):
    return lax.dot_general(a, b, (((1,), (1,)), ((), ())), preferred_element_type=f32)


def neighbours(v):
    rows = v.shape[0]
    row = lax.broadcasted_iota(jnp.int32, (8, v.shape[1]), 0)
    before, after = pltpu.roll(v, 1, 0), pltpu.roll(v, rows - 1, 0)
    before = jnp.concatenate([jnp.where(row == 0, 0.0, before[:8]), before[8:]], axis=0)
    after = jnp.concatenate([after[:-8], jnp.where(row == 7, 0.0, after[-8:])], axis=0)
    return before.astype(bf16), after.astype(bf16)


PIECES = ((0, 1, "f"), (1, 2, "f"), (2, 3, "f"), (3, 4, "f"), (4, 6, "f"), (6, 8, "f"), (8, 9, "f"), (9, 11, "f"), (11, 12, "f"))
PARTS = ((4, 6, "f"), (6, 8, "f"), (9, 10, "l"), (10, 12, "f"), (8, 9, "l"), (3, 4, "f"), (0, 1, "f"), (1, 2, "f"), (2, 3, "f"))
PLANES = max(1, sum((g1 - g0) * (kind == "l") for g0, g1, kind in PARTS))
SCHEDULE = {
    "start": {
        0: (("z", 2), ("z", 1), ("z", 3), ("z", 0), ("z", 4),),
    },
    "activate": {
        0: (("l", 2), ("l", 1), ("z", 6), ("l", 3), ("l", 0), ("z", 5), ("d", 2),),
        1: (("d", 1), ("z", 8), ("l", 4), ("d", 0),),
        2: (("q", 2), ("q", 1), ("l", 5),),
    },
    "upstream": {
        1: (("d", 3),),
        2: (("z", 7), ("q", 0), ("d", 4),),
    },
    "encode": {
        0: (("d", 5),),
        1: (("q", 3),),
        2: (("q", 4), ("l", 6), ("l", 7), ("l", 8),),
    },
    "project": {
        2: (("q", 5),),
    },
    "quantize": {
        1: (("d", 6),),
    },
    "book0": {
        0: (("P", 0), ("d", 7),),
        1: (("q", 6),),
    },
    "book1": {
        0: (("d", 8), ("P", 1), ("A", 0),),
    },
    "decode": {
        1: (("q", 7),),
    },
    "kg9": {
        1: (("P", 2), ("q", 8),),
        2: (("B", 0),),
        4: (("A", 1), ("U", 2), ("P", 3),),
    },
    "decode_back": {
        1: (("A", 3), ("Z", 0),),
    },
    "pg8": {
        0: (("B", 1), ("P", 4),),
    },
    "encode_back": {
        2: (("U", 4), ("V", 2),),
    },
    "pg3": {
        0: (("P", 5), ("B", 3),),
    },
    "kg0": {
        0: (("P", 6), ("A", 5),),
        2: (("P", 7), ("A", 6),),
        4: (("P", 8), ("Z", 1), ("A", 7),),
    },
    "decoded": {
        0: (("A", 8), ("Z", 3),),
        2: (("B", 6), ("B", 5),),
        4: (("V", 4),),
        5: (("X", 2),),
    },
    "input": {
        0: (("E", 0), ("B", 8), ("B", 7), ("Z", 6), ("E", 1),),
        1: (("X", 4), ("Z", 5),),
        2: (("Z", 8),),
        3: (("F", 2), ("Z", 7),),
        4: (("E", 3),),
        5: (("E", 6),),
    },
    "end": {
        0: (("F", 4), ("R", 0), ("S", 0), ("E", 8), ("E", 5), ("E", 7), ("R", 1), ("S", 1), ("T", 0), ("T", 1), ("N", 0), ("N", 1),),
    },
}


def fused_kernel(
    lengths_hbm,
    frames_hbm,
    cot_hbm,
    index_hbm,
    conv_hbm,
    proj_hbm,
    books_hbm,
    mask_hbm,
    conv_rows_hbm,
    proj_rows_hbm,
    book_rows_hbm,
    conv_cols_hbm,
    proj_cols_hbm,
    book_cols_hbm,
    out_hbm,
    input_hbm,
    conv_grad,
    proj_grad,
    book_grad,
    conv_rows_out,
    conv_cols_out,
    proj_rows_out,
    proj_cols_out,
    book_rows_out,
    book_cols_out,
    conv_new,
    proj_new,
    book_new,
    W,
    G,
    RP,
    AX,
    AY,
    BX,
    BY,
    BXS,
    BYS,
    TS,
    ZR,
    FR,
    S,
    O,
    AT,
    ENCT,
    STRT,
    DINT,
    DEC,
    DGD,
    B1,
    B2,
    STR,
    OB,
    ZQ,
    PS,
    QX,
    QY,
    QS,
    QB,
    conv_weight,
    proj_weight,
    codebooks,
    lengths,
    frame_mask,
    conv_rows,
    proj_rows,
    book_rows,
    conv_cols,
    proj_cols,
    book_cols,
    OLD,
    MASK,
    IDX,
    CN,
    GF,
    ROWSTAT,
    STA,
    STB,
    RSUM,
    ssem,
    rsem,
    lsem,
):
    DB, LB = OB, B1
    me = lax.axis_index("dp")
    c = lax.axis_index("chan")
    z, y, x = me // (NY * NX), (me // NX) % NY, me % NX
    far_y, far_x, other = 1 - y, 1 - x, 1 - c

    def dp_of(zz, yy, xx):
        return (zz * (NY * NX) + yy * NX + xx, c)

    dev_x, dev_y, dev_diagonal = dp_of(z, y, far_x), dp_of(z, far_y, x), dp_of(z, far_y, far_x)
    dev_z = [dp_of(lax.rem(z + k, NZ), y, x) for k in range(1, NZ)]
    dev_peer = (me, other)
    to_z = [lax.rem(z + k, NZ) for k in range(1, NZ)]
    from_z = [lax.rem(z + NZ - k, NZ) for k in range(1, NZ)]
    cols = pl.ds(pl.multiple_of(c * HALF, HALF), HALF)
    cols_other = pl.ds(pl.multiple_of(other * HALF, HALF), HALF)
    quarter = (
        pl.ds(pl.multiple_of(c * HALF, HALF), 128),
        pl.ds(pl.multiple_of(c * HALF + 128, 128), 128),
    )
    mine = pl.ds(pl.multiple_of(c * ROWS, ROWS), ROWS)
    theirs = pl.ds(pl.multiple_of(other * ROWS, ROWS), ROWS)

    counter = [0]
    unsent = []

    def place(n=1):
        counter[0] += n
        return counter[0] - n

    def remote(src, dst, dev, at):
        return pltpu.make_async_remote_copy(
            src_ref=src,
            dst_ref=dst,
            send_sem=ssem.at[at],
            recv_sem=rsem.at[at],
            device_id=dev,
            device_id_type=MESH,
        )

    def send(src, dst, dev, at):
        remote(src(), dst(), dev, at).start()
        unsent.append((src, at))

    def arrived(dst, at):
        remote(dst, dst, dev_peer, at).wait_recv()

    barrier = pltpu.get_barrier_semaphore()
    partners = [dev_x, dev_y, dev_diagonal, dev_peer] + dev_z + [(dev[0], other) for dev in dev_z]
    for dev in partners:
        pl.semaphore_signal(barrier, inc=1, device_id=dev, device_id_type=MESH)
    weights_in = [
        pltpu.make_async_copy(src, dst, lsem.at[9 + i])
        for i, (src, dst) in enumerate(((conv_hbm, conv_weight), (proj_hbm, proj_weight), (books_hbm, codebooks)))
    ]
    for load in weights_in:
        load.start()
    index_in = pltpu.make_async_copy(index_hbm.at[:, c], IDX.at[:, c], lsem.at[2])
    index_in.start()
    frames_in = pltpu.make_async_copy(frames_hbm.at[mine, :], FR, lsem.at[0])
    frames_in.start()
    cot_in = pltpu.make_async_copy(cot_hbm.at[mine, :], OB.at[:, cols], lsem.at[1])
    cot_in.start()
    small_in = [
        pltpu.make_async_copy(src, dst, lsem.at[16 + i])
        for i, (src, dst) in enumerate(
            (
                (lengths_hbm, lengths),
                (mask_hbm, frame_mask),
                (conv_rows_hbm, conv_rows),
                (proj_rows_hbm, proj_rows),
                (book_rows_hbm, book_rows),
                (conv_cols_hbm, conv_cols.at[c]),
                (proj_cols_hbm, proj_cols.at[c]),
                (book_cols_hbm, book_cols.at[c]),
            )
        )
    ]
    for load in small_in:
        load.start()
    for load in weights_in:
        load.wait()

    for k in range(3):
        W[k, z, y, x, :, cols] = conv_weight[0, k].astype(bf16)
        W[9 + k, z, y, x, :, cols] = conv_weight[1, k].astype(bf16)
    W[3, z, y, x, :, cols] = proj_weight[0].astype(bf16)
    W[8, z, y, x, :, cols] = proj_weight[1].astype(bf16)
    for level in range(2):
        for t in range(2):
            W[4 + 2 * level + t, z, y, x, :, cols] = codebooks[level, BLOCK * t : BLOCK * (t + 1)].astype(bf16)
    pl.semaphore_wait(barrier, len(partners))

    pieces = PIECES
    at_z = [place(3) for p in pieces]
    at_l = [place(2) for p in pieces]
    at_d = [place(2) for p in pieces]
    at_p = [place(2) for p in pieces]
    at_cot, at_idx, at_count = place(), place(), place(6)

    def gather_z(p):
        g0, g1 = pieces[p][:2]
        for k in range(NZ - 1):
            own = lambda: W.at[g0:g1, z, y, x, :, cols]
            send(own, own, dev_z[k], at_z[p] + k)

    def gather_line(p):
        g0, g1 = pieces[p][:2]
        for k in range(NZ - 1):
            arrived(W.at[g0:g1, from_z[k], y, x, :, cols], at_z[p] + k)
        line = lambda: W.at[g0:g1, :, y, x, :, cols]
        send(line, line, dev_x, at_l[p])
        send(line, line, dev_y, at_l[p] + 1)

    def gather_diagonal(p):
        g0, g1 = pieces[p][:2]
        arrived(W.at[g0:g1, :, y, far_x, :, cols], at_l[p])
        arrived(W.at[g0:g1, :, far_y, x, :, cols], at_l[p] + 1)
        part_y = lambda: W.at[g0:g1, :, far_y, x, :, quarter[0]]
        send(part_y, part_y, dev_x, at_d[p])
        part_x = lambda: W.at[g0:g1, :, y, far_x, :, quarter[1]]
        send(part_x, part_x, dev_y, at_d[p] + 1)
        near = lambda: W.at[g0:g1, :, y, :, :, cols]
        send(near, near, dev_peer, at_p[p])

    def gather_peer(p):
        g0, g1 = pieces[p][:2]
        arrived(W.at[g0:g1, :, far_y, far_x, :, quarter[0]], at_d[p])
        arrived(W.at[g0:g1, :, far_y, far_x, :, quarter[1]], at_d[p] + 1)
        far = lambda: W.at[g0:g1, :, far_y, :, :, cols]
        send(far, far, dev_peer, at_p[p] + 1)

    def plane_own(p):
        g0, g1 = pieces[p][:2]
        own = lambda: W.at[g0:g1, z, y, x, :, cols]
        send(own, own, dev_x, at_l[p])
        send(own, own, dev_y, at_l[p] + 1)

    def plane_diagonal(p):
        g0, g1 = pieces[p][:2]
        arrived(W.at[g0:g1, z, y, far_x, :, cols], at_l[p])
        arrived(W.at[g0:g1, z, far_y, x, :, cols], at_l[p] + 1)
        part_y = lambda: W.at[g0:g1, z, far_y, x, :, quarter[0]]
        send(part_y, part_y, dev_x, at_d[p])
        part_x = lambda: W.at[g0:g1, z, y, far_x, :, quarter[1]]
        send(part_x, part_x, dev_y, at_d[p] + 1)

    def plane_line(p):
        g0, g1 = pieces[p][:2]
        arrived(W.at[g0:g1, z, far_y, far_x, :, quarter[0]], at_d[p])
        arrived(W.at[g0:g1, z, far_y, far_x, :, quarter[1]], at_d[p] + 1)
        plane = lambda: W.at[g0:g1, z, :, :, :, cols]
        for k in range(NZ - 1):
            send(plane, plane, dev_z[k], at_z[p] + k)

    def plane_peer(p):
        g0, g1 = pieces[p][:2]
        for k in range(NZ - 1):
            arrived(W.at[g0:g1, from_z[k], :, :, :, cols], at_z[p] + k)
        whole = lambda: W.at[g0:g1, :, :, :, :, cols]
        send(whole, whole, dev_peer, at_p[p])

    def gathered(p):
        g0, g1 = pieces[p][:2]
        if pieces[p][2] == "l":
            arrived(W.at[g0:g1, :, :, :, :, cols_other], at_p[p])
            return
        arrived(W.at[g0:g1, :, y, :, :, cols_other], at_p[p])
        arrived(W.at[g0:g1, :, far_y, :, :, cols_other], at_p[p] + 1)

    parts = PARTS
    local, planes = [], 0
    for g0, g1, kind in parts:
        local.append(planes)
        planes += (g1 - g0) * (kind == "l")
    at_rp = [place() for p in parts]
    at_ra = [place(2) for p in parts]
    at_rb = [place(2) for p in parts]
    at_rz = [place(3) for p in parts]

    def reduce_peer(p):
        g0, g1 = parts[p][:2]
        send(lambda: G.at[other, g0:g1], lambda: RP.at[g0:g1], dev_peer, at_rp[p])

    def reduce_a(p):
        g0, g1 = parts[p][:2]
        arrived(RP.at[g0:g1], at_rp[p])

        @pl.loop(g0, g1)
        def _(g):
            G[c, g] = (G[c, g].astype(f32) + RP[g].astype(f32)).astype(bf16)

        send(lambda: G.at[c, g0:g1, :, :, far_x, :, 0:128], lambda: AX.at[g0:g1], dev_x, at_ra[p])
        send(lambda: G.at[c, g0:g1, :, far_y, :, :, 128:256], lambda: AY.at[g0:g1], dev_y, at_ra[p] + 1)

    def reduce_b(p):
        g0, g1 = parts[p][:2]
        arrived(AX.at[g0:g1], at_ra[p])
        arrived(AY.at[g0:g1], at_ra[p] + 1)

        @pl.loop(g0, g1)
        def _(g):
            BXS[g] = (G[c, g, :, y, far_x, :, 128:256].astype(f32) + AY[g, :, far_x].astype(f32)).astype(bf16)
            BYS[g] = (G[c, g, :, far_y, x, :, 0:128].astype(f32) + AX[g, :, far_y].astype(f32)).astype(bf16)

        send(lambda: BXS.at[g0:g1], lambda: BX.at[g0:g1], dev_x, at_rb[p])
        send(lambda: BYS.at[g0:g1], lambda: BY.at[g0:g1], dev_y, at_rb[p] + 1)

    def reduce_z(p):
        g0, g1 = parts[p][:2]
        arrived(BX.at[g0:g1], at_rb[p])
        arrived(BY.at[g0:g1], at_rb[p] + 1)

        @pl.loop(g0, g1)
        def _(g):
            base = G[c, g, :, y, x].astype(f32)
            left = base[:, :, 0:128] + (AX[g, :, y].astype(f32) + BY[g].astype(f32))
            right = base[:, :, 128:256] + (AY[g, :, x].astype(f32) + BX[g].astype(f32))
            TS[g, :, :, 0:128] = left.astype(bf16)
            TS[g, :, :, 128:256] = right.astype(bf16)

        for k in range(NZ - 1):
            send(
                lambda k=k: TS.at[g0:g1, to_z[k]],
                lambda k=k: ZR.at[k, g0:g1],
                dev_z[k],
                at_rz[p] + k,
            )

    def reduce_end(p):
        g0, g1 = parts[p][:2]
        for k in range(NZ - 1):
            arrived(ZR.at[k, g0:g1], at_rz[p] + k)

        @pl.loop(g0, g1)
        def _(g):
            GF[g] = (TS[g, z].astype(f32) + ZR[0, g].astype(f32)) + (ZR[1, g].astype(f32) + ZR[2, g].astype(f32))

    def plane_reduce(p):
        g0, g1 = parts[p][:2]
        arrived(RP.at[g0:g1], at_rp[p])

        @pl.loop(g0, g1)
        def _(g):
            G[c, g] = (G[c, g].astype(f32) + RP[g].astype(f32)).astype(bf16)

        for k in range(NZ - 1):
            send(
                lambda k=k: G.at[c, g0:g1, to_z[k]],
                lambda k=k: ZQ.at[k, local[p] : local[p] + g1 - g0],
                dev_z[k],
                at_rz[p] + k,
            )

    def plane_a(p):
        g0, g1 = parts[p][:2]
        i0, i1 = local[p], local[p] + g1 - g0
        for k in range(NZ - 1):
            arrived(ZQ.at[k, i0:i1], at_rz[p] + k)
        for i in range(i0, i1):
            total = G[c, g0 + i - i0, z].astype(f32) + ZQ[0, i].astype(f32)
            PS[i] = (total + (ZQ[1, i].astype(f32) + ZQ[2, i].astype(f32))).astype(bf16)
        send(lambda: PS.at[i0:i1, :, far_x, :, 0:128], lambda: QX.at[i0:i1], dev_x, at_ra[p])
        send(lambda: PS.at[i0:i1, far_y, :, :, 128:256], lambda: QY.at[i0:i1], dev_y, at_ra[p] + 1)

    def plane_b(p):
        g0, g1 = parts[p][:2]
        i0, i1 = local[p], local[p] + g1 - g0
        arrived(QX.at[i0:i1], at_ra[p])
        arrived(QY.at[i0:i1], at_ra[p] + 1)
        for i in range(i0, i1):
            QS[0, i] = (PS[i, y, far_x, :, 128:256].astype(f32) + QY[i, far_x].astype(f32)).astype(bf16)
            QS[1, i] = (PS[i, far_y, x, :, 0:128].astype(f32) + QX[i, far_y].astype(f32)).astype(bf16)
        send(lambda: QS.at[0, i0:i1], lambda: QB.at[0, i0:i1], dev_x, at_rb[p])
        send(lambda: QS.at[1, i0:i1], lambda: QB.at[1, i0:i1], dev_y, at_rb[p] + 1)

    def plane_end(p):
        g0, g1 = parts[p][:2]
        i0, i1 = local[p], local[p] + g1 - g0
        arrived(QB.at[0, i0:i1], at_rb[p])
        arrived(QB.at[1, i0:i1], at_rb[p] + 1)
        for i in range(i0, i1):
            base = PS[i, y, x].astype(f32)
            left = base[:, 0:128] + (QX[i, y].astype(f32) + QB[1, i].astype(f32))
            right = base[:, 128:256] + (QY[i, x].astype(f32) + QB[0, i].astype(f32))
            GF[g0 + i - i0, :, 0:128] = left
            GF[g0 + i - i0, :, 128:256] = right

    sets = (((4, 12), (2, 3, 4, 5), STA), ((0, 4), (0, 1), STB))
    at_rows = [place() for q in sets]
    at_quad = [place(3) for q in sets]
    at_line = [place(3) for q in sets]
    at_both = [place(4) for q in sets]
    at_cols = place(3)
    beta = 1.0 - STEP ** (-0.8)

    def row_sums(q):
        (g0, g1), _, _ = sets[q]

        @pl.loop(g0, g1)
        def _(g):
            grad = GF[g]
            RSUM[0, g] = jnp.broadcast_to(jnp.sum(grad * grad + square_floor, axis=1, keepdims=True), (BLOCK, 128))

        send(lambda: RSUM.at[0, g0:g1], lambda: RSUM.at[1, g0:g1], dev_peer, at_rows[q])

    def statistics(q):
        (g0, g1), members, SUMS = sets[q]
        arrived(RSUM.at[1, g0:g1], at_rows[q])
        lane_at = lax.broadcasted_iota(jnp.int32, (1, 128), 1)
        packed = jnp.zeros((1, 128), f32)
        n = len(members)
        SUMS[0] = jnp.zeros(SUMS.shape[1:], f32)
        for j, i in enumerate(members):
            squares, weighted, rows = 0.0, 0.0, 0.0
            for g in range(*MATRICES[i]):
                rowstat = OLD[g] + (1.0 - beta) * (RSUM[0, g] + RSUM[1, g])
                ROWSTAT[g] = rowstat
                square = GF[g] * GF[g]
                squares = squares + (square + square_floor)
                weighted = weighted + square / lanes(rowstat, 2)
                rows = rows + rowstat
            SUMS[0, j : j + 1, :] = jnp.sum(squares, axis=0, keepdims=True)
            SUMS[0, n + j : n + j + 1, :] = jnp.sum(weighted, axis=0, keepdims=True)
            packed = jnp.where(lane_at == j, jnp.sum(rows, axis=0, keepdims=True), packed)
        SUMS[0, 2 * n : 2 * n + 1, 0:128] = packed
        for k, dev in enumerate((dev_x, dev_y, dev_diagonal)):
            send(lambda: SUMS.at[0], lambda k=k: SUMS.at[1 + k], dev, at_quad[q] + k)

    def quad_sums(q):
        SUMS = sets[q][2]
        for k in range(3):
            arrived(SUMS.at[1 + k], at_quad[q] + k)
        SUMS[4] = (SUMS[0] + SUMS[1]) + (SUMS[2] + SUMS[3])
        for k in range(NZ - 1):
            send(lambda: SUMS.at[4], lambda k=k: SUMS.at[5 + k], dev_z[k], at_line[q] + k)
        send(lambda: SUMS.at[4], lambda: SUMS.at[8], dev_peer, at_both[q])
        for k in range(NZ - 1):
            send(lambda: SUMS.at[4], lambda k=k: SUMS.at[9 + k], (dev_z[k][0], other), at_both[q] + 1 + k)

    def line_sums(q):
        _, members, SUMS = sets[q]
        for k in range(NZ - 1):
            arrived(SUMS.at[5 + k], at_line[q] + k)
        for k in range(NZ):
            arrived(SUMS.at[8 + k], at_both[q] + k)
        lane_at = lax.broadcasted_iota(jnp.int32, (1, 128), 1)
        n = len(members)
        totals, norms = [0.0] * n, [0.0] * n
        for slot0, core in ((4, c), (8, other)):
            sums = (SUMS[slot0] + SUMS[slot0 + 1]) + (SUMS[slot0 + 2] + SUMS[slot0 + 3])
            for j, i in enumerate(members):
                cols_ref, at = (
                    (conv_cols, 0),
                    (proj_cols, 0),
                    (book_cols, 0),
                    (book_cols, 1),
                    (proj_cols, 1),
                    (conv_cols, 1),
                )[i]
                colstat = beta * cols_ref[core, at : at + 1] + (1.0 - beta) * sums[j : j + 1]
                if slot0 == 4:
                    cols_out = (
                        conv_cols_out,
                        proj_cols_out,
                        book_cols_out,
                        book_cols_out,
                        proj_cols_out,
                        conv_cols_out,
                    )[i]
                    cols_out[at : at + 1] = colstat
                    totals[j] = jnp.sum(
                        jnp.where(lane_at == j, sums[2 * n : 2 * n + 1, 0:128], 0.0), axis=1, keepdims=True
                    )
                norms[j] = norms[j] + jnp.sum(sums[n + j : n + j + 1] / colstat, axis=1, keepdims=True)
        for j, i in enumerate(members):
            g0, g1 = MATRICES[i]
            size = (g1 - g0) * BLOCK * NZ * NY * NX * D
            factor = jnp.maximum(1.0, jnp.sqrt(totals[j] * norms[j] / size) / clip_level)
            rate = (2.0 / math.sqrt(KERNEL * D), 2.0 / math.sqrt(D), 2.0)[(0, 1, 2, 2, 1, 0)[i]]
            for k in range(g1 - g0):
                grad, rowstat = GF[g0 + k], ROWSTAT[g0 + k]
                row = rowstat.T[0:1]
                if i in (0, 5):
                    m = i // 5
                    colstat = conv_cols_out[m : m + 1]
                elif i in (1, 4):
                    m = i // 4
                    colstat = proj_cols_out[m : m + 1]
                else:
                    m = i - 2
                    colstat = book_cols_out[m : m + 1]
                update = grad * lax.rsqrt(lanes(rowstat, 2) * colstat / totals[j])
                step = rate * (update / factor)
                if i in (0, 5):
                    conv_grad[m, k] = grad
                    conv_new[m, k] = conv_weight[m, k] - step
                    conv_rows_out[k, m : m + 1] = row
                elif i in (1, 4):
                    proj_grad[m] = grad
                    proj_new[m] = proj_weight[m] - step
                    proj_rows_out[m : m + 1] = row
                else:
                    part = slice(BLOCK * k, BLOCK * (k + 1))
                    book_grad[m, part] = grad
                    book_new[m, part] = codebooks[m, part] - step
                    book_rows_out[m : m + 1, part] = row

    operations = {
        "z": gather_z,
        "l": gather_line,
        "d": gather_diagonal,
        "q": gather_peer,
        "P": reduce_peer,
        "A": reduce_a,
        "B": reduce_b,
        "Z": reduce_z,
        "E": reduce_end,
        "a": plane_own,
        "b": plane_diagonal,
        "e": plane_line,
        "h": plane_peer,
        "U": plane_reduce,
        "V": plane_a,
        "X": plane_b,
        "F": plane_end,
        "R": row_sums,
        "S": statistics,
        "T": quad_sums,
        "N": line_sums,
    }

    def perform(steps):
        for operation, p in steps:
            operations[operation](p)

    def after(phase, b):
        for k, steps in SCHEDULE.get(phase, {}).items():

            @pl.when(b == k)
            def _():
                perform(steps)

    def once(phase):
        perform(SCHEDULE.get(phase, {}).get(0, ()))

    waited = set()

    def need(a, b):
        for p, (g0, g1, _) in enumerate(pieces):
            if g0 < b and a < g1 and p not in waited:
                waited.add(p)
                gathered(p)

    def w(a, b):
        return W[a:b].reshape((b - a) * D, D)

    def each(phase, step):

        @pl.loop(0, CLIPS)
        def _(b):
            step(b, pl.multiple_of(b * MAXLEN, MAXLEN))
            after(phase, b)

    def put(half, group, value):
        G[half, group] = value.astype(bf16).reshape(NZ, NY, NX, BLOCK, HALF)

    once("start")
    for load in small_in:
        load.wait()
    lane_row = lax.broadcasted_iota(jnp.int32, (1, MAXLEN), 1)
    count = jnp.zeros((1, MAXLEN), f32)
    for core in range(2):
        for b in range(CLIPS):
            live = (lane_row < lengths[core * CLIPS + b]) & (frame_mask[core, b] > 0)
            count = count + jnp.where(live, 1.0, 0.0)
    CN[0] = jnp.broadcast_to(jnp.sum(count, axis=1, keepdims=True), (8, 128))
    for k, dev in enumerate((dev_x, dev_y, dev_diagonal)):
        send(lambda: CN.at[0], lambda k=k: CN.at[1 + k], dev, at_count + k)
    for k, old in enumerate((conv_cols, proj_cols, book_cols)):
        send(lambda old=old: old.at[c], lambda old=old: old.at[c], dev_peer, at_cols + k)
    send(lambda: index_hbm.at[:, other], lambda: IDX.at[:, c], dev_peer, at_idx)
    send(lambda: cot_hbm.at[theirs, :], lambda: OB.at[:, cols], dev_peer, at_cot)

    @pl.loop(0, CLIPS)
    def _(b):
        live = (lane_row < lengths[c * CLIPS + b]) & (frame_mask[c, b] > 0)
        row = jnp.where(live, 1.0, 0.0)
        MASK[pl.ds(pl.multiple_of(b * MAXLEN, MAXLEN), MAXLEN), :] = jnp.broadcast_to(row, (128, MAXLEN)).T

    for g in range(GROUPS12):
        if g < 3:
            row = conv_rows[g, 0:1]
        elif g >= 9:
            row = conv_rows[g - 9, 1:2]
        elif g in (3, 8):
            row = proj_rows[g // 8 : g // 8 + 1]
        else:
            level, t = (g - 4) // 2, g % 2
            row = book_rows[level : level + 1, BLOCK * t : BLOCK * (t + 1)]
        OLD[g] = beta * jnp.broadcast_to(row, (128, BLOCK)).T
    frames_in.wait()

    def activate(b, r0):
        rows = pl.ds(r0, MAXLEN)
        for k in range(0, D, 128):
            a = gelu_pair(FR[rows, k : k + 128].astype(f32))[0] * MASK[rows, :]
            S[rows, k : k + 128], S[rows, 2 * D + k : 2 * D + k + 128] = neighbours(a)
            a = a.astype(bf16)
            S[rows, D + k : D + k + 128] = a
            AT[k : k + 128, rows] = a.T

    each("activate", activate)
    for k in range(3):
        arrived(CN.at[1 + k], at_count + k)
    CN[4] = (CN[0] + CN[1]) + (CN[2] + CN[3])
    for k in range(NZ - 1):
        send(lambda: CN.at[4], lambda k=k: CN.at[5 + k], dev_z[k], at_count + 3 + k)
    cot_in.wait()
    index_in.wait()
    arrived(OB.at[:, cols_other], at_cot)
    arrived(IDX.at[:, other], at_idx)
    for k, old in enumerate((conv_cols, proj_cols, book_cols)):
        arrived(old.at[other], at_cols + k)

    def upstream(b, r0):
        rows = pl.ds(r0, MAXLEN)
        for k in range(0, D, 128):
            ob = OB[rows, k : k + 128].astype(f32) * MASK[rows, :]
            O[rows, 2 * D + k : 2 * D + k + 128], O[rows, k : k + 128] = neighbours(ob)
            O[rows, D + k : D + k + 128] = ob.astype(bf16)

    each("upstream", upstream)
    for k in range(NZ - 1):
        arrived(CN.at[5 + k], at_count + 3 + k)
    scale = 2.0 / ((CN[4, 0:1] + CN[5, 0:1]) + (CN[6, 0:1] + CN[7, 0:1]))
    need(0, 3)

    def encode(b, r0):
        m = lanes(MASK[pl.ds(r0, MAXLEN), :], 4)
        branch = dot_nn(S[pl.ds(r0, MAXLEN), :], w(0, 3))
        enc = ((FR[pl.ds(r0, MAXLEN), :].astype(f32) + branch) * m).astype(bf16)
        STR[pl.ds(r0, MAXLEN), :] = enc
        ENCT[:, pl.ds(r0, MAXLEN)] = enc.T

    each("encode", encode)

    def project(b, r0):
        DGD[pl.ds(r0, MAXLEN), :] = dot_nn(STR[pl.ds(r0, MAXLEN), :], w(3, 4))

    need(3, 4)
    each("project", project)

    def slot(row):
        return ((row >> 5) & 1) * 512 + (row >> 6) * BLOCK + (row & 31)

    def onehot_rows(l, g, b):
        lane = lax.broadcasted_iota(jnp.int32, (MAXLEN, 128), 1)
        col = jnp.broadcast_to(slot(IDX[l, g, b]), (128, MAXLEN)).T
        return jnp.concatenate(
            [jnp.where(col == lane + 128 * k, 1.0, 0.0).astype(bf16) for k in range(CODES // 128)], axis=1
        )

    def chosen(l, g, b):
        book = W[4 + 2 * l : 6 + 2 * l, :, :, :, :, HALF * g : HALF * (g + 1)].reshape(CODES, HALF)
        return dot_nn(onehot_rows(l, g, b), book)

    def level_one(b, r0):
        for g in range(2):
            DEC[pl.ds(r0, MAXLEN), HALF * g : HALF * (g + 1)] = chosen(0, g, b)

    need(4, 6)
    each("level_one", level_one)

    def quantize(b, r0):
        m = lanes(MASK[pl.ds(r0, MAXLEN), :], 2)
        sc = lanes(scale, 2) * m
        for g in range(2):
            gc = slice(HALF * g, HALF * (g + 1))
            level = (DEC[pl.ds(r0, MAXLEN), gc], chosen(1, g, b))
            latent = DGD[pl.ds(r0, MAXLEN), gc]
            quantized = level[0] + level[1]
            straight = (latent + (quantized - latent)).astype(bf16)
            resid_one = latent - level[0]
            resid_two = resid_one - level[1]
            pulled = sc * (resid_one + resid_two)
            STR[pl.ds(r0, MAXLEN), gc] = straight
            STRT[gc, pl.ds(r0, MAXLEN)] = straight.T
            B1[pl.ds(r0, MAXLEN), gc] = (-pulled).astype(bf16)
            B2[pl.ds(r0, MAXLEN), gc] = (-(sc * resid_two)).astype(bf16)

    need(6, 8)
    each("quantize", quantize)

    def halves_of_grad(phase, count, step):
        @pl.loop(0, 2 * count)
        def _(t):
            half = lax.rem(t + other, 2)
            step(t // 2, half, pl.ds(pl.multiple_of(half * HALF, HALF), HALF))
            after(phase, t)

    def book_grads(phase, l, back):
        def step(_, g, hc):
            code = lax.broadcasted_iota(jnp.int32, (CODES, MAXLEN), 0)
            onehot = jnp.concatenate(
                [
                    jnp.where(jnp.broadcast_to(slot(IDX[l, g, b]), (CODES, MAXLEN)) == code, 1.0, 0.0).astype(bf16)
                    for b in range(CLIPS)
                ],
                axis=1,
            )
            value = dot_nn(onehot, back[:, hc]).astype(bf16)
            G[g, 4 + 2 * l : 6 + 2 * l] = value.reshape(2, NZ, NY, NX, BLOCK, HALF)

        halves_of_grad(phase, 1, step)

    book_grads("book0", 0, B1)
    book_grads("book1", 1, B2)

    def decode(b, r0):
        rows = pl.ds(r0, MAXLEN)
        DEC[rows, :] = dot_nn(STR[rows, :], w(8, 9))
        for k in range(0, D, 128):
            value, slope = gelu_pair(DEC[rows, k : k + 128])
            value = value * MASK[rows, :]
            DGD[rows, k : k + 128] = slope * MASK[rows, :]
            S[rows, k : k + 128], S[rows, 2 * D + k : 2 * D + k + 128] = neighbours(value)
            value = value.astype(bf16)
            S[rows, D + k : D + k + 128] = value
            DINT[k : k + 128, rows] = value.T

    need(8, 9)
    each("decode", decode)

    def kernel_grad(phase, left, base):
        def step(k, half, _):
            put(half, base + k, dot_nn(left[...], O[:, pl.ds(pl.multiple_of(k * D + half * HALF, HALF), HALF)]))

        halves_of_grad(phase, KERNEL, step)

    kernel_grad("kg9", DINT, 9)

    def decode_back(b, r0):
        total = None
        for k in range(KERNEL):
            term = dot_nt(O[pl.ds(r0, MAXLEN), k * D : (k + 1) * D], w(9 + k, 10 + k))
            total = term if total is None else total + term
        back = O[pl.ds(r0, MAXLEN), D : 2 * D].astype(f32) + DGD[pl.ds(r0, MAXLEN), :] * total
        back = back.astype(bf16)
        DB[pl.ds(r0, MAXLEN), :] = back
        pulled = B1[pl.ds(r0, MAXLEN), :].astype(f32)
        LB[pl.ds(r0, MAXLEN), :] = (dot_nt(back, w(8, 9)) - pulled).astype(bf16)

    need(9, 12)
    each("decode_back", decode_back)

    def proj_grads(phase, left, right, group):
        def step(_, half, hc):
            put(half, group, dot_nn(left[...], right[:, hc]))

        halves_of_grad(phase, 1, step)

    proj_grads("pg8", STRT, DB, 8)

    def encode_back(b, r0):
        rows = pl.ds(r0, MAXLEN)
        DGD[rows, :] = dot_nt(LB[rows, :], w(3, 4)) * lanes(MASK[rows, :], 4)
        for k in range(0, D, 128):
            low = DGD[rows, k : k + 128].astype(bf16)
            O[rows, 2 * D + k : 2 * D + k + 128], O[rows, k : k + 128] = neighbours(low.astype(f32))
            O[rows, D + k : D + k + 128] = low

    each("encode_back", encode_back)
    proj_grads("pg3", ENCT, LB, 3)
    kernel_grad("kg0", AT, 0)

    def halves(phase, step):

        @pl.loop(0, 2 * CLIPS)
        def _(t):
            h = t % 2
            step(pl.multiple_of((t // 2) * MAXLEN, MAXLEN), h, pl.ds(pl.multiple_of(h * HALF, HALF), HALF))
            after(phase, t)

    def decoded_result(r0, h, hc):
        m = lanes(MASK[pl.ds(r0, MAXLEN), :], 2)
        kernel = W[9:12, :, :, :, :, hc].reshape(KERNEL * D, HALF)
        value = (DEC[pl.ds(r0, MAXLEN), hc] + dot_nn(S[pl.ds(r0, MAXLEN), :], kernel)) * m
        OB[pl.ds(r0, MAXLEN), hc] = value.astype(bf16)

    def input_back(r0, h, hc):
        m = lanes(MASK[pl.ds(r0, MAXLEN), :], 2)
        total = None
        for k in range(KERNEL):
            kernel = W[k, pl.ds(2 * h, 2)].reshape(HALF, D)
            term = dot_nt(O[pl.ds(r0, MAXLEN), k * D : (k + 1) * D], kernel)
            total = term if total is None else total + term
        slope = gelu_pair(FR[pl.ds(r0, MAXLEN), hc].astype(f32))[1]
        STR[pl.ds(r0, MAXLEN), hc] = (DGD[pl.ds(r0, MAXLEN), hc] + slope * m * total).astype(bf16)

    halves("decoded", decoded_result)
    out_own = pltpu.make_async_copy(OB.at[:, cols], out_hbm.at[mine, :], lsem.at[3])
    out_own.start()
    at_out = place()
    send(lambda: OB.at[:, cols_other], lambda: out_hbm.at[mine, :], dev_peer, at_out)
    halves("input", input_back)
    in_own = pltpu.make_async_copy(STR.at[:, cols], input_hbm.at[mine, :], lsem.at[4])
    in_own.start()
    at_in = place()
    send(lambda: STR.at[:, cols_other], lambda: input_hbm.at[mine, :], dev_peer, at_in)

    once("end")

    assert counter[0] <= SEMAPHORES

    arrived(out_hbm.at[theirs, :], at_out)
    arrived(input_hbm.at[theirs, :], at_in)
    out_own.wait()
    in_own.wait()
    for src, at in unsent:
        remote(src(), src(), dev_peer, at).wait_send()


def write_kernel(*refs):
    count = len(refs) // 2
    copies = [pltpu.make_async_copy(refs[i], refs[count + i], refs[-1].at[i]) for i in range(count)]
    for copy in copies:
        copy.start()
    for copy in copies:
        copy.wait()


def fused_body(
    frames,
    cotangent,
    lengths,
    frame_mask,
    code_index,
    conv_weight,
    proj_weight,
    codebooks,
    conv_rows,
    conv_cols,
    proj_rows,
    proj_cols,
    book_rows,
    book_cols,
):
    vmem = pl.BlockSpec(memory_space=pltpu.VMEM)
    hbm = pl.BlockSpec(memory_space=pl.ANY)
    quad = (NZ, NY, NX, BLOCK)
    out = pl.pallas_call(
        fused_kernel,
        out_shape=(
            pltpu.VMEM(cotangent.shape, bf16),
            pltpu.VMEM(cotangent.shape, bf16),
            pltpu.VMEM(conv_weight.shape, f32),
            pltpu.VMEM(proj_weight.shape, f32),
            pltpu.VMEM(codebooks.shape, f32),
            pltpu.VMEM((KERNEL, 2, BLOCK), f32),
            pltpu.VMEM(conv_cols.shape, f32),
            pltpu.VMEM(proj_rows.shape, f32),
            pltpu.VMEM(proj_cols.shape, f32),
            pltpu.VMEM(book_rows.shape, f32),
            pltpu.VMEM(book_cols.shape, f32),
            pltpu.VMEM(conv_weight.shape, f32),
            pltpu.VMEM(proj_weight.shape, f32),
            pltpu.VMEM(codebooks.shape, f32),
        ),
        in_specs=[hbm] * 14,
        out_specs=(vmem,) * 14,
        scratch_shapes=[
            pltpu.VMEM((GROUPS12,) + quad + (D,), bf16),
            pltpu.VMEM((2, GROUPS12) + quad + (HALF,), bf16),
            pltpu.VMEM((GROUPS12,) + quad + (HALF,), bf16),
            pltpu.VMEM((GROUPS12, NZ, NY, BLOCK, 128), bf16),
            pltpu.VMEM((GROUPS12, NZ, NX, BLOCK, 128), bf16),
            pltpu.VMEM((GROUPS12, NZ, BLOCK, 128), bf16),
            pltpu.VMEM((GROUPS12, NZ, BLOCK, 128), bf16),
            pltpu.VMEM((GROUPS12, NZ, BLOCK, 128), bf16),
            pltpu.VMEM((GROUPS12, NZ, BLOCK, 128), bf16),
            pltpu.VMEM((GROUPS12, NZ, BLOCK, HALF), bf16),
            pltpu.VMEM((NZ - 1, GROUPS12, BLOCK, HALF), bf16),
            pltpu.VMEM((ROWS, D), bf16),
            pltpu.VMEM((ROWS, 3 * D), bf16),
            pltpu.VMEM((ROWS, 3 * D), bf16),
            pltpu.VMEM((D, ROWS), bf16),
            pltpu.VMEM((D, ROWS), bf16),
            pltpu.VMEM((D, ROWS), bf16),
            pltpu.VMEM((D, ROWS), bf16),
            pltpu.VMEM((ROWS, D), f32),
            pltpu.VMEM((ROWS, D), f32),
            pltpu.VMEM((ROWS, D), bf16),
            pltpu.VMEM((ROWS, D), bf16),
            pltpu.VMEM((ROWS, D), bf16),
            pltpu.VMEM((ROWS, D), bf16),
            pltpu.VMEM((NZ - 1, PLANES, NY, NX, BLOCK, HALF), bf16),
            pltpu.VMEM((PLANES, NY, NX, BLOCK, HALF), bf16),
            pltpu.VMEM((PLANES, NY, BLOCK, 128), bf16),
            pltpu.VMEM((PLANES, NX, BLOCK, 128), bf16),
            pltpu.VMEM((2, PLANES, BLOCK, 128), bf16),
            pltpu.VMEM((2, PLANES, BLOCK, 128), bf16),
            pltpu.VMEM(conv_weight.shape, f32),
            pltpu.VMEM(proj_weight.shape, f32),
            pltpu.VMEM(codebooks.shape, f32),
            pltpu.SMEM(lengths.shape, jnp.int32),
            pltpu.VMEM((2, CLIPS, 1, MAXLEN), jnp.int32),
            pltpu.VMEM((KERNEL, 2, BLOCK), f32),
            pltpu.VMEM(proj_rows.shape, f32),
            pltpu.VMEM(book_rows.shape, f32),
            pltpu.VMEM((2,) + conv_cols.shape, f32),
            pltpu.VMEM((2,) + proj_cols.shape, f32),
            pltpu.VMEM((2,) + book_cols.shape, f32),
            pltpu.VMEM((GROUPS12, BLOCK, 128), f32),
            pltpu.VMEM((ROWS, 128), f32),
            pltpu.VMEM((2, 2, CLIPS, 1, MAXLEN), jnp.int32),
            pltpu.VMEM((8, 8, 128), f32),
            pltpu.VMEM((GROUPS12, BLOCK, HALF), f32),
            pltpu.VMEM((GROUPS12, BLOCK, 128), f32),
            pltpu.VMEM((12, 16, HALF), f32),
            pltpu.VMEM((12, 8, HALF), f32),
            pltpu.VMEM((2, GROUPS12, BLOCK, 128), f32),
            pltpu.SemaphoreType.DMA((SEMAPHORES,)),
            pltpu.SemaphoreType.DMA((SEMAPHORES,)),
            pltpu.SemaphoreType.DMA((24,)),
        ],
        compiler_params=pltpu.CompilerParams(
            collective_id=0, has_side_effects=True, vmem_limit_bytes=58 * 2**20
        ),
        name="step",
    )(
        lengths,
        frames,
        cotangent,
        code_index.reshape(2, 2, CLIPS, 1, MAXLEN),
        conv_weight,
        proj_weight,
        codebooks,
        frame_mask.reshape(2, CLIPS, 1, MAXLEN),
        jnp.swapaxes(conv_rows, 0, 1),
        proj_rows,
        book_rows,
        conv_cols,
        proj_cols,
        book_cols,
    )
    out = pl.pallas_call(
        write_kernel,
        out_shape=tuple(jax.ShapeDtypeStruct(array.shape, array.dtype) for array in out),
        in_specs=[hbm] * len(out),
        out_specs=(hbm,) * len(out),
        scratch_shapes=[pltpu.SemaphoreType.DMA((len(out),))],
        compiler_params=pltpu.CompilerParams(vmem_limit_bytes=2 * 2**20),
        name="write",
    )(*out)
    return out[:5] + (jnp.swapaxes(out[5], 0, 1),) + out[6:]


def solution(mesh):
    placed = (
        P("dp", None),
        P("dp", "chan"),
        P("dp"),
        P("dp"),
        P(None, "dp", "chan"),
        P(None, None, "dp", "chan"),
        P(None, "dp", "chan"),
        P(None, "dp", "chan"),
        P(None, None, "dp"),
        P(None, "chan"),
        P(None, "dp"),
        P(None, "chan"),
        P(None, "dp"),
        P(None, "chan"),
    )
    fits = mesh.shape["dp"] == NZ * NY * NX and mesh.shape["chan"] == 2
    return jax.shard_map(
        fused_body if fits else general_body,
        mesh=mesh,
        in_specs=placed,
        out_specs=(
            P("dp", "chan"),
            P("dp", "chan"),
            P(None, None, "dp", "chan"),
            P(None, "dp", "chan"),
            P(None, "dp", "chan"),
            P(None, None, "dp"),
            P(None, "chan"),
            P(None, "dp"),
            P(None, "chan"),
            P(None, "dp"),
            P(None, "chan"),
            P(None, None, "dp", "chan"),
            P(None, "dp", "chan"),
            P(None, "dp", "chan"),
        ),
        check_vma=False,
    )
```

```python
import functools
import math

import jax
import jax.numpy as jnp
from jax import lax
from jax.experimental import pallas as pl
from jax.experimental.pallas import tpu as pltpu
from jax.sharding import PartitionSpec as P

D = 512
CODES = 1024
KERNEL = 3
STEP = 10
MAXLEN = 512
MICRO = 2


square_floor = 1e-30
clip_level = 0.5
f32 = jnp.float32
bf16 = jnp.bfloat16


def shifted(signal, length):
    channels = signal.shape[-1]
    blocks = signal.reshape(-1, length, channels)
    padded = jnp.pad(blocks, ((0, 0), (1, 1), (0, 0)))
    joined = jnp.concatenate(
        [padded[:, 0:length], padded[:, 1 : length + 1], padded[:, 2 : length + 2]], axis=2
    )
    return joined.reshape(-1, 3 * channels)


def unshift(partial_terms, length):
    channels = partial_terms.shape[-1] // 3
    blocks = partial_terms.reshape(-1, length, 3, channels)
    padded = jnp.pad(blocks, ((0, 0), (1, 1), (0, 0), (0, 0)))
    summed = padded[:, 2 : length + 2, 0] + padded[:, 1 : length + 1, 1] + padded[:, 0:length, 2]
    return summed.reshape(-1, channels)


def gelu_back(values, upstream):
    return jax.vjp(jax.nn.gelu, values)[1](upstream)[0]


def fetch(conv_weight, proj_weight, codebooks):
    return (
        lax.all_gather(conv_weight.astype(bf16), "dp", axis=2, tiled=True),
        lax.all_gather(proj_weight.astype(bf16), "dp", axis=1, tiled=True),
        lax.all_gather(codebooks.astype(bf16), "dp", axis=1, tiled=True),
    )


def reduce_grads(conv_total, proj_total, book_total):
    return (
        lax.psum_scatter(conv_total, "dp", scatter_dimension=2, tiled=True),
        lax.psum_scatter(proj_total, "dp", scatter_dimension=1, tiled=True),
        lax.psum_scatter(book_total, "dp", scatter_dimension=1, tiled=True),
    )


def contract(left, right):
    return jnp.einsum("fc,fd->cd", left, right, preferred_element_type=f32)


def transpose_product(left, right):
    return jnp.einsum("fd,cd->fc", left, right, preferred_element_type=f32)


def general_body(
    frames,
    cotangent,
    lengths,
    frame_mask,
    code_index,
    conv_weight,
    proj_weight,
    codebooks,
    conv_rows,
    conv_cols,
    proj_rows,
    proj_cols,
    book_rows,
    book_cols,
):
    length = MAXLEN
    block_rows = frames.shape[0] // MICRO
    half_width = cotangent.shape[1]
    chan_place = lax.axis_index("chan")
    row_place = jnp.arange(frames.shape[0], dtype=jnp.int32) % length
    live = (row_place < jnp.repeat(lengths, length, total_repeat_length=frames.shape[0])) & (
        frame_mask > 0
    )
    weight_mask = live.astype(f32)[:, None]
    live_total = lax.psum(jnp.sum(weight_mask), "dp")
    vq_scale = 2.0 / live_total
    running = None
    out_pieces = []
    grad_pieces = []
    for block_number in range(MICRO):
        first_row = block_number * block_rows
        last_row = first_row + block_rows
        conv_bank, proj_bank, book_bank = fetch(conv_weight, proj_weight, codebooks)
        conv_enc = conv_bank[0].reshape(-1, half_width)
        conv_dec = conv_bank[1].reshape(-1, half_width)
        frame_part = frames[first_row:last_row]
        frame_wide = frame_part.astype(f32)
        own_part = lax.dynamic_slice_in_dim(frame_wide, chan_place * half_width, half_width, 1)
        masked = weight_mask[first_row:last_row]
        cot_part = jnp.where(masked > 0, cotangent[first_row:last_row], jnp.zeros((), bf16))
        code_range = jnp.arange(book_bank.shape[1], dtype=jnp.int32)
        onehot_one = (code_index[0, first_row:last_row, 0][:, None] == code_range[None, :]).astype(
            bf16
        )
        onehot_two = (code_index[1, first_row:last_row, 0][:, None] == code_range[None, :]).astype(
            bf16
        )
        activated = (jax.nn.gelu(frame_wide) * masked).astype(bf16)
        stack_one = shifted(activated, length)
        branch = jnp.dot(stack_one, conv_enc, preferred_element_type=f32)
        encoded = (own_part + branch) * masked
        enc_full = lax.all_gather(encoded.astype(bf16), "chan", axis=1, tiled=True)
        latent = jnp.dot(enc_full, proj_bank[0], preferred_element_type=f32)
        level_one = jnp.dot(onehot_one, book_bank[0], preferred_element_type=f32)
        level_two = jnp.dot(onehot_two, book_bank[1], preferred_element_type=f32)
        quantized = level_one + level_two
        straight = (latent + (quantized - latent)).astype(bf16)
        straight_full = lax.all_gather(straight, "chan", axis=1, tiled=True)
        decoded = jnp.dot(straight_full, proj_bank[1], preferred_element_type=f32)
        decoder_in = (jax.nn.gelu(decoded) * masked).astype(bf16)
        decoder_full = lax.all_gather(decoder_in, "chan", axis=1, tiled=True)
        stack_two = shifted(decoder_full, length)
        result = (decoded + jnp.dot(stack_two, conv_dec, preferred_element_type=f32)) * masked
        out_pieces.append(result.astype(bf16))
        conv_dec_grad = contract(stack_two, cot_part)
        in_partial = unshift(transpose_product(cot_part, conv_dec), length)
        in_back = lax.psum_scatter(in_partial, "chan", scatter_dimension=1, tiled=True)
        decoded_back = (cot_part.astype(f32) + gelu_back(decoded, masked * in_back)).astype(bf16)
        proj_dec_grad = contract(straight_full, decoded_back)
        straight_back = lax.psum_scatter(
            transpose_product(decoded_back, proj_bank[1]), "chan", scatter_dimension=1, tiled=True
        )
        resid_one = latent - level_one
        resid_two = resid_one - level_two
        pulled = vq_scale * masked * (resid_one + resid_two)
        latent_back = (straight_back + pulled).astype(bf16)
        one_back = (-pulled).astype(bf16)
        two_back = (-(vq_scale * masked * resid_two)).astype(bf16)
        book_one_grad = contract(onehot_one, one_back)
        book_two_grad = contract(onehot_two, two_back)
        proj_enc_grad = contract(enc_full, latent_back)
        encoded_back = lax.psum_scatter(
            transpose_product(latent_back, proj_bank[0]), "chan", scatter_dimension=1, tiled=True
        )
        branch_back = (encoded_back * masked).astype(bf16)
        conv_enc_grad = contract(stack_one, branch_back)
        activated_back = unshift(transpose_product(branch_back, conv_enc), length)
        input_partial = gelu_back(frame_wide, masked * activated_back)
        input_own = lax.psum_scatter(input_partial, "chan", scatter_dimension=1, tiled=True)
        grad_pieces.append((encoded_back * masked + input_own).astype(bf16))
        conv_blockgrad = jnp.stack(
            [
                conv_enc_grad.reshape(KERNEL, -1, half_width),
                conv_dec_grad.reshape(KERNEL, -1, half_width),
            ]
        )
        proj_blockgrad = jnp.stack([proj_enc_grad, proj_dec_grad])
        book_blockgrad = jnp.stack([book_one_grad, book_two_grad])
        reduced = reduce_grads(conv_blockgrad, proj_blockgrad, book_blockgrad)
        running = (
            reduced
            if running is None
            else (running[0] + reduced[0], running[1] + reduced[1], running[2] + reduced[2])
        )
    conv_grad, proj_grad, book_grad = running
    decoded_out = jnp.concatenate(out_pieces, axis=0)
    input_grad = jnp.concatenate(grad_pieces, axis=0)
    beta_two = 1.0 - STEP ** (-0.8)
    squares_conv = conv_grad * conv_grad + square_floor
    squares_proj = proj_grad * proj_grad + square_floor
    squares_book = book_grad * book_grad + square_floor
    row_sums = lax.psum(
        (
            jnp.sum(squares_conv, axis=3),
            jnp.sum(squares_proj, axis=2),
            jnp.sum(squares_book, axis=2),
        ),
        "chan",
    )
    rowstat_conv = beta_two * conv_rows + (1.0 - beta_two) * row_sums[0]
    rowstat_proj = beta_two * proj_rows + (1.0 - beta_two) * row_sums[1]
    rowstat_book = beta_two * book_rows + (1.0 - beta_two) * row_sums[2]
    col_sums = lax.psum(
        (
            jnp.sum(squares_conv, axis=(1, 2)),
            jnp.sum(squares_proj, axis=1),
            jnp.sum(squares_book, axis=1),
            jnp.sum(rowstat_conv, axis=(1, 2)),
            jnp.sum(rowstat_proj, axis=1),
            jnp.sum(rowstat_book, axis=1),
        ),
        "dp",
    )
    colstat_conv = beta_two * conv_cols + (1.0 - beta_two) * col_sums[0]
    colstat_proj = beta_two * proj_cols + (1.0 - beta_two) * col_sums[1]
    colstat_book = beta_two * book_cols + (1.0 - beta_two) * col_sums[2]
    update_conv = conv_grad * lax.rsqrt(
        rowstat_conv[..., None] * colstat_conv[:, None, None, :] / col_sums[3][:, None, None, None]
    )
    update_proj = proj_grad * lax.rsqrt(
        rowstat_proj[..., None] * colstat_proj[:, None, :] / col_sums[4][:, None, None]
    )
    update_book = book_grad * lax.rsqrt(
        rowstat_book[..., None] * colstat_book[:, None, :] / col_sums[5][:, None, None]
    )
    norm_sums = lax.psum(
        (
            jnp.sum(update_conv * update_conv, axis=(1, 2, 3)),
            jnp.sum(update_proj * update_proj, axis=(1, 2)),
            jnp.sum(update_book * update_book, axis=(1, 2)),
        ),
        ("dp", "chan"),
    )
    factor_conv = jnp.maximum(1.0, jnp.sqrt(norm_sums[0] / (KERNEL * D * D)) / clip_level)
    factor_proj = jnp.maximum(1.0, jnp.sqrt(norm_sums[1] / (D * D)) / clip_level)
    factor_book = jnp.maximum(1.0, jnp.sqrt(norm_sums[2] / (CODES * D)) / clip_level)
    rate_conv = 2.0 / math.sqrt(KERNEL * D)
    rate_proj = 2.0 / math.sqrt(D)
    updated_conv = conv_weight - rate_conv * (update_conv / factor_conv[:, None, None, None])
    updated_proj = proj_weight - rate_proj * (update_proj / factor_proj[:, None, None])
    updated_book = codebooks - 2.0 * (update_book / factor_book[:, None, None])
    return (
        decoded_out,
        input_grad,
        conv_grad,
        proj_grad,
        book_grad,
        rowstat_conv,
        colstat_conv,
        rowstat_proj,
        colstat_proj,
        rowstat_book,
        colstat_book,
        updated_conv,
        updated_proj,
        updated_book,
    )


MESH = pl.DeviceIdType.MESH
CLIPS = 3
ROWS = CLIPS * MAXLEN
GROUPS12 = 12
NZ, NY, NX = 4, 2, 2
BLOCK = 32
SEMAPHORES = 256
HALF = 256
GELU_A = math.sqrt(2.0 / math.pi)
GELU_B = 0.044715
MATRICES = ((0, 3), (3, 4), (4, 6), (6, 8), (8, 9), (9, 12))


def gelu_pair(x):
    x2 = x * x
    t = jnp.tanh(x * (GELU_A + GELU_A * GELU_B * x2))
    half = 0.5 + 0.5 * t
    value = x * half
    return value, half + value * (1.0 - t) * (GELU_A + 3.0 * GELU_A * GELU_B * x2)


def lanes(m, n):
    return jnp.concatenate([m] * n, axis=1)


def dot_nn(a, b):
    return jnp.dot(a, b, preferred_element_type=f32)


def dot_nt(a, b):
    return lax.dot_general(a, b, (((1,), (1,)), ((), ())), preferred_element_type=f32)


def neighbours(v):
    rows = v.shape[0]
    row = lax.broadcasted_iota(jnp.int32, (8, v.shape[1]), 0)
    before, after = pltpu.roll(v, 1, 0), pltpu.roll(v, rows - 1, 0)
    before = jnp.concatenate([jnp.where(row == 0, 0.0, before[:8]), before[8:]], axis=0)
    after = jnp.concatenate([after[:-8], jnp.where(row == 7, 0.0, after[-8:])], axis=0)
    return before.astype(bf16), after.astype(bf16)


PIECES = ((0, 1, "f"), (1, 2, "f"), (2, 3, "f"), (3, 4, "f"), (4, 6, "f"), (6, 8, "f"), (8, 9, "f"), (9, 11, "f"), (11, 12, "f"))
PARTS = ((4, 6, "f"), (6, 8, "f"), (9, 10, "l"), (10, 12, "f"), (8, 9, "l"), (3, 4, "f"), (0, 1, "f"), (1, 2, "f"), (2, 3, "f"))
PLANES = max(1, sum((g1 - g0) * (kind == "l") for g0, g1, kind in PARTS))
SCHEDULE = {
    "start": {
        0: (("z", 2), ("z", 1), ("z", 3), ("z", 0), ("z", 4),),
    },
    "activate": {
        0: (("l", 2), ("l", 1), ("z", 6), ("l", 3), ("l", 0), ("z", 5), ("d", 2),),
        1: (("d", 1), ("z", 8), ("l", 4), ("d", 0),),
        2: (("q", 2), ("q", 1), ("l", 5),),
    },
    "upstream": {
        1: (("d", 3),),
        2: (("z", 7), ("q", 0), ("d", 4),),
    },
    "encode": {
        0: (("d", 5),),
        1: (("q", 3),),
        2: (("q", 4), ("l", 6), ("l", 7),),
    },
    "project": {
        1: (("l", 8),),
        2: (("q", 5),),
    },
    "quantize": {
        1: (("d", 6),),
    },
    "book0": {
        0: (("P", 0), ("d", 7),),
        1: (("q", 6),),
    },
    "book1": {
        0: (("d", 8), ("P", 1), ("A", 0),),
    },
    "decode": {
        1: (("q", 7),),
    },
    "kg9": {
        1: (("P", 2), ("q", 8),),
        2: (("B", 0),),
        4: (("A", 1), ("U", 2), ("P", 3),),
    },
    "decode_back": {
        1: (("A", 3), ("Z", 0),),
    },
    "pg8": {
        0: (("B", 1), ("P", 4),),
    },
    "encode_back": {
        2: (("U", 4), ("V", 2),),
    },
    "pg3": {
        0: (("P", 5), ("B", 3),),
    },
    "kg0": {
        0: (("P", 6), ("A", 5),),
        2: (("P", 7), ("A", 6),),
        4: (("P", 8), ("Z", 1), ("A", 7),),
    },
    "decoded": {
        0: (("A", 8), ("Z", 3),),
        2: (("B", 6), ("B", 5),),
        4: (("X", 2), ("V", 4),),
    },
    "input": {
        0: (("E", 0), ("B", 8), ("B", 7), ("Z", 6), ("E", 1),),
        1: (("X", 4), ("Z", 5),),
        2: (("Z", 8),),
        3: (("F", 2), ("Z", 7),),
        4: (("E", 3),),
        5: (("E", 6),),
    },
    "end": {
        0: (("F", 4), ("R", 0), ("S", 0), ("E", 8), ("E", 5), ("E", 7), ("R", 1), ("S", 1), ("T", 0), ("T", 1), ("N", 0), ("N", 1),),
    },
}


def fused_kernel(
    lengths_hbm,
    frames_hbm,
    cot_hbm,
    index_hbm,
    conv_hbm,
    proj_hbm,
    books_hbm,
    mask_hbm,
    conv_rows_hbm,
    proj_rows_hbm,
    book_rows_hbm,
    conv_cols_hbm,
    proj_cols_hbm,
    book_cols_hbm,
    out_hbm,
    input_hbm,
    conv_grad,
    proj_grad,
    book_grad,
    conv_rows_out,
    conv_cols_out,
    proj_rows_out,
    proj_cols_out,
    book_rows_out,
    book_cols_out,
    conv_new,
    proj_new,
    book_new,
    W,
    G,
    RP,
    AX,
    AY,
    BX,
    BY,
    BXS,
    BYS,
    TS,
    ZR,
    FR,
    S,
    O,
    AT,
    ENCT,
    STRT,
    DINT,
    DEC,
    DGD,
    B1,
    B2,
    STR,
    OB,
    ZQ,
    PS,
    QX,
    QY,
    QS,
    QB,
    conv_weight,
    proj_weight,
    codebooks,
    lengths,
    frame_mask,
    conv_rows,
    proj_rows,
    book_rows,
    conv_cols,
    proj_cols,
    book_cols,
    OLD,
    MASK,
    IDX,
    CN,
    GF,
    ROWSTAT,
    STA,
    STB,
    RSUM,
    ssem,
    rsem,
    lsem,
):
    DB, LB = OB, B1
    me = lax.axis_index("dp")
    c = lax.axis_index("chan")
    z, y, x = me // (NY * NX), (me // NX) % NY, me % NX
    far_y, far_x, other = 1 - y, 1 - x, 1 - c

    def dp_of(zz, yy, xx):
        return (zz * (NY * NX) + yy * NX + xx, c)

    dev_x, dev_y, dev_diagonal = dp_of(z, y, far_x), dp_of(z, far_y, x), dp_of(z, far_y, far_x)
    dev_z = [dp_of(lax.rem(z + k, NZ), y, x) for k in range(1, NZ)]
    dev_peer = (me, other)
    to_z = [lax.rem(z + k, NZ) for k in range(1, NZ)]
    from_z = [lax.rem(z + NZ - k, NZ) for k in range(1, NZ)]
    cols = pl.ds(pl.multiple_of(c * HALF, HALF), HALF)
    cols_other = pl.ds(pl.multiple_of(other * HALF, HALF), HALF)
    quarter = (
        pl.ds(pl.multiple_of(c * HALF, HALF), 128),
        pl.ds(pl.multiple_of(c * HALF + 128, 128), 128),
    )
    mine = pl.ds(pl.multiple_of(c * ROWS, ROWS), ROWS)
    theirs = pl.ds(pl.multiple_of(other * ROWS, ROWS), ROWS)

    counter = [0]
    unsent = []

    def place(n=1):
        counter[0] += n
        return counter[0] - n

    def remote(src, dst, dev, at):
        return pltpu.make_async_remote_copy(
            src_ref=src,
            dst_ref=dst,
            send_sem=ssem.at[at],
            recv_sem=rsem.at[at],
            device_id=dev,
            device_id_type=MESH,
        )

    def send(src, dst, dev, at):
        remote(src(), dst(), dev, at).start()
        unsent.append((src, at))

    def arrived(dst, at):
        remote(dst, dst, dev_peer, at).wait_recv()

    barrier = pltpu.get_barrier_semaphore()
    partners = [dev_x, dev_y, dev_diagonal, dev_peer] + dev_z + [(dev[0], other) for dev in dev_z]
    for dev in partners:
        pl.semaphore_signal(barrier, inc=1, device_id=dev, device_id_type=MESH)
    weights_in = [
        pltpu.make_async_copy(src, dst, lsem.at[9 + i])
        for i, (src, dst) in enumerate(((conv_hbm, conv_weight), (proj_hbm, proj_weight), (books_hbm, codebooks)))
    ]
    for load in weights_in:
        load.start()
    index_in = pltpu.make_async_copy(index_hbm.at[:, c], IDX.at[:, c], lsem.at[2])
    index_in.start()
    frames_in = pltpu.make_async_copy(frames_hbm.at[mine, :], FR, lsem.at[0])
    frames_in.start()
    cot_in = pltpu.make_async_copy(cot_hbm.at[mine, :], OB.at[:, cols], lsem.at[1])
    cot_in.start()
    small_in = [
        pltpu.make_async_copy(src, dst, lsem.at[16 + i])
        for i, (src, dst) in enumerate(
            (
                (lengths_hbm, lengths),
                (mask_hbm, frame_mask),
                (conv_rows_hbm, conv_rows),
                (proj_rows_hbm, proj_rows),
                (book_rows_hbm, book_rows),
                (conv_cols_hbm, conv_cols.at[c]),
                (proj_cols_hbm, proj_cols.at[c]),
                (book_cols_hbm, book_cols.at[c]),
            )
        )
    ]
    for load in small_in:
        load.start()
    for load in weights_in:
        load.wait()

    for k in range(3):
        W[k, z, y, x, :, cols] = conv_weight[0, k].astype(bf16)
        W[9 + k, z, y, x, :, cols] = conv_weight[1, k].astype(bf16)
    W[3, z, y, x, :, cols] = proj_weight[0].astype(bf16)
    W[8, z, y, x, :, cols] = proj_weight[1].astype(bf16)
    for level in range(2):
        for t in range(2):
            W[4 + 2 * level + t, z, y, x, :, cols] = codebooks[level, BLOCK * t : BLOCK * (t + 1)].astype(bf16)
    pl.semaphore_wait(barrier, len(partners))

    pieces = PIECES
    at_z = [place(3) for p in pieces]
    at_l = [place(2) for p in pieces]
    at_d = [place(2) for p in pieces]
    at_p = [place(2) for p in pieces]
    at_cot, at_idx, at_count = place(), place(), place(6)

    def gather_z(p):
        g0, g1 = pieces[p][:2]
        for k in range(NZ - 1):
            own = lambda: W.at[g0:g1, z, y, x, :, cols]
            send(own, own, dev_z[k], at_z[p] + k)

    def gather_line(p):
        g0, g1 = pieces[p][:2]
        for k in range(NZ - 1):
            arrived(W.at[g0:g1, from_z[k], y, x, :, cols], at_z[p] + k)
        line = lambda: W.at[g0:g1, :, y, x, :, cols]
        send(line, line, dev_x, at_l[p])
        send(line, line, dev_y, at_l[p] + 1)

    def gather_diagonal(p):
        g0, g1 = pieces[p][:2]
        arrived(W.at[g0:g1, :, y, far_x, :, cols], at_l[p])
        arrived(W.at[g0:g1, :, far_y, x, :, cols], at_l[p] + 1)
        part_y = lambda: W.at[g0:g1, :, far_y, x, :, quarter[0]]
        send(part_y, part_y, dev_x, at_d[p])
        part_x = lambda: W.at[g0:g1, :, y, far_x, :, quarter[1]]
        send(part_x, part_x, dev_y, at_d[p] + 1)
        near = lambda: W.at[g0:g1, :, y, :, :, cols]
        send(near, near, dev_peer, at_p[p])

    def gather_peer(p):
        g0, g1 = pieces[p][:2]
        arrived(W.at[g0:g1, :, far_y, far_x, :, quarter[0]], at_d[p])
        arrived(W.at[g0:g1, :, far_y, far_x, :, quarter[1]], at_d[p] + 1)
        far = lambda: W.at[g0:g1, :, far_y, :, :, cols]
        send(far, far, dev_peer, at_p[p] + 1)

    def plane_own(p):
        g0, g1 = pieces[p][:2]
        own = lambda: W.at[g0:g1, z, y, x, :, cols]
        send(own, own, dev_x, at_l[p])
        send(own, own, dev_y, at_l[p] + 1)

    def plane_diagonal(p):
        g0, g1 = pieces[p][:2]
        arrived(W.at[g0:g1, z, y, far_x, :, cols], at_l[p])
        arrived(W.at[g0:g1, z, far_y, x, :, cols], at_l[p] + 1)
        part_y = lambda: W.at[g0:g1, z, far_y, x, :, quarter[0]]
        send(part_y, part_y, dev_x, at_d[p])
        part_x = lambda: W.at[g0:g1, z, y, far_x, :, quarter[1]]
        send(part_x, part_x, dev_y, at_d[p] + 1)

    def plane_line(p):
        g0, g1 = pieces[p][:2]
        arrived(W.at[g0:g1, z, far_y, far_x, :, quarter[0]], at_d[p])
        arrived(W.at[g0:g1, z, far_y, far_x, :, quarter[1]], at_d[p] + 1)
        plane = lambda: W.at[g0:g1, z, :, :, :, cols]
        for k in range(NZ - 1):
            send(plane, plane, dev_z[k], at_z[p] + k)

    def plane_peer(p):
        g0, g1 = pieces[p][:2]
        for k in range(NZ - 1):
            arrived(W.at[g0:g1, from_z[k], :, :, :, cols], at_z[p] + k)
        whole = lambda: W.at[g0:g1, :, :, :, :, cols]
        send(whole, whole, dev_peer, at_p[p])

    def gathered(p):
        g0, g1 = pieces[p][:2]
        if pieces[p][2] == "l":
            arrived(W.at[g0:g1, :, :, :, :, cols_other], at_p[p])
            return
        arrived(W.at[g0:g1, :, y, :, :, cols_other], at_p[p])
        arrived(W.at[g0:g1, :, far_y, :, :, cols_other], at_p[p] + 1)

    parts = PARTS
    local, planes = [], 0
    for g0, g1, kind in parts:
        local.append(planes)
        planes += (g1 - g0) * (kind == "l")
    at_rp = [place() for p in parts]
    at_ra = [place(2) for p in parts]
    at_rb = [place(2) for p in parts]
    at_rz = [place(3) for p in parts]

    def reduce_peer(p):
        g0, g1 = parts[p][:2]
        send(lambda: G.at[other, g0:g1], lambda: RP.at[g0:g1], dev_peer, at_rp[p])

    def reduce_a(p):
        g0, g1 = parts[p][:2]
        arrived(RP.at[g0:g1], at_rp[p])

        @pl.loop(g0, g1)
        def _(g):
            G[c, g] = G[c, g] + RP[g]

        send(lambda: G.at[c, g0:g1, :, :, far_x, :, 0:128], lambda: AX.at[g0:g1], dev_x, at_ra[p])
        send(lambda: G.at[c, g0:g1, :, far_y, :, :, 128:256], lambda: AY.at[g0:g1], dev_y, at_ra[p] + 1)

    def reduce_b(p):
        g0, g1 = parts[p][:2]
        arrived(AX.at[g0:g1], at_ra[p])
        arrived(AY.at[g0:g1], at_ra[p] + 1)

        @pl.loop(g0, g1)
        def _(g):
            BXS[g] = (G[c, g, :, y, far_x, :, 128:256].astype(f32) + AY[g, :, far_x].astype(f32)).astype(bf16)
            BYS[g] = (G[c, g, :, far_y, x, :, 0:128].astype(f32) + AX[g, :, far_y].astype(f32)).astype(bf16)

        send(lambda: BXS.at[g0:g1], lambda: BX.at[g0:g1], dev_x, at_rb[p])
        send(lambda: BYS.at[g0:g1], lambda: BY.at[g0:g1], dev_y, at_rb[p] + 1)

    def reduce_z(p):
        g0, g1 = parts[p][:2]
        arrived(BX.at[g0:g1], at_rb[p])
        arrived(BY.at[g0:g1], at_rb[p] + 1)

        @pl.loop(g0, g1)
        def _(g):
            base = G[c, g, :, y, x].astype(f32)
            left = base[:, :, 0:128] + (AX[g, :, y].astype(f32) + BY[g].astype(f32))
            right = base[:, :, 128:256] + (AY[g, :, x].astype(f32) + BX[g].astype(f32))
            TS[g, :, :, 0:128] = left.astype(bf16)
            TS[g, :, :, 128:256] = right.astype(bf16)

        for k in range(NZ - 1):
            send(
                lambda k=k: TS.at[g0:g1, to_z[k]],
                lambda k=k: ZR.at[k, g0:g1],
                dev_z[k],
                at_rz[p] + k,
            )

    def reduce_end(p):
        g0, g1 = parts[p][:2]
        for k in range(NZ - 1):
            arrived(ZR.at[k, g0:g1], at_rz[p] + k)

        @pl.loop(g0, g1)
        def _(g):
            GF[g] = (TS[g, z].astype(f32) + ZR[0, g].astype(f32)) + (ZR[1, g].astype(f32) + ZR[2, g].astype(f32))

    def plane_reduce(p):
        g0, g1 = parts[p][:2]
        arrived(RP.at[g0:g1], at_rp[p])

        @pl.loop(g0, g1)
        def _(g):
            G[c, g] = G[c, g] + RP[g]

        for k in range(NZ - 1):
            send(
                lambda k=k: G.at[c, g0:g1, to_z[k]],
                lambda k=k: ZQ.at[k, local[p] : local[p] + g1 - g0],
                dev_z[k],
                at_rz[p] + k,
            )

    def plane_a(p):
        g0, g1 = parts[p][:2]
        i0, i1 = local[p], local[p] + g1 - g0
        for k in range(NZ - 1):
            arrived(ZQ.at[k, i0:i1], at_rz[p] + k)
        for i in range(i0, i1):
            total = G[c, g0 + i - i0, z].astype(f32) + ZQ[0, i].astype(f32)
            PS[i] = (total + (ZQ[1, i].astype(f32) + ZQ[2, i].astype(f32))).astype(bf16)
        send(lambda: PS.at[i0:i1, :, far_x, :, 0:128], lambda: QX.at[i0:i1], dev_x, at_ra[p])
        send(lambda: PS.at[i0:i1, far_y, :, :, 128:256], lambda: QY.at[i0:i1], dev_y, at_ra[p] + 1)

    def plane_b(p):
        g0, g1 = parts[p][:2]
        i0, i1 = local[p], local[p] + g1 - g0
        arrived(QX.at[i0:i1], at_ra[p])
        arrived(QY.at[i0:i1], at_ra[p] + 1)
        for i in range(i0, i1):
            QS[0, i] = (PS[i, y, far_x, :, 128:256].astype(f32) + QY[i, far_x].astype(f32)).astype(bf16)
            QS[1, i] = (PS[i, far_y, x, :, 0:128].astype(f32) + QX[i, far_y].astype(f32)).astype(bf16)
        send(lambda: QS.at[0, i0:i1], lambda: QB.at[0, i0:i1], dev_x, at_rb[p])
        send(lambda: QS.at[1, i0:i1], lambda: QB.at[1, i0:i1], dev_y, at_rb[p] + 1)

    def plane_end(p):
        g0, g1 = parts[p][:2]
        i0, i1 = local[p], local[p] + g1 - g0
        arrived(QB.at[0, i0:i1], at_rb[p])
        arrived(QB.at[1, i0:i1], at_rb[p] + 1)
        for i in range(i0, i1):
            base = PS[i, y, x].astype(f32)
            left = base[:, 0:128] + (QX[i, y].astype(f32) + QB[1, i].astype(f32))
            right = base[:, 128:256] + (QY[i, x].astype(f32) + QB[0, i].astype(f32))
            GF[g0 + i - i0, :, 0:128] = left
            GF[g0 + i - i0, :, 128:256] = right

    sets = (((4, 12), (2, 3, 4, 5), STA), ((0, 4), (0, 1), STB))
    at_rows = [place() for q in sets]
    at_quad = [place(3) for q in sets]
    at_line = [place(3) for q in sets]
    at_both = [place(4) for q in sets]
    at_cols = place(3)
    beta = 1.0 - STEP ** (-0.8)

    def row_sums(q):
        (g0, g1), _, _ = sets[q]

        @pl.loop(g0, g1)
        def _(g):
            grad = GF[g]
            RSUM[0, g] = jnp.broadcast_to(jnp.sum(grad * grad + square_floor, axis=1, keepdims=True), (BLOCK, 128))

        send(lambda: RSUM.at[0, g0:g1], lambda: RSUM.at[1, g0:g1], dev_peer, at_rows[q])

    def statistics(q):
        (g0, g1), members, SUMS = sets[q]
        arrived(RSUM.at[1, g0:g1], at_rows[q])
        lane_at = lax.broadcasted_iota(jnp.int32, (1, 128), 1)
        packed = jnp.zeros((1, 128), f32)
        n = len(members)
        SUMS[0] = jnp.zeros(SUMS.shape[1:], f32)
        for j, i in enumerate(members):
            squares, weighted, rows = 0.0, 0.0, 0.0
            for g in range(*MATRICES[i]):
                rowstat = OLD[g] + (1.0 - beta) * (RSUM[0, g] + RSUM[1, g])
                ROWSTAT[g] = rowstat
                square = GF[g] * GF[g]
                squares = squares + (square + square_floor)
                weighted = weighted + square / lanes(rowstat, 2)
                rows = rows + rowstat
            SUMS[0, j : j + 1, :] = jnp.sum(squares, axis=0, keepdims=True)
            SUMS[0, n + j : n + j + 1, :] = jnp.sum(weighted, axis=0, keepdims=True)
            packed = jnp.where(lane_at == j, jnp.sum(rows, axis=0, keepdims=True), packed)
        SUMS[0, 2 * n : 2 * n + 1, 0:128] = packed
        for k, dev in enumerate((dev_x, dev_y, dev_diagonal)):
            send(lambda: SUMS.at[0], lambda k=k: SUMS.at[1 + k], dev, at_quad[q] + k)

    def quad_sums(q):
        SUMS = sets[q][2]
        for k in range(3):
            arrived(SUMS.at[1 + k], at_quad[q] + k)
        SUMS[4] = (SUMS[0] + SUMS[1]) + (SUMS[2] + SUMS[3])
        for k in range(NZ - 1):
            send(lambda: SUMS.at[4], lambda k=k: SUMS.at[5 + k], dev_z[k], at_line[q] + k)
        send(lambda: SUMS.at[4], lambda: SUMS.at[8], dev_peer, at_both[q])
        for k in range(NZ - 1):
            send(lambda: SUMS.at[4], lambda k=k: SUMS.at[9 + k], (dev_z[k][0], other), at_both[q] + 1 + k)

    def line_sums(q):
        _, members, SUMS = sets[q]
        for k in range(NZ - 1):
            arrived(SUMS.at[5 + k], at_line[q] + k)
        for k in range(NZ):
            arrived(SUMS.at[8 + k], at_both[q] + k)
        lane_at = lax.broadcasted_iota(jnp.int32, (1, 128), 1)
        n = len(members)
        totals, norms = [0.0] * n, [0.0] * n
        for slot0, core in ((4, c), (8, other)):
            sums = (SUMS[slot0] + SUMS[slot0 + 1]) + (SUMS[slot0 + 2] + SUMS[slot0 + 3])
            for j, i in enumerate(members):
                cols_ref, at = (
                    (conv_cols, 0),
                    (proj_cols, 0),
                    (book_cols, 0),
                    (book_cols, 1),
                    (proj_cols, 1),
                    (conv_cols, 1),
                )[i]
                colstat = beta * cols_ref[core, at : at + 1] + (1.0 - beta) * sums[j : j + 1]
                if slot0 == 4:
                    cols_out = (
                        conv_cols_out,
                        proj_cols_out,
                        book_cols_out,
                        book_cols_out,
                        proj_cols_out,
                        conv_cols_out,
                    )[i]
                    cols_out[at : at + 1] = colstat
                    totals[j] = jnp.sum(
                        jnp.where(lane_at == j, sums[2 * n : 2 * n + 1, 0:128], 0.0), axis=1, keepdims=True
                    )
                norms[j] = norms[j] + jnp.sum(sums[n + j : n + j + 1] / colstat, axis=1, keepdims=True)
        for j, i in enumerate(members):
            g0, g1 = MATRICES[i]
            size = (g1 - g0) * BLOCK * NZ * NY * NX * D
            factor = jnp.maximum(1.0, jnp.sqrt(totals[j] * norms[j] / size) / clip_level)
            rate = (2.0 / math.sqrt(KERNEL * D), 2.0 / math.sqrt(D), 2.0)[(0, 1, 2, 2, 1, 0)[i]]
            for k in range(g1 - g0):
                grad, rowstat = GF[g0 + k], ROWSTAT[g0 + k]
                row = rowstat.T[0:1]
                if i in (0, 5):
                    m = i // 5
                    colstat = conv_cols_out[m : m + 1]
                elif i in (1, 4):
                    m = i // 4
                    colstat = proj_cols_out[m : m + 1]
                else:
                    m = i - 2
                    colstat = book_cols_out[m : m + 1]
                update = grad * lax.rsqrt(lanes(rowstat, 2) * colstat / totals[j])
                step = rate * (update / factor)
                if i in (0, 5):
                    conv_grad[m, k] = grad
                    conv_new[m, k] = conv_weight[m, k] - step
                    conv_rows_out[k, m : m + 1] = row
                elif i in (1, 4):
                    proj_grad[m] = grad
                    proj_new[m] = proj_weight[m] - step
                    proj_rows_out[m : m + 1] = row
                else:
                    part = slice(BLOCK * k, BLOCK * (k + 1))
                    book_grad[m, part] = grad
                    book_new[m, part] = codebooks[m, part] - step
                    book_rows_out[m : m + 1, part] = row

    operations = {
        "z": gather_z,
        "l": gather_line,
        "d": gather_diagonal,
        "q": gather_peer,
        "P": reduce_peer,
        "A": reduce_a,
        "B": reduce_b,
        "Z": reduce_z,
        "E": reduce_end,
        "a": plane_own,
        "b": plane_diagonal,
        "e": plane_line,
        "h": plane_peer,
        "U": plane_reduce,
        "V": plane_a,
        "X": plane_b,
        "F": plane_end,
        "R": row_sums,
        "S": statistics,
        "T": quad_sums,
        "N": line_sums,
    }

    def perform(steps):
        for operation, p in steps:
            operations[operation](p)

    def after(phase, b):
        for k, steps in SCHEDULE.get(phase, {}).items():

            @pl.when(b == k)
            def _():
                perform(steps)

    def once(phase):
        perform(SCHEDULE.get(phase, {}).get(0, ()))

    waited = set()

    def need(a, b):
        for p, (g0, g1, _) in enumerate(pieces):
            if g0 < b and a < g1 and p not in waited:
                waited.add(p)
                gathered(p)

    def w(a, b):
        return W[a:b].reshape((b - a) * D, D)

    def each(phase, step):

        @pl.loop(0, CLIPS)
        def _(b):
            step(b, pl.multiple_of(b * MAXLEN, MAXLEN))
            after(phase, b)

    def put(half, group, value):
        G[half, group] = value.astype(bf16).reshape(NZ, NY, NX, BLOCK, HALF)

    once("start")
    for load in small_in:
        load.wait()
    lane_row = lax.broadcasted_iota(jnp.int32, (1, MAXLEN), 1)
    count = jnp.zeros((1, MAXLEN), f32)
    for core in range(2):
        for b in range(CLIPS):
            live = (lane_row < lengths[core * CLIPS + b]) & (frame_mask[core, b] > 0)
            count = count + jnp.where(live, 1.0, 0.0)
    CN[0] = jnp.broadcast_to(jnp.sum(count, axis=1, keepdims=True), (8, 128))
    for k, dev in enumerate((dev_x, dev_y, dev_diagonal)):
        send(lambda: CN.at[0], lambda k=k: CN.at[1 + k], dev, at_count + k)
    for k, old in enumerate((conv_cols, proj_cols, book_cols)):
        send(lambda old=old: old.at[c], lambda old=old: old.at[c], dev_peer, at_cols + k)
    send(lambda: index_hbm.at[:, other], lambda: IDX.at[:, c], dev_peer, at_idx)
    send(lambda: cot_hbm.at[theirs, :], lambda: OB.at[:, cols], dev_peer, at_cot)

    @pl.loop(0, CLIPS)
    def _(b):
        live = (lane_row < lengths[c * CLIPS + b]) & (frame_mask[c, b] > 0)
        row = jnp.where(live, 1.0, 0.0)
        MASK[pl.ds(pl.multiple_of(b * MAXLEN, MAXLEN), MAXLEN), :] = jnp.broadcast_to(row, (128, MAXLEN)).T

    for g in range(GROUPS12):
        if g < 3:
            row = conv_rows[g, 0:1]
        elif g >= 9:
            row = conv_rows[g - 9, 1:2]
        elif g in (3, 8):
            row = proj_rows[g // 8 : g // 8 + 1]
        else:
            level, t = (g - 4) // 2, g % 2
            row = book_rows[level : level + 1, BLOCK * t : BLOCK * (t + 1)]
        OLD[g] = beta * jnp.broadcast_to(row, (128, BLOCK)).T
    frames_in.wait()

    def activate(b, r0):
        rows = pl.ds(r0, MAXLEN)
        for k in range(0, D, 128):
            a = gelu_pair(FR[rows, k : k + 128].astype(f32))[0] * MASK[rows, :]
            S[rows, k : k + 128], S[rows, 2 * D + k : 2 * D + k + 128] = neighbours(a)
            a = a.astype(bf16)
            S[rows, D + k : D + k + 128] = a
            AT[k : k + 128, rows] = a.T

    each("activate", activate)
    for k in range(3):
        arrived(CN.at[1 + k], at_count + k)
    CN[4] = (CN[0] + CN[1]) + (CN[2] + CN[3])
    for k in range(NZ - 1):
        send(lambda: CN.at[4], lambda k=k: CN.at[5 + k], dev_z[k], at_count + 3 + k)
    cot_in.wait()
    index_in.wait()
    arrived(OB.at[:, cols_other], at_cot)
    arrived(IDX.at[:, other], at_idx)
    for k, old in enumerate((conv_cols, proj_cols, book_cols)):
        arrived(old.at[other], at_cols + k)

    def upstream(b, r0):
        rows = pl.ds(r0, MAXLEN)
        for k in range(0, D, 128):
            ob = OB[rows, k : k + 128].astype(f32) * MASK[rows, :]
            O[rows, 2 * D + k : 2 * D + k + 128], O[rows, k : k + 128] = neighbours(ob)
            O[rows, D + k : D + k + 128] = ob.astype(bf16)

    each("upstream", upstream)
    for k in range(NZ - 1):
        arrived(CN.at[5 + k], at_count + 3 + k)
    scale = 2.0 / ((CN[4, 0:1] + CN[5, 0:1]) + (CN[6, 0:1] + CN[7, 0:1]))
    need(0, 3)

    def encode(b, r0):
        m = lanes(MASK[pl.ds(r0, MAXLEN), :], 4)
        branch = dot_nn(S[pl.ds(r0, MAXLEN), :], w(0, 3))
        enc = ((FR[pl.ds(r0, MAXLEN), :].astype(f32) + branch) * m).astype(bf16)
        STR[pl.ds(r0, MAXLEN), :] = enc
        ENCT[:, pl.ds(r0, MAXLEN)] = enc.T

    each("encode", encode)

    def project(b, r0):
        DGD[pl.ds(r0, MAXLEN), :] = dot_nn(STR[pl.ds(r0, MAXLEN), :], w(3, 4))

    need(3, 4)
    each("project", project)

    def slot(row):
        return ((row >> 5) & 1) * 512 + (row >> 6) * BLOCK + (row & 31)

    def onehot_rows(l, g, b):
        lane = lax.broadcasted_iota(jnp.int32, (MAXLEN, 128), 1)
        col = jnp.broadcast_to(slot(IDX[l, g, b]), (128, MAXLEN)).T
        return jnp.concatenate(
            [jnp.where(col == lane + 128 * k, 1.0, 0.0).astype(bf16) for k in range(CODES // 128)], axis=1
        )

    def chosen(l, g, b):
        book = W[4 + 2 * l : 6 + 2 * l, :, :, :, :, HALF * g : HALF * (g + 1)].reshape(CODES, HALF)
        return dot_nn(onehot_rows(l, g, b), book)

    def level_one(b, r0):
        for g in range(2):
            DEC[pl.ds(r0, MAXLEN), HALF * g : HALF * (g + 1)] = chosen(0, g, b)

    need(4, 6)
    each("level_one", level_one)

    def quantize(b, r0):
        m = lanes(MASK[pl.ds(r0, MAXLEN), :], 2)
        sc = lanes(scale, 2) * m
        for g in range(2):
            gc = slice(HALF * g, HALF * (g + 1))
            level = (DEC[pl.ds(r0, MAXLEN), gc], chosen(1, g, b))
            latent = DGD[pl.ds(r0, MAXLEN), gc]
            quantized = level[0] + level[1]
            straight = (latent + (quantized - latent)).astype(bf16)
            resid_one = latent - level[0]
            resid_two = resid_one - level[1]
            pulled = sc * (resid_one + resid_two)
            STR[pl.ds(r0, MAXLEN), gc] = straight
            STRT[gc, pl.ds(r0, MAXLEN)] = straight.T
            B1[pl.ds(r0, MAXLEN), gc] = (-pulled).astype(bf16)
            B2[pl.ds(r0, MAXLEN), gc] = (-(sc * resid_two)).astype(bf16)

    need(6, 8)
    each("quantize", quantize)

    def halves_of_grad(phase, count, step):
        @pl.loop(0, 2 * count)
        def _(t):
            half = lax.rem(t + other, 2)
            step(t // 2, half, pl.ds(pl.multiple_of(half * HALF, HALF), HALF))
            after(phase, t)

    def book_grads(phase, l, back):
        def step(_, g, hc):
            code = lax.broadcasted_iota(jnp.int32, (CODES, MAXLEN), 0)
            onehot = jnp.concatenate(
                [
                    jnp.where(jnp.broadcast_to(slot(IDX[l, g, b]), (CODES, MAXLEN)) == code, 1.0, 0.0).astype(bf16)
                    for b in range(CLIPS)
                ],
                axis=1,
            )
            value = dot_nn(onehot, back[:, hc]).astype(bf16)
            G[g, 4 + 2 * l : 6 + 2 * l] = value.reshape(2, NZ, NY, NX, BLOCK, HALF)

        halves_of_grad(phase, 1, step)

    book_grads("book0", 0, B1)
    book_grads("book1", 1, B2)

    def decode(b, r0):
        rows = pl.ds(r0, MAXLEN)
        DEC[rows, :] = dot_nn(STR[rows, :], w(8, 9))
        for k in range(0, D, 128):
            value, slope = gelu_pair(DEC[rows, k : k + 128])
            value = value * MASK[rows, :]
            DGD[rows, k : k + 128] = slope * MASK[rows, :]
            S[rows, k : k + 128], S[rows, 2 * D + k : 2 * D + k + 128] = neighbours(value)
            value = value.astype(bf16)
            S[rows, D + k : D + k + 128] = value
            DINT[k : k + 128, rows] = value.T

    need(8, 9)
    each("decode", decode)

    def kernel_grad(phase, left, base):
        def step(k, half, _):
            put(half, base + k, dot_nn(left[...], O[:, pl.ds(pl.multiple_of(k * D + half * HALF, HALF), HALF)]))

        halves_of_grad(phase, KERNEL, step)

    kernel_grad("kg9", DINT, 9)

    def decode_back(b, r0):
        total = None
        for k in range(KERNEL):
            term = dot_nt(O[pl.ds(r0, MAXLEN), k * D : (k + 1) * D], w(9 + k, 10 + k))
            total = term if total is None else total + term
        back = O[pl.ds(r0, MAXLEN), D : 2 * D].astype(f32) + DGD[pl.ds(r0, MAXLEN), :] * total
        back = back.astype(bf16)
        DB[pl.ds(r0, MAXLEN), :] = back
        pulled = B1[pl.ds(r0, MAXLEN), :].astype(f32)
        LB[pl.ds(r0, MAXLEN), :] = (dot_nt(back, w(8, 9)) - pulled).astype(bf16)

    need(9, 12)
    each("decode_back", decode_back)

    def proj_grads(phase, left, right, group):
        def step(_, half, hc):
            put(half, group, dot_nn(left[...], right[:, hc]))

        halves_of_grad(phase, 1, step)

    proj_grads("pg8", STRT, DB, 8)

    def encode_back(b, r0):
        rows = pl.ds(r0, MAXLEN)
        DGD[rows, :] = dot_nt(LB[rows, :], w(3, 4)) * lanes(MASK[rows, :], 4)
        for k in range(0, D, 128):
            low = DGD[rows, k : k + 128].astype(bf16)
            O[rows, 2 * D + k : 2 * D + k + 128], O[rows, k : k + 128] = neighbours(low.astype(f32))
            O[rows, D + k : D + k + 128] = low

    each("encode_back", encode_back)
    proj_grads("pg3", ENCT, LB, 3)
    kernel_grad("kg0", AT, 0)

    def halves(phase, step):

        @pl.loop(0, 2 * CLIPS)
        def _(t):
            h = t % 2
            step(pl.multiple_of((t // 2) * MAXLEN, MAXLEN), h, pl.ds(pl.multiple_of(h * HALF, HALF), HALF))
            after(phase, t)

    def decoded_result(r0, h, hc):
        m = lanes(MASK[pl.ds(r0, MAXLEN), :], 2)
        kernel = W[9:12, :, :, :, :, hc].reshape(KERNEL * D, HALF)
        value = (DEC[pl.ds(r0, MAXLEN), hc] + dot_nn(S[pl.ds(r0, MAXLEN), :], kernel)) * m
        OB[pl.ds(r0, MAXLEN), hc] = value.astype(bf16)

    def input_back(r0, h, hc):
        m = lanes(MASK[pl.ds(r0, MAXLEN), :], 2)
        total = None
        for k in range(KERNEL):
            kernel = W[k, pl.ds(2 * h, 2)].reshape(HALF, D)
            term = dot_nt(O[pl.ds(r0, MAXLEN), k * D : (k + 1) * D], kernel)
            total = term if total is None else total + term
        slope = gelu_pair(FR[pl.ds(r0, MAXLEN), hc].astype(f32))[1]
        STR[pl.ds(r0, MAXLEN), hc] = (DGD[pl.ds(r0, MAXLEN), hc] + slope * m * total).astype(bf16)

    halves("decoded", decoded_result)
    out_own = pltpu.make_async_copy(OB.at[:, cols], out_hbm.at[mine, :], lsem.at[3])
    out_own.start()
    at_out = place()
    send(lambda: OB.at[:, cols_other], lambda: out_hbm.at[mine, :], dev_peer, at_out)
    halves("input", input_back)
    in_own = pltpu.make_async_copy(STR.at[:, cols], input_hbm.at[mine, :], lsem.at[4])
    in_own.start()
    at_in = place()
    send(lambda: STR.at[:, cols_other], lambda: input_hbm.at[mine, :], dev_peer, at_in)

    once("end")

    assert counter[0] <= SEMAPHORES

    arrived(out_hbm.at[theirs, :], at_out)
    arrived(input_hbm.at[theirs, :], at_in)
    out_own.wait()
    in_own.wait()
    for src, at in unsent:
        remote(src(), src(), dev_peer, at).wait_send()


def write_kernel(*refs):
    count = len(refs) // 2
    copies = [pltpu.make_async_copy(refs[i], refs[count + i], refs[-1].at[i]) for i in range(count)]
    for copy in copies:
        copy.start()
    for copy in copies:
        copy.wait()


def fused_body(
    frames,
    cotangent,
    lengths,
    frame_mask,
    code_index,
    conv_weight,
    proj_weight,
    codebooks,
    conv_rows,
    conv_cols,
    proj_rows,
    proj_cols,
    book_rows,
    book_cols,
):
    vmem = pl.BlockSpec(memory_space=pltpu.VMEM)
    hbm = pl.BlockSpec(memory_space=pl.ANY)
    quad = (NZ, NY, NX, BLOCK)
    out = pl.pallas_call(
        fused_kernel,
        out_shape=(
            pltpu.VMEM(cotangent.shape, bf16),
            pltpu.VMEM(cotangent.shape, bf16),
            pltpu.VMEM(conv_weight.shape, f32),
            pltpu.VMEM(proj_weight.shape, f32),
            pltpu.VMEM(codebooks.shape, f32),
            pltpu.VMEM((KERNEL, 2, BLOCK), f32),
            pltpu.VMEM(conv_cols.shape, f32),
            pltpu.VMEM(proj_rows.shape, f32),
            pltpu.VMEM(proj_cols.shape, f32),
            pltpu.VMEM(book_rows.shape, f32),
            pltpu.VMEM(book_cols.shape, f32),
            pltpu.VMEM(conv_weight.shape, f32),
            pltpu.VMEM(proj_weight.shape, f32),
            pltpu.VMEM(codebooks.shape, f32),
        ),
        in_specs=[hbm] * 14,
        out_specs=(vmem,) * 14,
        scratch_shapes=[
            pltpu.VMEM((GROUPS12,) + quad + (D,), bf16),
            pltpu.VMEM((2, GROUPS12) + quad + (HALF,), bf16),
            pltpu.VMEM((GROUPS12,) + quad + (HALF,), bf16),
            pltpu.VMEM((GROUPS12, NZ, NY, BLOCK, 128), bf16),
            pltpu.VMEM((GROUPS12, NZ, NX, BLOCK, 128), bf16),
            pltpu.VMEM((GROUPS12, NZ, BLOCK, 128), bf16),
            pltpu.VMEM((GROUPS12, NZ, BLOCK, 128), bf16),
            pltpu.VMEM((GROUPS12, NZ, BLOCK, 128), bf16),
            pltpu.VMEM((GROUPS12, NZ, BLOCK, 128), bf16),
            pltpu.VMEM((GROUPS12, NZ, BLOCK, HALF), bf16),
            pltpu.VMEM((NZ - 1, GROUPS12, BLOCK, HALF), bf16),
            pltpu.VMEM((ROWS, D), bf16),
            pltpu.VMEM((ROWS, 3 * D), bf16),
            pltpu.VMEM((ROWS, 3 * D), bf16),
            pltpu.VMEM((D, ROWS), bf16),
            pltpu.VMEM((D, ROWS), bf16),
            pltpu.VMEM((D, ROWS), bf16),
            pltpu.VMEM((D, ROWS), bf16),
            pltpu.VMEM((ROWS, D), f32),
            pltpu.VMEM((ROWS, D), f32),
            pltpu.VMEM((ROWS, D), bf16),
            pltpu.VMEM((ROWS, D), bf16),
            pltpu.VMEM((ROWS, D), bf16),
            pltpu.VMEM((ROWS, D), bf16),
            pltpu.VMEM((NZ - 1, PLANES, NY, NX, BLOCK, HALF), bf16),
            pltpu.VMEM((PLANES, NY, NX, BLOCK, HALF), bf16),
            pltpu.VMEM((PLANES, NY, BLOCK, 128), bf16),
            pltpu.VMEM((PLANES, NX, BLOCK, 128), bf16),
            pltpu.VMEM((2, PLANES, BLOCK, 128), bf16),
            pltpu.VMEM((2, PLANES, BLOCK, 128), bf16),
            pltpu.VMEM(conv_weight.shape, f32),
            pltpu.VMEM(proj_weight.shape, f32),
            pltpu.VMEM(codebooks.shape, f32),
            pltpu.SMEM(lengths.shape, jnp.int32),
            pltpu.VMEM((2, CLIPS, 1, MAXLEN), jnp.int32),
            pltpu.VMEM((KERNEL, 2, BLOCK), f32),
            pltpu.VMEM(proj_rows.shape, f32),
            pltpu.VMEM(book_rows.shape, f32),
            pltpu.VMEM((2,) + conv_cols.shape, f32),
            pltpu.VMEM((2,) + proj_cols.shape, f32),
            pltpu.VMEM((2,) + book_cols.shape, f32),
            pltpu.VMEM((GROUPS12, BLOCK, 128), f32),
            pltpu.VMEM((ROWS, 128), f32),
            pltpu.VMEM((2, 2, CLIPS, 1, MAXLEN), jnp.int32),
            pltpu.VMEM((8, 8, 128), f32),
            pltpu.VMEM((GROUPS12, BLOCK, HALF), f32),
            pltpu.VMEM((GROUPS12, BLOCK, 128), f32),
            pltpu.VMEM((12, 16, HALF), f32),
            pltpu.VMEM((12, 8, HALF), f32),
            pltpu.VMEM((2, GROUPS12, BLOCK, 128), f32),
            pltpu.SemaphoreType.DMA((SEMAPHORES,)),
            pltpu.SemaphoreType.DMA((SEMAPHORES,)),
            pltpu.SemaphoreType.DMA((24,)),
        ],
        compiler_params=pltpu.CompilerParams(
            collective_id=0, has_side_effects=True, vmem_limit_bytes=58 * 2**20
        ),
        name="step",
    )(
        lengths,
        frames,
        cotangent,
        code_index.reshape(2, 2, CLIPS, 1, MAXLEN),
        conv_weight,
        proj_weight,
        codebooks,
        frame_mask.reshape(2, CLIPS, 1, MAXLEN),
        jnp.swapaxes(conv_rows, 0, 1),
        proj_rows,
        book_rows,
        conv_cols,
        proj_cols,
        book_cols,
    )
    out = pl.pallas_call(
        write_kernel,
        out_shape=tuple(jax.ShapeDtypeStruct(array.shape, array.dtype) for array in out),
        in_specs=[hbm] * len(out),
        out_specs=(hbm,) * len(out),
        scratch_shapes=[pltpu.SemaphoreType.DMA((len(out),))],
        compiler_params=pltpu.CompilerParams(vmem_limit_bytes=2 * 2**20),
        name="write",
    )(*out)
    return out[:5] + (jnp.swapaxes(out[5], 0, 1),) + out[6:]


def solution(mesh):
    placed = (
        P("dp", None),
        P("dp", "chan"),
        P("dp"),
        P("dp"),
        P(None, "dp", "chan"),
        P(None, None, "dp", "chan"),
        P(None, "dp", "chan"),
        P(None, "dp", "chan"),
        P(None, None, "dp"),
        P(None, "chan"),
        P(None, "dp"),
        P(None, "chan"),
        P(None, "dp"),
        P(None, "chan"),
    )
    fits = mesh.shape["dp"] == NZ * NY * NX and mesh.shape["chan"] == 2
    return jax.shard_map(
        fused_body if fits else general_body,
        mesh=mesh,
        in_specs=placed,
        out_specs=(
            P("dp", "chan"),
            P("dp", "chan"),
            P(None, None, "dp", "chan"),
            P(None, "dp", "chan"),
            P(None, "dp", "chan"),
            P(None, None, "dp"),
            P(None, "chan"),
            P(None, "dp"),
            P(None, "chan"),
            P(None, "dp"),
            P(None, "chan"),
            P(None, None, "dp", "chan"),
            P(None, "dp", "chan"),
            P(None, "dp", "chan"),
        ),
        check_vma=False,
    )
```
